32 devices in a mesh: samp: 8 (over y, x, core), feat: 4 (over z).
Axes of the slice: x: 2, y: 2, z: 4, core: 2. Of those that a mesh axis runs over, the one named last changes fastest.
Arguments:
- labels: int32 [131072], P('samp'), may hold values 0 or 1
- beta: float32 [262144], P('feat'), may hold values from -1.2 to 1.2
- tile_rows: int32 [8, 4, 64], P('samp', 'feat'), may hold values from 0 to 127, as said below
- tile_cols: int32 [8, 4, 64], P('samp', 'feat'), may hold values from 0 to 511, as said below
- tile_values: bfloat16 [8, 4, 64, 128, 128], P('samp', 'feat'), may hold values from -0.5 to 0.5
- block_order: int32 [4, 4], P('feat'), may hold values from 0 to 511, as said below
- hess_inv: float32 [4, 4, 128, 128], P('feat')
Outputs:
- beta_new: float32 [262144], P('feat')
- residual: float32 [131072], P(('samp', 'feat'))
The draws below stay inside these ranges and needn't reach their ends.
Inputs may be any that keep to these rules, and one draw needn't show every extreme that they name: `tile_rows`: row block numbers within a samp index. `tile_cols`: feature block numbers within a feat index. Each row of block_order holds 4 distinct block numbers.
All inputs are finite; a program needn't handle non-finite values. No bound on the sum of `labels` on one device may be relied on, other than what follows from the above.
Results may differ from the reference program's by a relative error of at most 0.0025.
Values sent between devices are 32-bit elements; how exact they have to be, the bound alone decides.
No kernel may reach another device: no remote copies, remote signals or barrier semaphores. Data moves between devices by JAX's collectives and lax.ppermute only.
A program may use at most 64 MiB of HBM per device.

```python
import jax
import jax.numpy as jnp
from jax import lax

TILE = 128
FEAT_BLOCKS = 512
GROUP_BLOCKS = 32
TILES = 64
SECTIONS = 4
ROW_BLOCKS = 128
ROWS_DEV = 16384
SAMPLES = 131072
FEATURES = 262144
N_SAMP = 8
N_FEAT = 4


def tile_layout(key):
    base = jax.random.fold_in(key, 11)
    key_order, key_section, key_kind, key_offset, key_col, key_row = jax.random.split(base, 6)
    samp_count = SAMPLES // ROWS_DEV
    order_keys = jax.random.split(key_order, SECTIONS)
    raw_order = jax.vmap(lambda subkey: jax.random.permutation(subkey, FEAT_BLOCKS)[:SECTIONS])(order_keys).astype(jnp.int32)
    order_rows = jnp.arange(SECTIONS, dtype=jnp.int32)
    shifting = jnp.where(order_rows == 0, FEAT_BLOCKS - 1 - raw_order[:, 0], 0)
    shifting = jnp.where(order_rows == 1, -raw_order[:, 0], shifting)
    block_order = ((raw_order + shifting[:, None]) % FEAT_BLOCKS).astype(jnp.int32)
    shape = (samp_count, SECTIONS, TILES)
    slot_ids = jnp.arange(TILES, dtype=jnp.int32)[None, None, :]
    section_pick = jax.random.randint(key_section, shape, 0, SECTIONS)
    section_pick = jnp.where(slot_ids < SECTIONS, slot_ids, section_pick).astype(jnp.int32)
    background = (jax.random.randint(key_kind, shape, 0, 2) == 1) & (slot_ids >= SECTIONS)
    feat_index = jnp.arange(SECTIONS, dtype=jnp.int32)[None, :, None]
    group_index = (feat_index - section_pick) % SECTIONS
    offsets = jax.random.randint(key_offset, shape, 0, GROUP_BLOCKS).astype(jnp.int32)
    offsets = offsets.at[0, 0, 0].set(0).at[0, SECTIONS - 1, 0].set(GROUP_BLOCKS - 1)
    row_ids = group_index * GROUP_BLOCKS + offsets
    row_ids = jnp.where(background, jax.random.randint(key_row, shape, 0, ROW_BLOCKS), row_ids)
    full_order = jnp.broadcast_to(block_order[None, :, :], (samp_count, SECTIONS, SECTIONS))
    visited = jnp.take_along_axis(full_order, section_pick, axis=2)
    col_ids = jnp.where(background, jax.random.randint(key_col, shape, 0, FEAT_BLOCKS), visited)
    return (row_ids.astype(jnp.int32), col_ids.astype(jnp.int32), block_order)


def draw_tile_rows(key, part):
    return tile_layout(key)[0]


def draw_tile_cols(key, part):
    return tile_layout(key)[1]


def draw_block_order(key, part):
    return tile_layout(key)[2]


def draw_hess_inv(key, part):
    key_diag, key_spread = jax.random.split(jax.random.fold_in(key, 23))
    shape = (SECTIONS, SECTIONS, TILE, TILE)
    diagonal = jax.random.uniform(key_diag, (SECTIONS, SECTIONS, TILE), jnp.float32, 0.05, 0.15)
    spread_part = jax.random.normal(key_spread, shape, jnp.float32)
    spread_part = spread_part * (0.033 * TILE ** (-0.5))
    identity = jnp.eye(TILE, dtype=jnp.float32)
    return spread_part * (1.0 - identity) + identity * diagonal[..., None]


def set_ends(result, rng, smallest, largest):
    spot = [jax.random.randint(jax.random.fold_in(rng, axis), (), 0, length) for axis, length in enumerate(result.shape)]
    main_axis = result.shape.index(max(result.shape))
    beside = spot[:main_axis] + [(spot[main_axis] + 1) % result.shape[main_axis]] + spot[main_axis + 1:]
    return result.at[tuple(spot)].set(smallest).at[tuple(beside)].set(largest)


def steps_of(own_key, shape, cuts, least, high):
    def one(dim, shards_of):
        steps = jax.random.uniform(jax.random.fold_in(jax.random.fold_in(own_key, 6), dim), (shards_of,), jnp.float32, least / len(cuts), high / len(cuts))
        return jnp.repeat(jnp.exp(steps), shape[dim] // shards_of).reshape((-1,) + (1,) * (len(shape) - dim - 1))

    loudness = one(*cuts[0])
    for cut in cuts[1:]:
        loudness = loudness * one(*cut)
    return loudness


def bell_draw(stream_key, extent, scale, limit, pieces=(), held_as=jnp.bfloat16):
    drawn = jax.random.normal(stream_key, extent, jnp.float32) * scale
    if len(pieces) > 0:
        drawn = steps_of(stream_key, extent, pieces, -0.22, 0.18) * drawn
    return jnp.clip(drawn, min=-limit, max=limit).astype(held_as)


def setup_inputs(seed: int = 0) -> dict:
    streams_of = jax.random.split(jax.random.key(seed), 8)
    labels = set_ends((jax.random.randint(streams_of[0], (SAMPLES,), 0, 2) < 1).astype(jnp.int32), jax.random.fold_in(streams_of[0], 1), 0, 1)
    beta = bell_draw(streams_of[1], (FEATURES,), 0.2, 1.2, ((0, 4),), jnp.float32)
    tile_rows = draw_tile_rows(jax.random.fold_in(streams_of[7], 71), 0)
    tile_cols = draw_tile_cols(jax.random.fold_in(streams_of[7], 71), 0)
    tile_values = bell_draw(streams_of[4], (N_SAMP, N_FEAT, TILES, TILE, TILE), TILE ** -0.5, 0.5, ((0, 8), (1, 4)))
    block_order = draw_block_order(jax.random.fold_in(streams_of[7], 71), 0)
    hess_inv = draw_hess_inv(jax.random.fold_in(streams_of[7], 71), 0)
    return dict(labels=labels, beta=beta, tile_rows=tile_rows, tile_cols=tile_cols, tile_values=tile_values, block_order=block_order, hess_inv=hess_inv)


exact_prec = lax.Precision.HIGHEST
l1_penalty = 0.25


def reference(labels, beta, tile_rows, tile_cols, tile_values, block_order, hess_inv):
    blocks = beta.reshape(N_FEAT, FEAT_BLOCKS, TILE)
    rounded_beta = blocks.astype(jnp.bfloat16).astype(jnp.float32)
    block_ids = jnp.arange(ROW_BLOCKS, dtype=jnp.int32)

    def margin_rows(packed):
        row_ids, col_ids, values = packed
        picked = jax.vmap(lambda table, index: table[index])(rounded_beta, col_ids)
        products = jnp.einsum("jkrc,jkc->jkr", values.astype(jnp.float32), picked, precision=exact_prec)
        placing = (row_ids[:, :, None] == block_ids[None, None, :]).astype(jnp.float32)
        partial_sum = jnp.einsum("jkb,jkr->jbr", placing, products, precision=exact_prec)
        return jnp.sum(partial_sum, axis=0)

    margins = lax.map(margin_rows, (tile_rows, tile_cols, tile_values))
    probability = jax.nn.sigmoid(margins)
    weight = (probability * (1.0 - probability)).reshape(N_SAMP, N_FEAT, GROUP_BLOCKS, TILE)
    residual = (labels.reshape(N_SAMP, ROW_BLOCKS, TILE).astype(jnp.float32) - probability).reshape(N_SAMP, N_FEAT, GROUP_BLOCKS, TILE)
    feat_ids = jnp.arange(N_FEAT, dtype=jnp.int32)
    sub_ids = jnp.arange(GROUP_BLOCKS, dtype=jnp.int32)
    for section_index in range(SECTIONS):
        groups = (feat_ids - section_index) % N_FEAT
        targets = block_order[:, section_index]
        inverses = hess_inv[:, section_index]

        def choose(row_ids, col_ids):
            offsets = row_ids - groups[:, None] * GROUP_BLOCKS
            matches = (col_ids == targets[:, None]) & (offsets >= 0) & (offsets < GROUP_BLOCKS)
            return ((offsets[:, :, None] == sub_ids[None, None, :]) & matches[:, :, None]).astype(jnp.float32)

        def gradient_part(packed):
            row_ids, col_ids, values, part_resid = packed
            chosen = choose(row_ids, col_ids)
            rounded = lax.optimization_barrier(part_resid[groups].astype(jnp.bfloat16)).astype(jnp.float32)
            resid_tiles = jnp.einsum("jkg,jgt->jkt", chosen, rounded, precision=exact_prec)
            return jnp.einsum("jkrc,jkr->jc", values.astype(jnp.float32), resid_tiles, precision=exact_prec)

        gradient = jnp.sum(lax.map(gradient_part, (tile_rows, tile_cols, tile_values, residual)), axis=0)
        current = blocks[feat_ids, targets]
        moved_block = current + jnp.einsum("jab,jb->ja", inverses, gradient, precision=exact_prec)
        shrunk = jnp.sign(moved_block) * jnp.maximum(jnp.abs(moved_block) - l1_penalty, 0.0)
        change = lax.optimization_barrier((shrunk - current).astype(jnp.bfloat16)).astype(jnp.float32)
        blocks = blocks.at[feat_ids, targets].set(shrunk)

        def update_part(packed):
            row_ids, col_ids, values, part_resid, part_weight = packed
            chosen = choose(row_ids, col_ids)
            image_rows = jnp.einsum("jkrc,jc->jkr", values.astype(jnp.float32), change, precision=exact_prec)
            landed = jnp.einsum("jkg,jkr->jgr", chosen, image_rows, precision=exact_prec)
            return part_resid.at[groups].set(part_resid[groups] - part_weight[groups] * landed)

        residual = lax.map(update_part, (tile_rows, tile_cols, tile_values, residual, weight))
    return blocks.reshape(-1), residual.reshape(-1)
```

```python
import jax
import jax.numpy as jnp
from jax import lax
from jax.sharding import PartitionSpec as P

exact_prec = lax.Precision.HIGHEST
l1_penalty = 0.25


def from_behind(value, axis, steps):
    count = lax.axis_size(axis)
    pairs = [(source, (source + steps) % count) for source in range(count)]
    return lax.ppermute(value, axis, pairs)


def exchange(parts, axis):
    return lax.all_to_all(parts, axis, 0, 0)


def per_device(labels, beta, tile_rows, tile_cols, tile_values, block_order, hess_inv):
    cycle_size = lax.axis_size("feat")
    samp_count = lax.axis_size("samp")
    my_index = lax.axis_index("feat")
    row_ids = tile_rows[0, 0]
    col_ids = tile_cols[0, 0]
    values = tile_values[0, 0]
    tile_edge = values.shape[-1]
    row_blocks = labels.shape[0] // tile_edge
    group_blocks = row_blocks // cycle_size
    blocks = beta.reshape(-1, tile_edge)
    picked = jnp.take(blocks, col_ids, axis=0, mode="clip").astype(jnp.bfloat16)
    products = jnp.einsum("krc,kc->kr", values, picked, preferred_element_type=jnp.float32)
    placing = (row_ids[:, None] == jnp.arange(row_blocks, dtype=jnp.int32)[None, :]).astype(
        jnp.float32
    )
    partial_sum = jnp.dot(placing.T, products, precision=exact_prec)
    parts = exchange(partial_sum.reshape(cycle_size, group_blocks, tile_edge), "feat")
    margins = jnp.sum(parts, axis=0)
    probability = jax.nn.sigmoid(margins)
    weight = probability * (1.0 - probability)
    own_labels = lax.dynamic_slice_in_dim(
        labels.reshape(row_blocks, tile_edge), my_index * group_blocks, group_blocks, 0
    )
    residual = own_labels.astype(jnp.float32) - probability
    sub_ids = jnp.arange(group_blocks, dtype=jnp.int32)
    inverses = hess_inv[0]
    targets = block_order[0]
    old_blocks = jnp.take(blocks, targets, axis=0, mode="clip")
    state = jnp.stack([residual, weight])
    for section in range(cycle_size):
        group_index = (my_index - section) % cycle_size
        target = targets[section]
        offsets = row_ids - group_index * group_blocks
        matches = (col_ids == target) & (offsets >= 0) & (offsets < group_blocks)
        chosen = (offsets[:, None] == sub_ids[None, :]) & matches[:, None]
        residual, weight = state[0], state[1]
        rounded = residual.astype(jnp.bfloat16)
        resid_tiles = jnp.dot(
            chosen.astype(jnp.bfloat16), rounded, preferred_element_type=jnp.float32
        ).astype(jnp.bfloat16)
        local_grad = jnp.einsum(
            "krc,kr->c", values, resid_tiles, preferred_element_type=jnp.float32
        )
        spread = jnp.broadcast_to(local_grad[None], (samp_count, tile_edge))
        gradient = jnp.sum(exchange(spread, "samp"), axis=0)
        current = old_blocks[section]
        moved_block = current + jnp.dot(inverses[section], gradient, precision=exact_prec)
        shrunk = jnp.sign(moved_block) * jnp.maximum(jnp.abs(moved_block) - l1_penalty, 0.0)
        change = (shrunk - current).astype(jnp.bfloat16)
        image_rows = jnp.einsum("krc,c->kr", values, change, preferred_element_type=jnp.float32)
        landed = jnp.dot(chosen.astype(jnp.float32).T, image_rows, precision=exact_prec)
        residual = residual - weight * landed
        blocks = lax.dynamic_update_index_in_dim(blocks, shrunk, target, 0)
        if section + 1 < cycle_size:
            state = from_behind(jnp.stack([residual, weight]), "feat", 1)
        else:
            residual = from_behind(residual, "feat", 1)
    return (blocks.reshape(-1), residual.reshape(-1))


def solution(mesh):
    placed = (
        P("samp"),
        P("feat"),
        P("samp", "feat", None),
        P("samp", "feat", None),
        P("samp", "feat", None, None, None),
        P("feat", None),
        P("feat", None, None, None),
    )
    return jax.shard_map(
        per_device,
        mesh=mesh,
        in_specs=placed,
        out_specs=(P("feat"), P(("samp", "feat"))),
        check_vma=False,
    )
```

```python
import jax
import jax.numpy as jnp
from jax import lax
from jax.sharding import PartitionSpec as P

exact_prec = lax.Precision.HIGHEST
l1_penalty = 0.25


def from_behind(value, axis, steps):
    count = lax.axis_size(axis)
    pairs = [(source, (source + steps) % count) for source in range(count)]
    return lax.ppermute(value, axis, pairs)


def exchange(parts, axis):
    return lax.all_to_all(parts, axis, 0, 0)


def summed(value, axis):
    count = lax.axis_size(axis)
    if count & (count - 1):
        return lax.psum(value, axis)
    distance = 1
    while distance < count:
        pairs = [(source, source ^ distance) for source in range(count)]
        value = value + lax.ppermute(value, axis, pairs)
        distance *= 2
    return value


def per_device(labels, beta, tile_rows, tile_cols, tile_values, block_order, hess_inv):
    cycle_size = lax.axis_size("feat")
    my_index = lax.axis_index("feat")
    row_ids = tile_rows[0, 0]
    col_ids = tile_cols[0, 0]
    values = tile_values[0, 0]
    tile_edge = values.shape[-1]
    row_blocks = labels.shape[0] // tile_edge
    group_blocks = row_blocks // cycle_size
    blocks = beta.reshape(-1, tile_edge)
    picked = jnp.take(blocks, col_ids, axis=0, mode="clip").astype(jnp.bfloat16)
    products = jnp.einsum("krc,kc->kr", values, picked, preferred_element_type=jnp.float32)
    placing = (row_ids[:, None] == jnp.arange(row_blocks, dtype=jnp.int32)[None, :]).astype(
        jnp.float32
    )
    partial_sum = jnp.dot(placing.T, products, precision=exact_prec)
    parts = exchange(partial_sum.reshape(cycle_size, group_blocks, tile_edge), "feat")
    margins = jnp.sum(parts, axis=0)
    probability = jax.nn.sigmoid(margins)
    weight = probability * (1.0 - probability)
    own_labels = lax.dynamic_slice_in_dim(
        labels.reshape(row_blocks, tile_edge), my_index * group_blocks, group_blocks, 0
    )
    residual = own_labels.astype(jnp.float32) - probability
    sub_ids = jnp.arange(group_blocks, dtype=jnp.int32)
    inverses = hess_inv[0]
    targets = block_order[0]
    old_blocks = jnp.take(blocks, targets, axis=0, mode="clip")
    state = jnp.stack([residual, weight])
    for section in range(cycle_size):
        group_index = (my_index - section) % cycle_size
        target = targets[section]
        offsets = row_ids - group_index * group_blocks
        matches = (col_ids == target) & (offsets >= 0) & (offsets < group_blocks)
        chosen = (offsets[:, None] == sub_ids[None, :]) & matches[:, None]
        residual, weight = state[0], state[1]
        rounded = residual.astype(jnp.bfloat16)
        resid_tiles = jnp.dot(
            chosen.astype(jnp.bfloat16), rounded, preferred_element_type=jnp.float32
        ).astype(jnp.bfloat16)
        local_grad = jnp.einsum(
            "krc,kr->c", values, resid_tiles, preferred_element_type=jnp.float32
        )
        gradient = summed(local_grad, "samp")
        current = old_blocks[section]
        moved_block = current + jnp.dot(inverses[section], gradient, precision=exact_prec)
        shrunk = jnp.sign(moved_block) * jnp.maximum(jnp.abs(moved_block) - l1_penalty, 0.0)
        change = (shrunk - current).astype(jnp.bfloat16)
        image_rows = jnp.einsum("krc,c->kr", values, change, preferred_element_type=jnp.float32)
        landed = jnp.dot(chosen.astype(jnp.float32).T, image_rows, precision=exact_prec)
        residual = residual - weight * landed
        blocks = lax.dynamic_update_index_in_dim(blocks, shrunk, target, 0)
        if section + 1 < cycle_size:
            state = from_behind(jnp.stack([residual, weight]), "feat", 1)
        else:
            residual = from_behind(residual, "feat", 1)
    return (blocks.reshape(-1), residual.reshape(-1))


def solution(mesh):
    placed = (
        P("samp"),
        P("feat"),
        P("samp", "feat", None),
        P("samp", "feat", None),
        P("samp", "feat", None, None, None),
        P("feat", None),
        P("feat", None, None, None),
    )
    return jax.shard_map(
        per_device,
        mesh=mesh,
        in_specs=placed,
        out_specs=(P("feat"), P(("samp", "feat"))),
        check_vma=False,
    )
```

```python
import jax
import jax.numpy as jnp
from jax import lax
from jax.sharding import PartitionSpec as P

exact_prec = lax.Precision.HIGHEST
l1_penalty = 0.25
both_axes = ("samp", "feat")


def on_planes(samp_pairs, planes):
    count = lax.axis_size("feat")
    return [
        (source * count + plane, target * count + plane)
        for plane in planes
        for source, target in samp_pairs
    ]


def summed(value, planes):
    count = lax.axis_size("samp")
    if count < 2 or count & (count - 1):
        return lax.psum(value, "samp")
    inward = [(even, even + 1) for even in range(0, count, 2)]
    value = value + lax.ppermute(value, both_axes, on_planes(inward, planes))
    distance = 2
    while distance < count:
        across = [(odd, odd ^ distance) for odd in range(1, count, 2)]
        value = value + lax.ppermute(value, both_axes, on_planes(across, planes))
        distance *= 2
    outward = [(even + 1, even) for even in range(0, count, 2)]
    copied = lax.ppermute(value, both_axes, on_planes(outward, planes))
    return jnp.where(lax.axis_index("samp") % 2 == 1, value, copied)


def to_next(value, planes):
    samp_count, feat_count = lax.axis_size("samp"), lax.axis_size("feat")
    pairs = [
        (row * feat_count + plane, row * feat_count + (plane + 1) % feat_count)
        for row in range(samp_count)
        for plane in planes
    ]
    return lax.ppermute(value, both_axes, pairs)


def per_device(labels, beta, tile_rows, tile_cols, tile_values, block_order, hess_inv):
    cycle_size = lax.axis_size("feat")
    strand_count = 2 if cycle_size % 2 == 0 else 1
    my_index = lax.axis_index("feat")
    row_ids = tile_rows[0, 0]
    col_ids = tile_cols[0, 0]
    values = tile_values[0, 0]
    tile_edge = values.shape[-1]
    row_blocks = labels.shape[0] // tile_edge
    group_blocks = row_blocks // cycle_size
    blocks = beta.reshape(-1, tile_edge)
    picked = jnp.take(blocks, col_ids, axis=0, mode="clip").astype(jnp.bfloat16)
    products = jnp.einsum("krc,kc->kr", values, picked, preferred_element_type=jnp.float32)
    placing = (row_ids[:, None] == jnp.arange(row_blocks, dtype=jnp.int32)[None, :]).astype(
        jnp.float32
    )
    partial_sum = jnp.dot(placing.T, products, precision=exact_prec)
    parts = lax.all_to_all(
        partial_sum.reshape(cycle_size, group_blocks, tile_edge), "feat", 0, 0
    )
    margins = jnp.sum(parts, axis=0)
    probability = jax.nn.sigmoid(margins)
    first_weight = probability * (1.0 - probability)
    own_labels = lax.dynamic_slice_in_dim(
        labels.reshape(row_blocks, tile_edge), my_index * group_blocks, group_blocks, 0
    )
    first_residual = own_labels.astype(jnp.float32) - probability
    sub_ids = jnp.arange(group_blocks, dtype=jnp.int32)
    inverses = hess_inv[0]
    targets = block_order[0]
    old_blocks = jnp.take(blocks, targets, axis=0, mode="clip")
    chosen = []
    for section in range(cycle_size):
        offsets = row_ids - ((my_index - section) % cycle_size) * group_blocks
        matches = (col_ids == targets[section]) & (offsets >= 0) & (offsets < group_blocks)
        chosen.append((offsets[:, None] == sub_ids[None, :]) & matches[:, None])

    def update(section, residual, weight, planes):
        rounded = residual.astype(jnp.bfloat16)
        resid_tiles = jnp.dot(
            chosen[section].astype(jnp.bfloat16), rounded, preferred_element_type=jnp.float32
        ).astype(jnp.bfloat16)
        local_grad = jnp.einsum(
            "krc,kr->c", values, resid_tiles, preferred_element_type=jnp.float32
        )
        gradient = summed(local_grad, planes)
        current = old_blocks[section]
        moved_block = current + jnp.dot(inverses[section], gradient, precision=exact_prec)
        shrunk = jnp.sign(moved_block) * jnp.maximum(jnp.abs(moved_block) - l1_penalty, 0.0)
        change = (shrunk - current).astype(jnp.bfloat16)
        image_rows = jnp.einsum("krc,c->kr", values, change, preferred_element_type=jnp.float32)
        landed = jnp.dot(chosen[section].astype(jnp.float32).T, image_rows, precision=exact_prec)
        return shrunk, residual - weight * landed

    state = jnp.stack([first_residual, first_weight])
    states = [state] * strand_count
    for section in range(cycle_size):
        shrunk_block = None
        for strand in range(strand_count):
            planes = [
                plane
                for plane in range(cycle_size)
                if (plane - section - strand) % strand_count == 0
            ]
            active = (my_index - section - strand) % strand_count == 0

            def work(state, section=section, planes=planes):
                shrunk, residual = update(section, state[0], state[1], planes)
                if section + 1 < cycle_size:
                    return shrunk, jnp.stack([residual, state[1]])
                return shrunk, residual

            def rest(state, section=section):
                kept = state if section + 1 < cycle_size else state[0]
                return jnp.zeros((tile_edge,), jnp.float32), kept

            shrunk, moving = lax.cond(active, work, rest, states[strand])
            later = (strand + 1) % strand_count
            if later != strand and (section + 1 < cycle_size or strand + 1 < strand_count):
                moving, states[later] = lax.optimization_barrier((moving, states[later]))
            states[strand] = to_next(moving, planes)
            shrunk_block = shrunk if strand == 0 else jnp.where(active, shrunk, shrunk_block)
        blocks = lax.dynamic_update_index_in_dim(blocks, shrunk_block, targets[section], 0)
    results = states
    residual = results[0]
    if strand_count == 2:
        from_first = (my_index - cycle_size) % strand_count == 0
        residual = jnp.where(from_first, results[0], results[1])
    return (blocks.reshape(-1), residual.reshape(-1))


def solution(mesh):
    placed = (
        P("samp"),
        P("feat"),
        P("samp", "feat", None),
        P("samp", "feat", None),
        P("samp", "feat", None, None, None),
        P("feat", None),
        P("feat", None, None, None),
    )
    return jax.shard_map(
        per_device,
        mesh=mesh,
        in_specs=placed,
        out_specs=(P("feat"), P(("samp", "feat"))),
        check_vma=False,
    )
```

```python
import functools

import jax
import jax.numpy as jnp
from jax import lax
from jax.experimental import pallas as pl
from jax.experimental.pallas import tpu as pltpu
from jax.sharding import PartitionSpec as P

exact_prec = lax.Precision.HIGHEST
l1_penalty = 0.25
chunk = 16

VMEM = pl.BlockSpec(memory_space=pltpu.VMEM)
SMEM = pl.BlockSpec(memory_space=pltpu.SMEM)


def float_of(shape):
    return jax.ShapeDtypeStruct(shape, jnp.float32)


def call(kernel, out_shape, in_specs):
    single = not isinstance(out_shape, tuple)
    return pl.pallas_call(
        kernel,
        out_shape=out_shape,
        in_specs=in_specs,
        out_specs=VMEM if single else tuple(VMEM for _ in out_shape),
        compiler_params=pltpu.CompilerParams(vmem_limit_bytes=24 << 20),
    )


def tile_products(vectors_of, values_ref):
    tiles, edge, _ = values_ref.shape
    sub = lax.broadcasted_iota(jnp.int32, (chunk, edge), 0)
    pieces = []
    for first in range(0, tiles, chunk):
        vectors = vectors_of(first)
        piece = jnp.zeros((chunk, edge), jnp.float32)
        for inner in range(chunk):
            product = lax.dot_general(
                vectors,
                values_ref[first + inner],
                (((1,), (1,)), ((), ())),
                preferred_element_type=jnp.float32,
            )
            piece = jnp.where(sub == inner, product, piece)
        pieces.append(piece)
    return jnp.concatenate(pieces, axis=0)


def margins_kernel(
    cols_smem, targets_smem, rows_ref, cols_ref, beta_ref, values_ref,
    partial_ref, chosen_ref, old_ref, picked_ref,
):
    tiles = cols_smem.shape[0]
    sections = targets_smem.shape[0]
    row_blocks = partial_ref.shape[0]
    group_blocks = chosen_ref.shape[1]
    for tile in range(tiles):
        picked_ref[pl.ds(tile, 1), :] = beta_ref[pl.ds(cols_smem[tile], 1), :]

    def vectors_of(first):
        return picked_ref[pl.ds(first, chunk), :].astype(jnp.bfloat16)

    products = tile_products(vectors_of, values_ref)
    rows = rows_ref[...]
    block_ids = lax.broadcasted_iota(jnp.int32, (row_blocks, tiles), 0)
    placing = (block_ids == rows).astype(jnp.float32)
    partial_ref[...] = jnp.dot(
        placing, products, precision=exact_prec, preferred_element_type=jnp.float32
    )
    my_index = lax.axis_index("feat")
    sub_ids = lax.broadcasted_iota(jnp.int32, (group_blocks, tiles), 0)
    for section in range(sections):
        group = lax.rem(my_index - section + sections, sections)
        hit = (sub_ids + group * group_blocks == rows) & (cols_ref[...] == targets_smem[section])
        chosen_ref[section] = hit.astype(jnp.float32)
        old_ref[pl.ds(section, 1), :] = beta_ref[pl.ds(targets_smem[section], 1), :]


def gradient_part(residual, chosen, values_ref):
    tiles, edge, _ = values_ref.shape
    picked = lax.dot_general(
        chosen.astype(jnp.bfloat16),
        residual.astype(jnp.bfloat16),
        (((0,), (0,)), ((), ())),
        preferred_element_type=jnp.float32,
    )
    sub = lax.broadcasted_iota(jnp.int32, (chunk, edge), 0)
    spread = []
    for tile in range(tiles):
        first = tile - tile % chunk
        kept = jnp.where(sub == tile - first, picked[first : first + chunk], 0.0)
        spread.append(kept.astype(jnp.bfloat16))
    summed = jnp.dot(
        jnp.concatenate(spread, axis=1),
        values_ref[...].reshape(tiles * edge, edge),
        preferred_element_type=jnp.float32,
    )
    return jnp.sum(summed, axis=0, keepdims=True)


def first_kernel(parts_ref, labels_ref, chosen_ref, values_ref, state_ref, grad_ref):
    group_blocks = parts_ref.shape[1]
    start = pl.multiple_of(lax.axis_index("feat") * group_blocks, 8)
    margins = parts_ref[0]
    for part in range(1, parts_ref.shape[0]):
        margins = margins + parts_ref[part]
    probability = 1.0 / (1.0 + jnp.exp(-margins))
    residual = labels_ref[pl.ds(start, group_blocks), :].astype(jnp.float32) - probability
    state_ref[0] = residual
    state_ref[1] = probability * (1.0 - probability)
    grad = gradient_part(residual, chosen_ref[0], values_ref)
    grad_ref[...] = jnp.broadcast_to(grad, grad_ref.shape)


def gradient_kernel(section, state_ref, chosen_ref, values_ref, grad_ref):
    grad = gradient_part(state_ref[0], chosen_ref[section], values_ref)
    grad_ref[...] = jnp.broadcast_to(grad, grad_ref.shape)


def update_kernel(
    section, grads_ref, state_ref, chosen_ref, old_ref, inverses_ref, values_ref,
    moved_ref, shrunk_ref,
):
    edge = grads_ref.shape[1]
    gradient = jnp.sum(grads_ref[...], axis=0, keepdims=True)
    step = lax.dot_general(
        jnp.broadcast_to(gradient, (8, edge)),
        inverses_ref[section],
        (((1,), (1,)), ((), ())),
        precision=exact_prec,
        preferred_element_type=jnp.float32,
    )
    old = old_ref[pl.ds(section, 1), :]
    raised = old + step
    size = jnp.maximum(jnp.abs(raised) - l1_penalty, 0.0)
    shrunk = jnp.where(raised < 0.0, -size, size)
    shrunk_ref[...] = shrunk[0:1]
    change = jnp.broadcast_to((shrunk - old)[0:1], (chunk, edge)).astype(jnp.bfloat16)
    image = tile_products(lambda first: change, values_ref)
    landed = jnp.dot(
        chosen_ref[section], image, precision=exact_prec, preferred_element_type=jnp.float32
    )
    weight = state_ref[1]
    residual = state_ref[0] - weight * landed
    if len(moved_ref.shape) == 3:
        moved_ref[0] = residual
        moved_ref[1] = weight
    else:
        moved_ref[...] = residual


def from_behind(value, axis, steps):
    count = lax.axis_size(axis)
    pairs = [(source, (source + steps) % count) for source in range(count)]
    return lax.ppermute(value, axis, pairs)


def gathered(parts, axis):
    count, edge = parts.shape
    return lax.all_to_all(parts.reshape(count, 1, edge), axis, 0, 0).reshape(count, edge)


def per_device(labels, beta, tile_rows, tile_cols, tile_values, block_order, hess_inv):
    sections = lax.axis_size("feat")
    samp_count = lax.axis_size("samp")
    values = tile_values[0, 0]
    tiles, edge, _ = values.shape
    row_blocks = labels.shape[0] // edge
    group_blocks = row_blocks // sections
    blocks = beta.reshape(-1, edge)
    inverses = hess_inv[0]
    targets = block_order[0]
    partial_sum, chosen, old_blocks = pl.pallas_call(
        margins_kernel,
        out_shape=(
            float_of((row_blocks, edge)),
            float_of((sections, group_blocks, tiles)),
            float_of((sections, edge)),
        ),
        in_specs=[SMEM, SMEM, VMEM, VMEM, VMEM, VMEM],
        out_specs=(VMEM, VMEM, VMEM),
        scratch_shapes=[pltpu.VMEM((tiles, edge), jnp.float32)],
        compiler_params=pltpu.CompilerParams(vmem_limit_bytes=24 << 20),
    )(tile_cols[0, 0], targets, tile_rows[0], tile_cols[0], blocks, values)
    parts = lax.all_to_all(partial_sum.reshape(sections, group_blocks, edge), "feat", 0, 0)
    state, grads = call(
        first_kernel,
        (float_of((2, group_blocks, edge)), float_of((samp_count, edge))),
        [VMEM] * 4,
    )(parts, labels.reshape(row_blocks, edge), chosen, values)
    shrunk_blocks = []
    for section in range(sections):
        final = section + 1 == sections
        moved_shape = (group_blocks, edge) if final else (2, group_blocks, edge)
        moving, shrunk = call(
            functools.partial(update_kernel, section),
            (float_of(moved_shape), float_of((1, edge))),
            [VMEM] * 6,
        )(gathered(grads, "samp"), state, chosen, old_blocks, inverses, values)
        shrunk_blocks.append(shrunk)
        state = from_behind(moving, "feat", 1)
        if not final:
            grads = call(
                functools.partial(gradient_kernel, section + 1),
                float_of((samp_count, edge)),
                [VMEM] * 3,
            )(state, chosen, values)
    block_ids = jnp.arange(blocks.shape[0], dtype=jnp.int32)[:, None]
    for section in range(sections):
        blocks = jnp.where(block_ids == targets[section], shrunk_blocks[section], blocks)
    return (blocks.reshape(-1), state.reshape(-1))


def solution(mesh):
    placed = (
        P("samp"),
        P("feat"),
        P("samp", "feat", None),
        P("samp", "feat", None),
        P("samp", "feat", None, None, None),
        P("feat", None),
        P("feat", None, None, None),
    )
    return jax.shard_map(
        per_device,
        mesh=mesh,
        in_specs=placed,
        out_specs=(P("feat"), P(("samp", "feat"))),
        check_vma=False,
    )
```

```python
import functools

import jax
import jax.numpy as jnp
from jax import lax
from jax.experimental import pallas as pl
from jax.experimental.pallas import tpu as pltpu
from jax.sharding import PartitionSpec as P

exact_prec = lax.Precision.HIGHEST
l1_penalty = 0.25
chunk = 16

VMEM = pl.BlockSpec(memory_space=pltpu.VMEM)
SMEM = pl.BlockSpec(memory_space=pltpu.SMEM)
HBM = pl.BlockSpec(memory_space=pltpu.HBM)


def float_of(shape):
    return jax.ShapeDtypeStruct(shape, jnp.float32)


def call(kernel, out_shape, in_specs):
    single = not isinstance(out_shape, tuple)
    return pl.pallas_call(
        kernel,
        out_shape=out_shape,
        in_specs=in_specs,
        out_specs=VMEM if single else tuple(VMEM for _ in out_shape),
        compiler_params=pltpu.CompilerParams(vmem_limit_bytes=24 << 20),
    )


def tile_products(vectors_of, tiles_of, tiles):
    pieces = []
    for first in range(0, tiles, chunk):
        vectors = vectors_of(first)
        edge = vectors.shape[1]
        products = lax.dot_general(
            vectors,
            tiles_of(first).reshape(chunk * edge, edge),
            (((1,), (1,)), ((), ())),
            preferred_element_type=jnp.float32,
        )
        sub = lax.broadcasted_iota(jnp.int32, (chunk, edge), 0)
        piece = products[:, :edge]
        for inner in range(1, chunk):
            piece = jnp.where(sub == inner, products[:, inner * edge : (inner + 1) * edge], piece)
        pieces.append(piece)
    return jnp.concatenate(pieces, axis=0)


def placed_sum(chosen, rows):
    high = rows.astype(jnp.bfloat16)
    rest = rows - high.astype(jnp.float32)
    middle = rest.astype(jnp.bfloat16)
    low = (rest - middle.astype(jnp.float32)).astype(jnp.bfloat16)
    ones = chosen.astype(jnp.bfloat16)
    return sum(
        jnp.dot(ones, part, preferred_element_type=jnp.float32) for part in (low, middle, high)
    )


def margins_kernel(
    cols_hbm, targets_hbm, rows_hbm, beta_hbm, values_hbm, partial_ref, old_ref,
    picked_ref, beta_ref, rows_ref, values_ref, cols_smem, targets_smem, small_sem, tile_sem,
):
    tiles = cols_smem.shape[1]
    sections = targets_smem.shape[1]
    row_blocks = partial_ref.shape[0]
    small = [
        pltpu.make_async_copy(cols_hbm, cols_smem, small_sem.at[0]),
        pltpu.make_async_copy(beta_hbm, beta_ref, small_sem.at[1]),
        pltpu.make_async_copy(targets_hbm, targets_smem, small_sem.at[2]),
        pltpu.make_async_copy(rows_hbm, rows_ref, small_sem.at[3]),
    ]
    large = [
        pltpu.make_async_copy(
            values_hbm.at[pl.ds(first, chunk)],
            values_ref.at[pl.ds(first, chunk)],
            tile_sem.at[first // chunk],
        )
        for first in range(0, tiles, chunk)
    ]
    for copy in small + large:
        copy.start()
    for copy in small:
        copy.wait()
    for tile in range(tiles):
        picked_ref[pl.ds(tile, 1), :] = beta_ref[pl.ds(cols_smem[0, tile], 1), :]
    for section in range(sections):
        old_ref[pl.ds(section, 1), :] = beta_ref[pl.ds(targets_smem[0, section], 1), :]

    def tiles_of(first):
        large[first // chunk].wait()
        return values_ref[pl.ds(first, chunk)]

    products = tile_products(
        lambda first: picked_ref[pl.ds(first, chunk), :].astype(jnp.bfloat16), tiles_of, tiles
    )
    block_ids = lax.broadcasted_iota(jnp.int32, (row_blocks, tiles), 0)
    placing = (block_ids == rows_ref[...]).astype(jnp.float32)
    partial_ref[...] = placed_sum(placing, products)


def gradient_part(residual, chosen, values_ref):
    tiles, edge, _ = values_ref.shape
    picked = lax.dot_general(
        chosen.astype(jnp.bfloat16),
        residual.astype(jnp.bfloat16),
        (((0,), (0,)), ((), ())),
        preferred_element_type=jnp.float32,
    )
    sub = lax.broadcasted_iota(jnp.int32, (chunk, edge), 0)
    spread = []
    for tile in range(tiles):
        first = tile - tile % chunk
        kept = jnp.where(sub == tile - first, picked[first : first + chunk], 0.0)
        spread.append(kept.astype(jnp.bfloat16))
    summed = jnp.dot(
        jnp.concatenate(spread, axis=1),
        values_ref[...].reshape(tiles * edge, edge),
        preferred_element_type=jnp.float32,
    )
    return jnp.sum(summed, axis=0, keepdims=True)


def first_kernel(
    parts_ref, labels_ref, rows_ref, cols_ref, targets_ref, values_ref,
    state_ref, grad_ref, chosen_ref,
):
    sections, group_blocks, _ = parts_ref.shape
    my_index = lax.axis_index("feat")
    sub_ids = lax.broadcasted_iota(jnp.int32, chosen_ref.shape[1:], 0)
    for section in range(sections):
        group = lax.rem(my_index - section + sections, sections)
        same_row = sub_ids + group * group_blocks == rows_ref[...]
        same_col = cols_ref[...] == targets_ref[:, section : section + 1]
        chosen_ref[section] = (same_row & same_col).astype(jnp.float32)
    start = pl.multiple_of(my_index * group_blocks, 8)
    margins = parts_ref[0]
    for part in range(1, parts_ref.shape[0]):
        margins = margins + parts_ref[part]
    probability = 1.0 / (1.0 + jnp.exp(-margins))
    residual = labels_ref[pl.ds(start, group_blocks), :].astype(jnp.float32) - probability
    state_ref[0] = residual
    state_ref[1] = probability * (1.0 - probability)
    grad = gradient_part(residual, chosen_ref[0], values_ref)
    grad_ref[...] = jnp.broadcast_to(grad, grad_ref.shape)


def gradient_kernel(section, state_ref, chosen_ref, values_ref, grad_ref):
    grad = gradient_part(state_ref[0], chosen_ref[section], values_ref)
    grad_ref[...] = jnp.broadcast_to(grad, grad_ref.shape)


def update_kernel(
    section, grads_ref, state_ref, chosen_ref, old_ref, inverses_ref, values_ref,
    moved_ref, shrunk_ref,
):
    tiles, edge, _ = values_ref.shape
    gradient = jnp.sum(grads_ref[...], axis=0, keepdims=True)
    step = jnp.sum(inverses_ref[section] * gradient, axis=1, keepdims=True)
    square = (edge, edge)
    on_diagonal = lax.broadcasted_iota(jnp.int32, square, 0) == lax.broadcasted_iota(
        jnp.int32, square, 1
    )
    step = jnp.sum(jnp.where(on_diagonal, step, 0.0), axis=0, keepdims=True)
    old = old_ref[pl.ds(section, 1), :]
    raised = old + step
    size = jnp.maximum(jnp.abs(raised) - l1_penalty, 0.0)
    shrunk = jnp.where(raised < 0.0, -size, size)
    shrunk_ref[...] = shrunk
    change = jnp.broadcast_to(shrunk - old, (chunk, edge)).astype(jnp.bfloat16)
    image = tile_products(
        lambda first: change, lambda first: values_ref[pl.ds(first, chunk)], tiles
    )
    landed = placed_sum(chosen_ref[section], image)
    weight = state_ref[1]
    residual = state_ref[0] - weight * landed
    if len(moved_ref.shape) == 3:
        moved_ref[0] = residual
        moved_ref[1] = weight
    else:
        moved_ref[...] = residual


def blocks_kernel(sections, targets_smem, beta_ref, *refs):
    blocks_ref = refs[sections]
    blocks_ref[...] = beta_ref[...]
    for section in range(sections):
        blocks_ref[pl.ds(targets_smem[0, section], 1), :] = refs[section][...]


def from_behind(value, axis, steps):
    count = lax.axis_size(axis)
    pairs = [(source, (source + steps) % count) for source in range(count)]
    return lax.ppermute(value, axis, pairs)


def gathered(parts, axis):
    count, edge = parts.shape
    return lax.all_to_all(parts.reshape(count, 1, edge), axis, 0, 0).reshape(count, edge)


def per_device(labels, beta, tile_rows, tile_cols, tile_values, block_order, hess_inv):
    sections = lax.axis_size("feat")
    samp_count = lax.axis_size("samp")
    tiles, edge = tile_values.shape[2], tile_values.shape[4]
    row_blocks = labels.shape[0] // edge
    group_blocks = row_blocks // sections
    blocks = beta.reshape(-1, edge)
    inverses = hess_inv[0]
    values = tile_values[0, 0]
    partial_sum, old_blocks = pl.pallas_call(
        margins_kernel,
        out_shape=(float_of((row_blocks, edge)), float_of((sections, edge))),
        in_specs=[HBM] * 5,
        out_specs=(VMEM, VMEM),
        scratch_shapes=[
            pltpu.VMEM((tiles, edge), jnp.float32),
            pltpu.VMEM(blocks.shape, jnp.float32),
            pltpu.VMEM((1, tiles), jnp.int32),
            pltpu.VMEM(values.shape, jnp.bfloat16),
            pltpu.SMEM((1, tiles), jnp.int32),
            pltpu.SMEM((1, sections), jnp.int32),
            pltpu.SemaphoreType.DMA((4,)),
            pltpu.SemaphoreType.DMA((tiles // chunk,)),
        ],
        compiler_params=pltpu.CompilerParams(vmem_limit_bytes=58 << 20),
    )(tile_cols[0], block_order, tile_rows[0], blocks, values)
    parts = lax.all_to_all(partial_sum.reshape(sections, group_blocks, edge), "feat", 0, 0)
    state, grads, chosen = call(
        first_kernel,
        (
            float_of((2, group_blocks, edge)),
            float_of((samp_count, edge)),
            float_of((sections, group_blocks, tiles)),
        ),
        [VMEM] * 6,
    )(parts, labels.reshape(row_blocks, edge), tile_rows[0], tile_cols[0], block_order, values)
    shrunk_blocks = []
    for section in range(sections):
        final = section + 1 == sections
        moved_shape = (group_blocks, edge) if final else (2, group_blocks, edge)
        moving, shrunk = call(
            functools.partial(update_kernel, section),
            (float_of(moved_shape), float_of((1, edge))),
            [VMEM] * 6,
        )(gathered(grads, "samp"), state, chosen, old_blocks, inverses, values)
        shrunk_blocks.append(shrunk)
        state = from_behind(moving, "feat", 1)
        if not final:
            grads = call(
                functools.partial(gradient_kernel, section + 1),
                float_of((samp_count, edge)),
                [VMEM] * 3,
            )(state, chosen, values)
    blocks = call(
        functools.partial(blocks_kernel, sections),
        float_of(blocks.shape),
        [SMEM] + [VMEM] * (1 + sections),
    )(block_order, blocks, *shrunk_blocks)
    return (blocks.reshape(-1), state.reshape(-1))


def solution(mesh):
    placed = (
        P("samp"),
        P("feat"),
        P("samp", "feat", None),
        P("samp", "feat", None),
        P("samp", "feat", None, None, None),
        P("feat", None),
        P("feat", None, None, None),
    )
    return jax.shard_map(
        per_device,
        mesh=mesh,
        in_specs=placed,
        out_specs=(P("feat"), P(("samp", "feat"))),
        check_vma=False,
    )
```

```python
import functools

import jax
import jax.numpy as jnp
from jax import lax
from jax.experimental import pallas as pl
from jax.experimental.pallas import tpu as pltpu
from jax.sharding import PartitionSpec as P

exact_prec = lax.Precision.HIGHEST
l1_penalty = 0.25
chunk = 16

VMEM = pl.BlockSpec(memory_space=pltpu.VMEM)
SMEM = pl.BlockSpec(memory_space=pltpu.SMEM)
HBM = pl.BlockSpec(memory_space=pltpu.HBM)


def float_of(shape):
    return jax.ShapeDtypeStruct(shape, jnp.float32)


def call(kernel, out_shape, in_specs):
    single = not isinstance(out_shape, tuple)
    return pl.pallas_call(
        kernel,
        out_shape=out_shape,
        in_specs=in_specs,
        out_specs=VMEM if single else tuple(VMEM for _ in out_shape),
        compiler_params=pltpu.CompilerParams(vmem_limit_bytes=24 << 20),
    )


def tile_products(vectors_of, tiles_of, tiles):
    pieces = []
    for first in range(0, tiles, chunk):
        vectors = vectors_of(first)
        edge = vectors.shape[1]
        products = lax.dot_general(
            vectors,
            tiles_of(first).reshape(chunk * edge, edge),
            (((1,), (1,)), ((), ())),
            preferred_element_type=jnp.float32,
        )
        sub = lax.broadcasted_iota(jnp.int32, (chunk, edge), 0)
        piece = products[:, :edge]
        for inner in range(1, chunk):
            piece = jnp.where(sub == inner, products[:, inner * edge : (inner + 1) * edge], piece)
        pieces.append(piece)
    return jnp.concatenate(pieces, axis=0)


def placed_sum(chosen, rows):
    high = rows.astype(jnp.bfloat16)
    rest = rows - high.astype(jnp.float32)
    middle = rest.astype(jnp.bfloat16)
    low = (rest - middle.astype(jnp.float32)).astype(jnp.bfloat16)
    ones = chosen.astype(jnp.bfloat16)
    return sum(
        jnp.dot(ones, part, preferred_element_type=jnp.float32) for part in (low, middle, high)
    )


def margins_kernel(
    cols_hbm, targets_hbm, rows_hbm, beta_hbm, values_hbm, partial_ref, old_ref,
    picked_ref, beta_ref, rows_ref, values_ref, cols_smem, targets_smem, small_sem, tile_sem,
):
    tiles = cols_smem.shape[1]
    sections = targets_smem.shape[1]
    row_blocks = partial_ref.shape[0]
    small = [
        pltpu.make_async_copy(cols_hbm, cols_smem, small_sem.at[0]),
        pltpu.make_async_copy(beta_hbm, beta_ref, small_sem.at[1]),
        pltpu.make_async_copy(targets_hbm, targets_smem, small_sem.at[2]),
        pltpu.make_async_copy(rows_hbm, rows_ref, small_sem.at[3]),
    ]
    large = [
        pltpu.make_async_copy(
            values_hbm.at[pl.ds(first, chunk)],
            values_ref.at[pl.ds(first, chunk)],
            tile_sem.at[first // chunk],
        )
        for first in range(0, tiles, chunk)
    ]
    for copy in small + large:
        copy.start()
    for copy in small:
        copy.wait()
    for tile in range(tiles):
        picked_ref[pl.ds(tile, 1), :] = beta_ref[pl.ds(cols_smem[0, tile], 1), :]
    for section in range(sections):
        old_ref[pl.ds(section, 1), :] = beta_ref[pl.ds(targets_smem[0, section], 1), :]

    def tiles_of(first):
        large[first // chunk].wait()
        return values_ref[pl.ds(first, chunk)]

    products = tile_products(
        lambda first: picked_ref[pl.ds(first, chunk), :].astype(jnp.bfloat16), tiles_of, tiles
    )
    block_ids = lax.broadcasted_iota(jnp.int32, (row_blocks, tiles), 0)
    placing = (block_ids == rows_ref[...]).astype(jnp.float32)
    partial_ref[...] = placed_sum(placing, products)


def gradient_part(residual, chosen, values_ref):
    tiles, edge, _ = values_ref.shape
    picked = lax.dot_general(
        chosen.astype(jnp.bfloat16),
        residual.astype(jnp.bfloat16),
        (((0,), (0,)), ((), ())),
        preferred_element_type=jnp.float32,
    )
    sub = lax.broadcasted_iota(jnp.int32, (chunk, edge), 0)
    spread = []
    for tile in range(tiles):
        first = tile - tile % chunk
        kept = jnp.where(sub == tile - first, picked[first : first + chunk], 0.0)
        spread.append(kept.astype(jnp.bfloat16))
    summed = jnp.dot(
        jnp.concatenate(spread, axis=1),
        values_ref[...].reshape(tiles * edge, edge),
        preferred_element_type=jnp.float32,
    )
    return jnp.sum(summed, axis=0, keepdims=True)


def first_kernel(
    parts_ref, labels_ref, rows_ref, cols_ref, targets_ref, values_ref,
    state_ref, grad_ref, chosen_ref,
):
    sections, group_blocks, _ = parts_ref.shape
    my_index = lax.axis_index("feat")
    sub_ids = lax.broadcasted_iota(jnp.int32, chosen_ref.shape[1:], 0)
    for section in range(sections):
        group = lax.rem(my_index - section + sections, sections)
        same_row = sub_ids + group * group_blocks == rows_ref[...]
        same_col = cols_ref[...] == targets_ref[:, section : section + 1]
        chosen_ref[section] = (same_row & same_col).astype(jnp.float32)
    start = pl.multiple_of(my_index * group_blocks, 8)
    margins = parts_ref[0]
    for part in range(1, parts_ref.shape[0]):
        margins = margins + parts_ref[part]
    probability = 1.0 / (1.0 + jnp.exp(-margins))
    residual = labels_ref[pl.ds(start, group_blocks), :].astype(jnp.float32) - probability
    state_ref[0] = residual
    state_ref[1] = probability * (1.0 - probability)
    grad = gradient_part(residual, chosen_ref[0], values_ref)
    grad_ref[...] = jnp.broadcast_to(grad, grad_ref.shape)


def gradient_kernel(section, state_ref, chosen_ref, values_ref, grad_ref):
    grad = gradient_part(state_ref[0], chosen_ref[section], values_ref)
    grad_ref[...] = jnp.broadcast_to(grad, grad_ref.shape)


def update_kernel(
    section, grads_ref, state_ref, chosen_ref, old_ref, inverses_ref, values_ref,
    moved_ref, shrunk_ref,
):
    tiles, edge, _ = values_ref.shape
    gradient = jnp.sum(grads_ref[...], axis=0, keepdims=True)
    step = jnp.sum(inverses_ref[section] * gradient, axis=1, keepdims=True)
    square = (edge, edge)
    on_diagonal = lax.broadcasted_iota(jnp.int32, square, 0) == lax.broadcasted_iota(
        jnp.int32, square, 1
    )
    step = jnp.sum(jnp.where(on_diagonal, step, 0.0), axis=0, keepdims=True)
    old = old_ref[pl.ds(section, 1), :]
    raised = old + step
    size = jnp.maximum(jnp.abs(raised) - l1_penalty, 0.0)
    shrunk = jnp.where(raised < 0.0, -size, size)
    shrunk_ref[...] = shrunk
    change = jnp.broadcast_to(shrunk - old, (chunk, edge)).astype(jnp.bfloat16)
    image = tile_products(
        lambda first: change, lambda first: values_ref[pl.ds(first, chunk)], tiles
    )
    landed = placed_sum(chosen_ref[section], image)
    weight = state_ref[1]
    residual = state_ref[0] - weight * landed
    if len(moved_ref.shape) == 3:
        moved_ref[0] = residual
        moved_ref[1] = weight
    else:
        moved_ref[...] = residual


def blocks_kernel(sections, targets_smem, beta_ref, *refs):
    blocks_ref = refs[sections]
    blocks_ref[...] = beta_ref[...]
    for section in range(sections):
        blocks_ref[pl.ds(targets_smem[0, section], 1), :] = refs[section][...]


def from_behind(value, axis, steps):
    count = lax.axis_size(axis)
    pairs = [(source, (source + steps) % count) for source in range(count)]
    return lax.ppermute(value, axis, pairs)


def gathered(parts, axis):
    count, edge = parts.shape
    order = [index ^ 1 for index in range(count)] if count % 2 == 0 else list(range(count))
    received = lax.all_to_all(
        parts.reshape(count, 1, edge), axis, 0, 0, axis_index_groups=[order]
    )
    return received.reshape(count, edge)


def per_device(labels, beta, tile_rows, tile_cols, tile_values, block_order, hess_inv):
    sections = lax.axis_size("feat")
    samp_count = lax.axis_size("samp")
    tiles, edge = tile_values.shape[2], tile_values.shape[4]
    row_blocks = labels.shape[0] // edge
    group_blocks = row_blocks // sections
    blocks = beta.reshape(-1, edge)
    inverses = hess_inv[0]
    values = tile_values[0, 0]
    partial_sum, old_blocks = pl.pallas_call(
        margins_kernel,
        out_shape=(float_of((row_blocks, edge)), float_of((sections, edge))),
        in_specs=[HBM] * 5,
        out_specs=(VMEM, VMEM),
        scratch_shapes=[
            pltpu.VMEM((tiles, edge), jnp.float32),
            pltpu.VMEM(blocks.shape, jnp.float32),
            pltpu.VMEM((1, tiles), jnp.int32),
            pltpu.VMEM(values.shape, jnp.bfloat16),
            pltpu.SMEM((1, tiles), jnp.int32),
            pltpu.SMEM((1, sections), jnp.int32),
            pltpu.SemaphoreType.DMA((4,)),
            pltpu.SemaphoreType.DMA((tiles // chunk,)),
        ],
        compiler_params=pltpu.CompilerParams(vmem_limit_bytes=58 << 20),
    )(tile_cols[0], block_order, tile_rows[0], blocks, values)
    parts = lax.all_to_all(partial_sum.reshape(sections, group_blocks, edge), "feat", 0, 0)
    state, grads, chosen = call(
        first_kernel,
        (
            float_of((2, group_blocks, edge)),
            float_of((samp_count, edge)),
            float_of((sections, group_blocks, tiles)),
        ),
        [VMEM] * 6,
    )(parts, labels.reshape(row_blocks, edge), tile_rows[0], tile_cols[0], block_order, values)
    shrunk_blocks = []
    for section in range(sections):
        final = section + 1 == sections
        moved_shape = (group_blocks, edge) if final else (2, group_blocks, edge)
        moving, shrunk = call(
            functools.partial(update_kernel, section),
            (float_of(moved_shape), float_of((1, edge))),
            [VMEM] * 6,
        )(gathered(grads, "samp"), state, chosen, old_blocks, inverses, values)
        shrunk_blocks.append(shrunk)
        state = from_behind(moving.reshape(-1) if final else moving, "feat", 1)
        if not final:
            grads = call(
                functools.partial(gradient_kernel, section + 1),
                float_of((samp_count, edge)),
                [VMEM] * 3,
            )(state, chosen, values)
    blocks = call(
        functools.partial(blocks_kernel, sections),
        float_of(blocks.shape),
        [SMEM] + [VMEM] * (1 + sections),
    )(block_order, blocks, *shrunk_blocks)
    return (blocks.reshape(-1), state)


def solution(mesh):
    placed = (
        P("samp"),
        P("feat"),
        P("samp", "feat", None),
        P("samp", "feat", None),
        P("samp", "feat", None, None, None),
        P("feat", None),
        P("feat", None, None, None),
    )
    return jax.shard_map(
        per_device,
        mesh=mesh,
        in_specs=placed,
        out_specs=(P("feat"), P(("samp", "feat"))),
        check_vma=False,
    )
```

```python
import functools

import jax
import jax.numpy as jnp
from jax import lax
from jax.experimental import pallas as pl
from jax.experimental.pallas import tpu as pltpu
from jax.sharding import PartitionSpec as P

exact_prec = lax.Precision.HIGHEST
l1_penalty = 0.25
chunk = 16

VMEM = pl.BlockSpec(memory_space=pltpu.VMEM)
SMEM = pl.BlockSpec(memory_space=pltpu.SMEM)
HBM = pl.BlockSpec(memory_space=pltpu.HBM)


def float_of(shape):
    return jax.ShapeDtypeStruct(shape, jnp.float32)


def call(kernel, out_shape, in_specs):
    single = not isinstance(out_shape, tuple)
    return pl.pallas_call(
        kernel,
        out_shape=out_shape,
        in_specs=in_specs,
        out_specs=VMEM if single else tuple(VMEM for _ in out_shape),
        compiler_params=pltpu.CompilerParams(vmem_limit_bytes=24 << 20),
    )


def middle_first(count):
    return sorted(range(count), key=lambda index: (abs(index - count // 2), index))


def tile_products(vectors_of, tiles_of, tiles):
    pieces = []
    for first in range(0, tiles, chunk):
        vectors = vectors_of(first)
        edge = vectors.shape[1]
        products = lax.dot_general(
            vectors,
            tiles_of(first).reshape(chunk * edge, edge),
            (((1,), (1,)), ((), ())),
            preferred_element_type=jnp.float32,
        )
        sub = lax.broadcasted_iota(jnp.int32, (chunk, edge), 0)
        piece = products[:, :edge]
        for inner in range(1, chunk):
            piece = jnp.where(sub == inner, products[:, inner * edge : (inner + 1) * edge], piece)
        pieces.append(piece)
    return jnp.concatenate(pieces, axis=0)


def placed_sum(chosen, rows):
    high = rows.astype(jnp.bfloat16)
    rest = rows - high.astype(jnp.float32)
    middle = rest.astype(jnp.bfloat16)
    low = (rest - middle.astype(jnp.float32)).astype(jnp.bfloat16)
    ones = chosen.astype(jnp.bfloat16)
    return sum(
        jnp.dot(ones, part, preferred_element_type=jnp.float32) for part in (low, middle, high)
    )


def margins_kernel(
    cols_hbm, targets_hbm, rows_hbm, beta_hbm, values_hbm, partial_ref, old_ref,
    picked_ref, beta_ref, rows_ref, values_ref, cols_smem, targets_smem, small_sem, tile_sem,
):
    tiles = cols_smem.shape[1]
    sections = targets_smem.shape[1]
    row_blocks = partial_ref.shape[0]
    small = [
        pltpu.make_async_copy(cols_hbm, cols_smem, small_sem.at[0]),
        pltpu.make_async_copy(beta_hbm, beta_ref, small_sem.at[1]),
        pltpu.make_async_copy(targets_hbm, targets_smem, small_sem.at[2]),
        pltpu.make_async_copy(rows_hbm, rows_ref, small_sem.at[3]),
    ]
    large = [
        pltpu.make_async_copy(
            values_hbm.at[pl.ds(first, chunk)],
            values_ref.at[pl.ds(first, chunk)],
            tile_sem.at[first // chunk],
        )
        for first in range(0, tiles, chunk)
    ]
    for copy in small + large:
        copy.start()
    for copy in small:
        copy.wait()
    for tile in range(tiles):
        picked_ref[pl.ds(tile, 1), :] = beta_ref[pl.ds(cols_smem[0, tile], 1), :]
    for section in range(sections):
        old_ref[pl.ds(section, 1), :] = beta_ref[pl.ds(targets_smem[0, section], 1), :]

    def tiles_of(first):
        large[first // chunk].wait()
        return values_ref[pl.ds(first, chunk)]

    products = tile_products(
        lambda first: picked_ref[pl.ds(first, chunk), :].astype(jnp.bfloat16), tiles_of, tiles
    )
    block_ids = lax.broadcasted_iota(jnp.int32, (row_blocks, tiles), 0)
    placing = (block_ids == rows_ref[...]).astype(jnp.float32)
    partial = placed_sum(placing, products)
    group_blocks = row_blocks // sections
    for place, group in enumerate(middle_first(sections)):
        partial_ref[pl.ds(place * group_blocks, group_blocks), :] = partial[
            group * group_blocks : (group + 1) * group_blocks
        ]


def gradient_part(residual, chosen, values_ref):
    tiles, edge, _ = values_ref.shape
    picked = lax.dot_general(
        chosen.astype(jnp.bfloat16),
        residual.astype(jnp.bfloat16),
        (((0,), (0,)), ((), ())),
        preferred_element_type=jnp.float32,
    )
    sub = lax.broadcasted_iota(jnp.int32, (chunk, edge), 0)
    spread = []
    for tile in range(tiles):
        first = tile - tile % chunk
        kept = jnp.where(sub == tile - first, picked[first : first + chunk], 0.0)
        spread.append(kept.astype(jnp.bfloat16))
    summed = jnp.dot(
        jnp.concatenate(spread, axis=1),
        values_ref[...].reshape(tiles * edge, edge),
        preferred_element_type=jnp.float32,
    )
    return jnp.sum(summed, axis=0, keepdims=True)


def first_kernel(
    parts_ref, labels_ref, rows_ref, cols_ref, targets_ref, values_ref,
    residual_ref, weight_ref, grad_ref, chosen_ref,
):
    sections, group_blocks, _ = parts_ref.shape
    my_index = lax.axis_index("feat")
    sub_ids = lax.broadcasted_iota(jnp.int32, chosen_ref.shape[1:], 0)
    for section in range(sections):
        group = lax.rem(my_index - section + sections, sections)
        same_row = sub_ids + group * group_blocks == rows_ref[...]
        same_col = cols_ref[...] == targets_ref[:, section : section + 1]
        chosen_ref[section] = (same_row & same_col).astype(jnp.float32)
    start = pl.multiple_of(my_index * group_blocks, 8)
    margins = parts_ref[0]
    for part in range(1, parts_ref.shape[0]):
        margins = margins + parts_ref[part]
    probability = 1.0 / (1.0 + jnp.exp(-margins))
    residual = labels_ref[pl.ds(start, group_blocks), :].astype(jnp.float32) - probability
    residual_ref[...] = residual
    weight_ref[...] = probability * (1.0 - probability)
    grad = gradient_part(residual, chosen_ref[0], values_ref)
    grad_ref[...] = jnp.broadcast_to(grad, grad_ref.shape)


def gradient_kernel(section, residual_ref, chosen_ref, values_ref, grad_ref):
    grad = gradient_part(residual_ref[...], chosen_ref[section], values_ref)
    grad_ref[...] = jnp.broadcast_to(grad, grad_ref.shape)


def update_kernel(
    section, grads_ref, residual_ref, weight_ref, chosen_ref, old_ref, inverses_ref, values_ref,
    moved_ref, shrunk_ref,
):
    tiles, edge, _ = values_ref.shape
    gradient = jnp.sum(grads_ref[...], axis=0, keepdims=True)
    step = jnp.sum(inverses_ref[section] * gradient, axis=1, keepdims=True)
    square = (edge, edge)
    on_diagonal = lax.broadcasted_iota(jnp.int32, square, 0) == lax.broadcasted_iota(
        jnp.int32, square, 1
    )
    step = jnp.sum(jnp.where(on_diagonal, step, 0.0), axis=0, keepdims=True)
    old = old_ref[pl.ds(section, 1), :]
    raised = old + step
    size = jnp.maximum(jnp.abs(raised) - l1_penalty, 0.0)
    shrunk = jnp.where(raised < 0.0, -size, size)
    shrunk_ref[...] = shrunk
    change = jnp.broadcast_to(shrunk - old, (chunk, edge)).astype(jnp.bfloat16)
    image = tile_products(
        lambda first: change, lambda first: values_ref[pl.ds(first, chunk)], tiles
    )
    landed = placed_sum(chosen_ref[section], image)
    moved_ref[...] = residual_ref[...] - weight_ref[...] * landed


def blocks_kernel(sections, targets_smem, beta_ref, *refs):
    blocks_ref = refs[sections]
    blocks_ref[...] = beta_ref[...]
    for section in range(sections):
        blocks_ref[pl.ds(targets_smem[0, section], 1), :] = refs[section][...]


def from_behind(value, axis, steps):
    count = lax.axis_size(axis)
    pairs = [(source, (source + steps) % count) for source in range(count)]
    return lax.ppermute(value, axis, pairs)


def gathered(parts, axis):
    count, edge = parts.shape
    order = [index ^ 1 for index in range(count)] if count % 2 == 0 else list(range(count))
    received = lax.all_to_all(
        parts.reshape(count, 1, edge), axis, 0, 0, axis_index_groups=[order]
    )
    return received.reshape(count, edge)


def per_device(labels, beta, tile_rows, tile_cols, tile_values, block_order, hess_inv):
    sections = lax.axis_size("feat")
    samp_count = lax.axis_size("samp")
    tiles, edge = tile_values.shape[2], tile_values.shape[4]
    row_blocks = labels.shape[0] // edge
    group_blocks = row_blocks // sections
    blocks = beta.reshape(-1, edge)
    inverses = hess_inv[0]
    values = tile_values[0, 0]
    partial_sum, old_blocks = pl.pallas_call(
        margins_kernel,
        out_shape=(float_of((row_blocks, edge)), float_of((sections, edge))),
        in_specs=[HBM] * 5,
        out_specs=(VMEM, VMEM),
        scratch_shapes=[
            pltpu.VMEM((tiles, edge), jnp.float32),
            pltpu.VMEM(blocks.shape, jnp.float32),
            pltpu.VMEM((1, tiles), jnp.int32),
            pltpu.VMEM(values.shape, jnp.bfloat16),
            pltpu.SMEM((1, tiles), jnp.int32),
            pltpu.SMEM((1, sections), jnp.int32),
            pltpu.SemaphoreType.DMA((4,)),
            pltpu.SemaphoreType.DMA((tiles // chunk,)),
        ],
        compiler_params=pltpu.CompilerParams(vmem_limit_bytes=58 << 20),
    )(tile_cols[0], block_order, tile_rows[0], blocks, values)
    parts = lax.all_to_all(
        partial_sum.reshape(sections, group_blocks, edge),
        "feat",
        0,
        0,
        axis_index_groups=[middle_first(sections)],
    )
    group_shape = (group_blocks, edge)
    residual, weight, grads, chosen = call(
        first_kernel,
        (
            float_of(group_shape),
            float_of(group_shape),
            float_of((samp_count, edge)),
            float_of((sections, group_blocks, tiles)),
        ),
        [VMEM] * 6,
    )(parts, labels.reshape(row_blocks, edge), tile_rows[0], tile_cols[0], block_order, values)
    shrunk_blocks = []
    for section in range(sections):
        moving, shrunk = call(
            functools.partial(update_kernel, section),
            (float_of(group_shape), float_of((1, edge))),
            [VMEM] * 7,
        )(gathered(grads, "samp"), residual, weight, chosen, old_blocks, inverses, values)
        shrunk_blocks.append(shrunk)
        residual = from_behind(moving, "feat", 1)
        if section + 1 < sections:
            weight = from_behind(weight, "feat", 1)
            grads = call(
                functools.partial(gradient_kernel, section + 1),
                float_of((samp_count, edge)),
                [VMEM] * 3,
            )(residual, chosen, values)
    blocks = call(
        functools.partial(blocks_kernel, sections),
        float_of(blocks.shape),
        [SMEM] + [VMEM] * (1 + sections),
    )(block_order, blocks, *shrunk_blocks)
    return (blocks.reshape(-1), residual.reshape(-1))


def solution(mesh):
    placed = (
        P("samp"),
        P("feat"),
        P("samp", "feat", None),
        P("samp", "feat", None),
        P("samp", "feat", None, None, None),
        P("feat", None),
        P("feat", None, None, None),
    )
    return jax.shard_map(
        per_device,
        mesh=mesh,
        in_specs=placed,
        out_specs=(P("feat"), P(("samp", "feat"))),
        check_vma=False,
    )
```

```python
import functools

import jax
import jax.numpy as jnp
from jax import lax
from jax.experimental import pallas as pl
from jax.experimental.pallas import tpu as pltpu
from jax.sharding import PartitionSpec as P

exact_prec = lax.Precision.HIGHEST
l1_penalty = 0.25
chunk = 16

VMEM = pl.BlockSpec(memory_space=pltpu.VMEM)
SMEM = pl.BlockSpec(memory_space=pltpu.SMEM)
HBM = pl.BlockSpec(memory_space=pltpu.HBM)


def float_of(shape):
    return jax.ShapeDtypeStruct(shape, jnp.float32)


def call(kernel, out_shape, in_specs):
    single = not isinstance(out_shape, tuple)
    return pl.pallas_call(
        kernel,
        out_shape=out_shape,
        in_specs=in_specs,
        out_specs=VMEM if single else tuple(VMEM for _ in out_shape),
        compiler_params=pltpu.CompilerParams(vmem_limit_bytes=24 << 20),
    )


def middle_first(count):
    return sorted(range(count), key=lambda index: (abs(index - count // 2), index))


def tile_products(vectors_of, tiles_of, tiles):
    pieces = []
    for first in range(0, tiles, chunk):
        vectors = vectors_of(first)
        edge = vectors.shape[1]
        products = lax.dot_general(
            vectors,
            tiles_of(first).reshape(chunk * edge, edge),
            (((1,), (1,)), ((), ())),
            preferred_element_type=jnp.float32,
        )
        sub = lax.broadcasted_iota(jnp.int32, (chunk, edge), 0)
        piece = products[:, :edge]
        for inner in range(1, chunk):
            piece = jnp.where(sub == inner, products[:, inner * edge : (inner + 1) * edge], piece)
        pieces.append(piece)
    return jnp.concatenate(pieces, axis=0)


def placed_sum(chosen, rows):
    high = rows.astype(jnp.bfloat16)
    rest = rows - high.astype(jnp.float32)
    middle = rest.astype(jnp.bfloat16)
    low = (rest - middle.astype(jnp.float32)).astype(jnp.bfloat16)
    ones = chosen.astype(jnp.bfloat16)
    return sum(
        jnp.dot(ones, part, preferred_element_type=jnp.float32) for part in (low, middle, high)
    )


def margins_kernel(
    cols_hbm, targets_hbm, rows_hbm, beta_hbm, values_hbm, partial_ref, old_ref,
    picked_ref, beta_ref, rows_ref, values_ref, cols_smem, targets_smem, small_sem, tile_sem,
):
    tiles = cols_smem.shape[1]
    sections = targets_smem.shape[1]
    row_blocks = partial_ref.shape[0]
    small = [
        pltpu.make_async_copy(cols_hbm, cols_smem, small_sem.at[0]),
        pltpu.make_async_copy(beta_hbm, beta_ref, small_sem.at[1]),
        pltpu.make_async_copy(targets_hbm, targets_smem, small_sem.at[2]),
        pltpu.make_async_copy(rows_hbm, rows_ref, small_sem.at[3]),
    ]
    large = [
        pltpu.make_async_copy(
            values_hbm.at[pl.ds(first, chunk)],
            values_ref.at[pl.ds(first, chunk)],
            tile_sem.at[first // chunk],
        )
        for first in range(0, tiles, chunk)
    ]
    for copy in small + large:
        copy.start()
    for copy in small:
        copy.wait()
    for tile in range(tiles):
        picked_ref[pl.ds(tile, 1), :] = beta_ref[pl.ds(cols_smem[0, tile], 1), :]
    for section in range(sections):
        old_ref[pl.ds(section, 1), :] = beta_ref[pl.ds(targets_smem[0, section], 1), :]

    def tiles_of(first):
        large[first // chunk].wait()
        return values_ref[pl.ds(first, chunk)]

    products = tile_products(
        lambda first: picked_ref[pl.ds(first, chunk), :].astype(jnp.bfloat16), tiles_of, tiles
    )
    block_ids = lax.broadcasted_iota(jnp.int32, (row_blocks, tiles), 0)
    placing = (block_ids == rows_ref[...]).astype(jnp.float32)
    partial = placed_sum(placing, products)
    group_blocks = row_blocks // sections
    for place, group in enumerate(middle_first(sections)):
        partial_ref[pl.ds(place * group_blocks, group_blocks), :] = partial[
            group * group_blocks : (group + 1) * group_blocks
        ]


def gradient_part(residual, chosen, values_ref):
    tiles, edge, _ = values_ref.shape
    picked = lax.dot_general(
        chosen.astype(jnp.bfloat16),
        residual.astype(jnp.bfloat16),
        (((0,), (0,)), ((), ())),
        preferred_element_type=jnp.float32,
    )
    sub = lax.broadcasted_iota(jnp.int32, (chunk, edge), 0)
    spread = []
    for tile in range(tiles):
        first = tile - tile % chunk
        kept = jnp.where(sub == tile - first, picked[first : first + chunk], 0.0)
        spread.append(kept.astype(jnp.bfloat16))
    summed = jnp.dot(
        jnp.concatenate(spread, axis=1),
        values_ref[...].reshape(tiles * edge, edge),
        preferred_element_type=jnp.float32,
    )
    return jnp.sum(summed, axis=0, keepdims=True)


def first_kernel(
    parts_ref, labels_ref, rows_ref, cols_ref, targets_ref, values_ref,
    state_ref, grad_ref, chosen_ref,
):
    sections, group_blocks, _ = parts_ref.shape
    my_index = lax.axis_index("feat")
    sub_ids = lax.broadcasted_iota(jnp.int32, chosen_ref.shape[1:], 0)
    for section in range(sections):
        group = lax.rem(my_index - section + sections, sections)
        same_row = sub_ids + group * group_blocks == rows_ref[...]
        same_col = cols_ref[...] == targets_ref[:, section : section + 1]
        chosen_ref[section] = (same_row & same_col).astype(jnp.float32)
    start = pl.multiple_of(my_index * group_blocks, 8)
    margins = parts_ref[0]
    for part in range(1, parts_ref.shape[0]):
        margins = margins + parts_ref[part]
    probability = 1.0 / (1.0 + jnp.exp(-margins))
    residual = labels_ref[pl.ds(start, group_blocks), :].astype(jnp.float32) - probability
    state_ref[0] = residual
    state_ref[1] = probability * (1.0 - probability)
    grad = gradient_part(residual, chosen_ref[0], values_ref)
    grad_ref[...] = jnp.broadcast_to(grad, grad_ref.shape)


def gradient_kernel(section, state_ref, chosen_ref, values_ref, grad_ref):
    grad = gradient_part(state_ref[0], chosen_ref[section], values_ref)
    grad_ref[...] = jnp.broadcast_to(grad, grad_ref.shape)


def update_kernel(
    section, grads_ref, state_ref, chosen_ref, old_ref, inverses_ref, values_ref,
    moved_ref, shrunk_ref,
):
    tiles, edge, _ = values_ref.shape
    gradient = jnp.sum(grads_ref[...], axis=0, keepdims=True)
    step = jnp.sum(inverses_ref[section] * gradient, axis=1, keepdims=True)
    square = (edge, edge)
    on_diagonal = lax.broadcasted_iota(jnp.int32, square, 0) == lax.broadcasted_iota(
        jnp.int32, square, 1
    )
    step = jnp.sum(jnp.where(on_diagonal, step, 0.0), axis=0, keepdims=True)
    old = old_ref[pl.ds(section, 1), :]
    raised = old + step
    size = jnp.maximum(jnp.abs(raised) - l1_penalty, 0.0)
    shrunk = jnp.where(raised < 0.0, -size, size)
    shrunk_ref[...] = shrunk
    change = jnp.broadcast_to(shrunk - old, (chunk, edge)).astype(jnp.bfloat16)
    image = tile_products(
        lambda first: change, lambda first: values_ref[pl.ds(first, chunk)], tiles
    )
    landed = placed_sum(chosen_ref[section], image)
    weight = state_ref[1]
    residual = state_ref[0] - weight * landed
    if len(moved_ref.shape) == 3:
        moved_ref[0] = residual
        moved_ref[1] = weight
    else:
        moved_ref[...] = residual


def blocks_kernel(sections, targets_smem, beta_ref, *refs):
    blocks_ref = refs[sections]
    blocks_ref[...] = beta_ref[...]
    for section in range(sections):
        blocks_ref[pl.ds(targets_smem[0, section], 1), :] = refs[section][...]


def from_behind(value, axis, steps):
    count = lax.axis_size(axis)
    pairs = [(source, (source + steps) % count) for source in range(count)]
    return lax.ppermute(value, axis, pairs)


def gathered(parts, axis):
    count, edge = parts.shape
    order = list(range(count))
    if count % 2 == 0:
        half = count // 2
        far_apart = [pair // 2 if pair % 2 == 0 else half - 1 - pair // 2 for pair in range(half)]
        order = [2 * chip + 1 for chip in far_apart] + [2 * chip for chip in far_apart]
    received = lax.all_to_all(
        parts.reshape(count, 1, edge), axis, 0, 0, axis_index_groups=[order]
    )
    return received.reshape(count, edge)


def per_device(labels, beta, tile_rows, tile_cols, tile_values, block_order, hess_inv):
    sections = lax.axis_size("feat")
    samp_count = lax.axis_size("samp")
    tiles, edge = tile_values.shape[2], tile_values.shape[4]
    row_blocks = labels.shape[0] // edge
    group_blocks = row_blocks // sections
    blocks = beta.reshape(-1, edge)
    inverses = hess_inv[0]
    values = tile_values[0, 0]
    partial_sum, old_blocks = pl.pallas_call(
        margins_kernel,
        out_shape=(float_of((row_blocks, edge)), float_of((sections, edge))),
        in_specs=[HBM] * 5,
        out_specs=(VMEM, VMEM),
        scratch_shapes=[
            pltpu.VMEM((tiles, edge), jnp.float32),
            pltpu.VMEM(blocks.shape, jnp.float32),
            pltpu.VMEM((1, tiles), jnp.int32),
            pltpu.VMEM(values.shape, jnp.bfloat16),
            pltpu.SMEM((1, tiles), jnp.int32),
            pltpu.SMEM((1, sections), jnp.int32),
            pltpu.SemaphoreType.DMA((4,)),
            pltpu.SemaphoreType.DMA((tiles // chunk,)),
        ],
        compiler_params=pltpu.CompilerParams(vmem_limit_bytes=58 << 20),
    )(tile_cols[0], block_order, tile_rows[0], blocks, values)
    parts = lax.all_to_all(
        partial_sum.reshape(sections, group_blocks, edge),
        "feat",
        0,
        0,
        axis_index_groups=[middle_first(sections)],
    )
    state, grads, chosen = call(
        first_kernel,
        (
            float_of((2, group_blocks, edge)),
            float_of((samp_count, edge)),
            float_of((sections, group_blocks, tiles)),
        ),
        [VMEM] * 6,
    )(parts, labels.reshape(row_blocks, edge), tile_rows[0], tile_cols[0], block_order, values)
    shrunk_blocks = []
    for section in range(sections):
        final = section + 1 == sections
        moved_shape = (group_blocks, edge) if final else (2, group_blocks, edge)
        moving, shrunk = call(
            functools.partial(update_kernel, section),
            (float_of(moved_shape), float_of((1, edge))),
            [VMEM] * 6,
        )(gathered(grads, "samp"), state, chosen, old_blocks, inverses, values)
        shrunk_blocks.append(shrunk)
        state = from_behind(moving, "feat", 1)
        if not final:
            grads = call(
                functools.partial(gradient_kernel, section + 1),
                float_of((samp_count, edge)),
                [VMEM] * 3,
            )(state, chosen, values)
    blocks = call(
        functools.partial(blocks_kernel, sections),
        float_of(blocks.shape),
        [SMEM] + [VMEM] * (1 + sections),
    )(block_order, blocks, *shrunk_blocks)
    return (blocks.reshape(-1), state.reshape(-1))


def solution(mesh):
    placed = (
        P("samp"),
        P("feat"),
        P("samp", "feat", None),
        P("samp", "feat", None),
        P("samp", "feat", None, None, None),
        P("feat", None),
        P("feat", None, None, None),
    )
    return jax.shard_map(
        per_device,
        mesh=mesh,
        in_specs=placed,
        out_specs=(P("feat"), P(("samp", "feat"))),
        check_vma=False,
    )
```

```python
import functools

import jax
import jax.numpy as jnp
from jax import lax
from jax.experimental import pallas as pl
from jax.experimental.pallas import tpu as pltpu
from jax.sharding import PartitionSpec as P

exact_prec = lax.Precision.HIGHEST
l1_penalty = 0.25
chunk = 16

VMEM = pl.BlockSpec(memory_space=pltpu.VMEM)
SMEM = pl.BlockSpec(memory_space=pltpu.SMEM)
HBM = pl.BlockSpec(memory_space=pltpu.HBM)


def float_of(shape):
    return jax.ShapeDtypeStruct(shape, jnp.float32)


def call(kernel, out_shape, in_specs, scratch_shapes=()):
    single = not isinstance(out_shape, tuple)
    return pl.pallas_call(
        kernel,
        out_shape=out_shape,
        in_specs=in_specs,
        out_specs=VMEM if single else tuple(VMEM for _ in out_shape),
        scratch_shapes=scratch_shapes,
        compiler_params=pltpu.CompilerParams(vmem_limit_bytes=24 << 20),
    )


def middle_first(count):
    return sorted(range(count), key=lambda index: (abs(index - count // 2), index))


def tile_products(vectors_of, tiles_of, tiles):
    pieces = []
    for first in range(0, tiles, chunk):
        vectors = vectors_of(first)
        edge = vectors.shape[1]
        products = lax.dot_general(
            vectors,
            tiles_of(first).reshape(chunk * edge, edge),
            (((1,), (1,)), ((), ())),
            preferred_element_type=jnp.float32,
        )
        sub = lax.broadcasted_iota(jnp.int32, (chunk, edge), 0)
        piece = products[:, :edge]
        for inner in range(1, chunk):
            piece = jnp.where(sub == inner, products[:, inner * edge : (inner + 1) * edge], piece)
        pieces.append(piece)
    return jnp.concatenate(pieces, axis=0)


def placed_sum(chosen, rows):
    high = rows.astype(jnp.bfloat16)
    rest = rows - high.astype(jnp.float32)
    middle = rest.astype(jnp.bfloat16)
    low = (rest - middle.astype(jnp.float32)).astype(jnp.bfloat16)
    ones = chosen.astype(jnp.bfloat16)
    return sum(
        jnp.dot(ones, part, preferred_element_type=jnp.float32) for part in (low, middle, high)
    )


def margins_kernel(
    cols_hbm, targets_hbm, rows_hbm, beta_hbm, values_hbm, partial_ref, old_ref,
    picked_ref, beta_ref, rows_ref, values_ref, cols_smem, targets_smem, small_sem, tile_sem,
):
    tiles = cols_smem.shape[1]
    sections = targets_smem.shape[1]
    row_blocks = partial_ref.shape[0]
    small = [
        pltpu.make_async_copy(cols_hbm, cols_smem, small_sem.at[0]),
        pltpu.make_async_copy(beta_hbm, beta_ref, small_sem.at[1]),
        pltpu.make_async_copy(targets_hbm, targets_smem, small_sem.at[2]),
        pltpu.make_async_copy(rows_hbm, rows_ref, small_sem.at[3]),
    ]
    large = [
        pltpu.make_async_copy(
            values_hbm.at[pl.ds(first, chunk)],
            values_ref.at[pl.ds(first, chunk)],
            tile_sem.at[first // chunk],
        )
        for first in range(0, tiles, chunk)
    ]
    for copy in small + large:
        copy.start()
    for copy in small:
        copy.wait()
    for tile in range(tiles):
        picked_ref[pl.ds(tile, 1), :] = beta_ref[pl.ds(cols_smem[0, tile], 1), :]
    for section in range(sections):
        old_ref[pl.ds(section, 1), :] = beta_ref[pl.ds(targets_smem[0, section], 1), :]

    def tiles_of(first):
        large[first // chunk].wait()
        return values_ref[pl.ds(first, chunk)]

    products = tile_products(
        lambda first: picked_ref[pl.ds(first, chunk), :].astype(jnp.bfloat16), tiles_of, tiles
    )
    block_ids = lax.broadcasted_iota(jnp.int32, (row_blocks, tiles), 0)
    placing = (block_ids == rows_ref[...]).astype(jnp.float32)
    partial = placed_sum(placing, products)
    group_blocks = row_blocks // sections
    for place, group in enumerate(middle_first(sections)):
        partial_ref[pl.ds(place * group_blocks, group_blocks), :] = partial[
            group * group_blocks : (group + 1) * group_blocks
        ]


def gradient_part(residual, chosen, values_ref):
    tiles, edge, _ = values_ref.shape
    picked = lax.dot_general(
        chosen.astype(jnp.bfloat16),
        residual.astype(jnp.bfloat16),
        (((0,), (0,)), ((), ())),
        preferred_element_type=jnp.float32,
    )
    sub = lax.broadcasted_iota(jnp.int32, (chunk, edge), 0)
    spread = []
    for tile in range(tiles):
        first = tile - tile % chunk
        kept = jnp.where(sub == tile - first, picked[first : first + chunk], 0.0)
        spread.append(kept.astype(jnp.bfloat16))
    summed = jnp.dot(
        jnp.concatenate(spread, axis=1),
        values_ref[...].reshape(tiles * edge, edge),
        preferred_element_type=jnp.float32,
    )
    return jnp.sum(summed, axis=0, keepdims=True)


def first_kernel(
    parts_ref, labels_ref, rows_ref, cols_ref, targets_ref, values_ref,
    state_ref, grad_ref, chosen_ref,
):
    sections, group_blocks, _ = parts_ref.shape
    my_index = lax.axis_index("feat")
    sub_ids = lax.broadcasted_iota(jnp.int32, chosen_ref.shape[1:], 0)
    for section in range(sections):
        group = lax.rem(my_index - section + sections, sections)
        same_row = sub_ids + group * group_blocks == rows_ref[...]
        same_col = cols_ref[...] == targets_ref[:, section : section + 1]
        chosen_ref[section] = (same_row & same_col).astype(jnp.float32)
    start = pl.multiple_of(my_index * group_blocks, 8)
    margins = parts_ref[0]
    for part in range(1, parts_ref.shape[0]):
        margins = margins + parts_ref[part]
    probability = 1.0 / (1.0 + jnp.exp(-margins))
    residual = labels_ref[pl.ds(start, group_blocks), :].astype(jnp.float32) - probability
    state_ref[0] = residual
    state_ref[1] = probability * (1.0 - probability)
    grad = gradient_part(residual, chosen_ref[0], values_ref)
    grad_ref[...] = jnp.broadcast_to(grad, grad_ref.shape)


def gradient_kernel(
    section, ahead_ref, aside_any, chosen_ref, values_ref, state_ref, grad_ref, aside_sem
):
    state_ref[...] = ahead_ref[...]

    @pl.when(lax.axis_index("feat") == 1)
    def _():
        copy = pltpu.make_async_copy(aside_any, state_ref, aside_sem)
        copy.start()
        copy.wait()

    grad = gradient_part(state_ref[0], chosen_ref[section], values_ref)
    grad_ref[...] = jnp.broadcast_to(grad, grad_ref.shape)


def update(
    section, grads_ref, state_ref, chosen_ref, old_ref, inverses_ref, values_ref,
    moved_ref, shrunk_ref,
):
    tiles, edge, _ = values_ref.shape
    gradient = jnp.sum(grads_ref[...], axis=0, keepdims=True)
    step = jnp.sum(inverses_ref[section] * gradient, axis=1, keepdims=True)
    square = (edge, edge)
    on_diagonal = lax.broadcasted_iota(jnp.int32, square, 0) == lax.broadcasted_iota(
        jnp.int32, square, 1
    )
    step = jnp.sum(jnp.where(on_diagonal, step, 0.0), axis=0, keepdims=True)
    old = old_ref[pl.ds(section, 1), :]
    raised = old + step
    size = jnp.maximum(jnp.abs(raised) - l1_penalty, 0.0)
    shrunk = jnp.where(raised < 0.0, -size, size)
    shrunk_ref[...] = shrunk
    change = jnp.broadcast_to(shrunk - old, (chunk, edge)).astype(jnp.bfloat16)
    image = tile_products(
        lambda first: change, lambda first: values_ref[pl.ds(first, chunk)], tiles
    )
    landed = placed_sum(chosen_ref[section], image)
    weight = state_ref[1]
    residual = state_ref[0] - weight * landed
    if len(moved_ref.shape) == 3:
        moved_ref[0] = residual
        moved_ref[1] = weight
    else:
        moved_ref[...] = residual


def update_kernel(section, *refs):
    update(section, *refs)


def update_where_kernel(section, on_first, *refs):
    state_ref, moved_ref, shrunk_ref = refs[1], refs[-2], refs[-1]
    mine = (lax.axis_index("feat") == 0) == on_first

    @pl.when(mine)
    def _():
        update(section, *refs)

    @pl.when(jnp.logical_not(mine))
    def _():
        moved_ref[...] = state_ref[...] if len(moved_ref.shape) == 3 else state_ref[0]
        shrunk_ref[...] = jnp.zeros_like(shrunk_ref)


def blocks_kernel(sections, targets_smem, beta_ref, *refs):
    blocks_ref = refs[sections]
    blocks_ref[...] = beta_ref[...]
    for section in range(sections):
        blocks_ref[pl.ds(targets_smem[0, section], 1), :] = refs[section][...]


def from_behind(value, axis, steps):
    count = lax.axis_size(axis)
    pairs = [(source, (source + steps) % count) for source in range(count)]
    return lax.ppermute(value, axis, pairs)


def swapped_in_pairs(value, axis):
    pairs = [(index, index ^ 1) for index in range(lax.axis_size(axis))]
    return lax.ppermute(value, axis, pairs)


def gathered(parts, axis):
    count, edge = parts.shape
    order = list(range(count))
    if count % 2 == 0:
        half = count // 2
        far_apart = [pair // 2 if pair % 2 == 0 else half - 1 - pair // 2 for pair in range(half)]
        order = [2 * chip + 1 for chip in far_apart] + [2 * chip for chip in far_apart]
    received = lax.all_to_all(
        parts.reshape(count, 1, edge), axis, 0, 0, axis_index_groups=[order]
    )
    return received.reshape(count, edge)


def per_device(labels, beta, tile_rows, tile_cols, tile_values, block_order, hess_inv):
    sections = lax.axis_size("feat")
    samp_count = lax.axis_size("samp")
    tiles, edge = tile_values.shape[2], tile_values.shape[4]
    row_blocks = labels.shape[0] // edge
    group_blocks = row_blocks // sections
    blocks = beta.reshape(-1, edge)
    inverses = hess_inv[0]
    values = tile_values[0, 0]
    partial_sum, old_blocks = pl.pallas_call(
        margins_kernel,
        out_shape=(float_of((row_blocks, edge)), float_of((sections, edge))),
        in_specs=[HBM] * 5,
        out_specs=(VMEM, VMEM),
        scratch_shapes=[
            pltpu.VMEM((tiles, edge), jnp.float32),
            pltpu.VMEM(blocks.shape, jnp.float32),
            pltpu.VMEM((1, tiles), jnp.int32),
            pltpu.VMEM(values.shape, jnp.bfloat16),
            pltpu.SMEM((1, tiles), jnp.int32),
            pltpu.SMEM((1, sections), jnp.int32),
            pltpu.SemaphoreType.DMA((4,)),
            pltpu.SemaphoreType.DMA((tiles // chunk,)),
        ],
        compiler_params=pltpu.CompilerParams(vmem_limit_bytes=58 << 20),
    )(tile_cols[0], block_order, tile_rows[0], blocks, values)
    parts = lax.all_to_all(
        partial_sum.reshape(sections, group_blocks, edge),
        "feat",
        0,
        0,
        axis_index_groups=[middle_first(sections)],
    )
    state, grads, chosen = call(
        first_kernel,
        (
            float_of((2, group_blocks, edge)),
            float_of((samp_count, edge)),
            float_of((sections, group_blocks, tiles)),
        ),
        [VMEM] * 6,
    )(parts, labels.reshape(row_blocks, edge), tile_rows[0], tile_cols[0], block_order, values)
    my_index = lax.axis_index("feat")
    first_apart = sections % 2 == 0
    shrunk_blocks = []
    for section in range(sections):
        final = section + 1 == sections
        moved_shape = (group_blocks, edge) if final else (2, group_blocks, edge)
        out_shape = (float_of(moved_shape), float_of((1, edge)))
        operands = (gathered(grads, "samp"), state, chosen, old_blocks, inverses, values)
        if first_apart:
            moving, shrunk = call(
                functools.partial(update_where_kernel, section, False), out_shape, [VMEM] * 6
            )(*operands)
            ahead = from_behind(moving, "feat", 1)

            def in_first_pair(*operands, section=section, out_shape=out_shape):
                moving, shrunk = call(
                    functools.partial(update_where_kernel, section, True), out_shape, [VMEM] * 6
                )(*operands)
                return swapped_in_pairs(moving, "feat"), shrunk

            def elsewhere(*operands, out_shape=out_shape):
                return tuple(jnp.zeros(part.shape, part.dtype) for part in out_shape)

            aside, shrunk_on_first = lax.cond(
                my_index <= 1, in_first_pair, elsewhere, *operands
            )
            shrunk = jnp.where(my_index == 0, shrunk_on_first, shrunk)
        else:
            moving, shrunk = call(
                functools.partial(update_kernel, section), out_shape, [VMEM] * 6
            )(*operands)
            ahead = from_behind(moving, "feat", 1)
            aside = ahead
        shrunk_blocks.append(shrunk)
        if final:
            residual = jnp.where(my_index == 1, aside, ahead)
        else:
            state, grads = call(
                functools.partial(gradient_kernel, section + 1),
                (float_of(moved_shape), float_of((samp_count, edge))),
                [VMEM, pl.BlockSpec(memory_space=pl.ANY), VMEM, VMEM],
                [pltpu.SemaphoreType.DMA],
            )(ahead, aside, chosen, values)
    blocks = call(
        functools.partial(blocks_kernel, sections),
        float_of(blocks.shape),
        [SMEM] + [VMEM] * (1 + sections),
    )(block_order, blocks, *shrunk_blocks)
    return (blocks.reshape(-1), residual.reshape(-1))


def solution(mesh):
    placed = (
        P("samp"),
        P("feat"),
        P("samp", "feat", None),
        P("samp", "feat", None),
        P("samp", "feat", None, None, None),
        P("feat", None),
        P("feat", None, None, None),
    )
    return jax.shard_map(
        per_device,
        mesh=mesh,
        in_specs=placed,
        out_specs=(P("feat"), P(("samp", "feat"))),
        check_vma=False,
    )
```

```python
import functools

import jax
import jax.numpy as jnp
from jax import lax
from jax.experimental import pallas as pl
from jax.experimental.pallas import tpu as pltpu
from jax.sharding import PartitionSpec as P

exact_prec = lax.Precision.HIGHEST
l1_penalty = 0.25
chunk = 16

VMEM = pl.BlockSpec(memory_space=pltpu.VMEM)
SMEM = pl.BlockSpec(memory_space=pltpu.SMEM)
HBM = pl.BlockSpec(memory_space=pltpu.HBM)


def float_of(shape):
    return jax.ShapeDtypeStruct(shape, jnp.float32)


def call(kernel, out_shape, in_specs, scratch_shapes):
    single = not isinstance(out_shape, tuple)
    return pl.pallas_call(
        kernel,
        out_shape=out_shape,
        in_specs=in_specs,
        out_specs=VMEM if single else tuple(VMEM for _ in out_shape),
        scratch_shapes=scratch_shapes,
        compiler_params=pltpu.CompilerParams(vmem_limit_bytes=24 << 20),
    )


def middle_first(count):
    return sorted(range(count), key=lambda index: (abs(index - count // 2), index))


def tile_products(vectors_of, tiles_of, tiles):
    pieces = []
    for first in range(0, tiles, chunk):
        vectors = vectors_of(first)
        edge = vectors.shape[1]
        products = lax.dot_general(
            vectors,
            tiles_of(first).reshape(chunk * edge, edge),
            (((1,), (1,)), ((), ())),
            preferred_element_type=jnp.float32,
        )
        sub = lax.broadcasted_iota(jnp.int32, (chunk, edge), 0)
        piece = products[:, :edge]
        for inner in range(1, chunk):
            piece = jnp.where(sub == inner, products[:, inner * edge : (inner + 1) * edge], piece)
        pieces.append(piece)
    return jnp.concatenate(pieces, axis=0)


def placed_sum(chosen, rows):
    high = rows.astype(jnp.bfloat16)
    rest = rows - high.astype(jnp.float32)
    middle = rest.astype(jnp.bfloat16)
    low = (rest - middle.astype(jnp.float32)).astype(jnp.bfloat16)
    ones = chosen.astype(jnp.bfloat16)
    return sum(
        jnp.dot(ones, part, preferred_element_type=jnp.float32) for part in (low, middle, high)
    )


def over_lanes(left, right):
    return lax.dot_general(
        left.astype(jnp.bfloat16),
        right.astype(jnp.bfloat16),
        (((1,), (1,)), ((), ())),
        preferred_element_type=jnp.float32,
    )


def listed(chosen):
    tiles = chosen.shape[1]
    square = (tiles, tiles)
    sub = lax.broadcasted_iota(jnp.int32, square, 0)
    lane = lax.broadcasted_iota(jnp.int32, square, 1)
    taken = jnp.sum(chosen, axis=0, keepdims=True)
    before = over_lanes(jnp.broadcast_to(taken, (8, tiles)), (lane < sub).astype(jnp.float32))
    in_slot = (sub == before[0:1].astype(jnp.int32)) & (taken > 0.0)
    in_slot = in_slot.astype(jnp.float32)
    numbers = lax.broadcasted_iota(jnp.int32, (8, tiles), 1) + 1
    ids = over_lanes(numbers.astype(jnp.float32), in_slot)[0:1].astype(jnp.int32) - 1
    return ids, over_lanes(in_slot, chosen), over_lanes(chosen, in_slot)


def margins_kernel(
    cols_hbm, targets_hbm, rows_hbm, beta_hbm, values_hbm,
    partial_ref, old_ref,
    picked_ref, beta_ref, rows_ref, values_ref, cols_smem, targets_smem, small_sem, tile_sem,
):
    tiles = cols_smem.shape[1]
    sections = targets_smem.shape[1]
    row_blocks = partial_ref.shape[0]
    small = [
        pltpu.make_async_copy(cols_hbm, cols_smem, small_sem.at[0]),
        pltpu.make_async_copy(beta_hbm, beta_ref, small_sem.at[1]),
        pltpu.make_async_copy(targets_hbm, targets_smem, small_sem.at[2]),
        pltpu.make_async_copy(rows_hbm, rows_ref, small_sem.at[3]),
    ]
    large = [
        pltpu.make_async_copy(
            values_hbm.at[pl.ds(first, chunk)],
            values_ref.at[pl.ds(first, chunk)],
            tile_sem.at[first // chunk],
        )
        for first in range(0, tiles, chunk)
    ]
    for copy in small + large:
        copy.start()
    for copy in small:
        copy.wait()
    for tile in range(tiles):
        picked_ref[pl.ds(tile, 1), :] = beta_ref[pl.ds(cols_smem[0, tile], 1), :]
    for section in range(sections):
        old_ref[pl.ds(section, 1), :] = beta_ref[pl.ds(targets_smem[0, section], 1), :]

    def tiles_of(first):
        large[first // chunk].wait()
        return values_ref[pl.ds(first, chunk)]

    products = tile_products(
        lambda first: picked_ref[pl.ds(first, chunk), :].astype(jnp.bfloat16), tiles_of, tiles
    )
    block_ids = lax.broadcasted_iota(jnp.int32, (row_blocks, tiles), 0)
    placing = (block_ids == rows_ref[...]).astype(jnp.float32)
    partial = placed_sum(placing, products)
    group_blocks = row_blocks // sections
    for place, group in enumerate(middle_first(sections)):
        partial_ref[pl.ds(place * group_blocks, group_blocks), :] = partial[
            group * group_blocks : (group + 1) * group_blocks
        ]


def listed_tiles(section, part, ids_ref, values_ref):
    return jnp.concatenate(
        [
            values_ref[jnp.maximum(ids_ref[section, part * chunk + inner], 0)]
            for inner in range(chunk)
        ],
        axis=0,
    )


def for_parts(section, ids_ref, run):
    run(0)
    for part in range(1, ids_ref.shape[1] // chunk):
        pl.when(ids_ref[section, part * chunk] >= 0)(functools.partial(run, part))


def gradient_part(section, residual, ids_ref, picking_ref, values_ref, total_ref):
    edge = values_ref.shape[2]
    picked = jnp.dot(
        picking_ref[section].astype(jnp.bfloat16),
        residual.astype(jnp.bfloat16),
        preferred_element_type=jnp.float32,
    )
    sub = lax.broadcasted_iota(jnp.int32, (chunk, edge), 0)

    def run(part):
        rows = picked[part * chunk : (part + 1) * chunk]
        spread = [
            jnp.where(sub == inner, rows, 0.0).astype(jnp.bfloat16) for inner in range(chunk)
        ]
        total = jnp.dot(
            jnp.concatenate(spread, axis=1),
            listed_tiles(section, part, ids_ref, values_ref),
            preferred_element_type=jnp.float32,
        )
        total_ref[...] = total if part == 0 else total_ref[...] + total

    for_parts(section, ids_ref, run)
    return jnp.sum(total_ref[...], axis=0, keepdims=True)


def first_kernel(
    parts_ref, labels_ref, rows_ref, cols_ref, targets_ref, values_ref,
    state_ref, grad_ref, ids_ref, picking_ref, placing_ref, total_ref,
):
    sections, group_blocks, _ = parts_ref.shape
    my_index = lax.axis_index("feat")
    sub_ids = lax.broadcasted_iota(jnp.int32, placing_ref.shape[1:], 0)
    for section in range(sections):
        group = lax.rem(my_index - section + sections, sections)
        same_row = sub_ids + group * group_blocks == rows_ref[...]
        same_col = cols_ref[...] == targets_ref[:, section : section + 1]
        ids, picking, placing = listed((same_row & same_col).astype(jnp.float32))
        ids_ref[pl.ds(section, 1), :] = ids
        picking_ref[section] = picking
        placing_ref[section] = placing
    start = pl.multiple_of(my_index * group_blocks, 8)
    margins = parts_ref[0]
    for part in range(1, parts_ref.shape[0]):
        margins = margins + parts_ref[part]
    probability = 1.0 / (1.0 + jnp.exp(-margins))
    residual = labels_ref[pl.ds(start, group_blocks), :].astype(jnp.float32) - probability
    state_ref[0] = residual
    state_ref[1] = probability * (1.0 - probability)
    grad = gradient_part(0, residual, ids_ref, picking_ref, values_ref, total_ref)
    grad_ref[...] = jnp.broadcast_to(grad, grad_ref.shape)


def gradient_kernel(section, state_ref, ids_ref, picking_ref, values_ref, grad_ref, total_ref):
    grad = gradient_part(section, state_ref[0], ids_ref, picking_ref, values_ref, total_ref)
    grad_ref[...] = jnp.broadcast_to(grad, grad_ref.shape)


def update_kernel(
    section, grads_ref, state_ref, ids_ref, placing_ref, old_ref, inverses_ref, values_ref,
    moved_ref, shrunk_ref, image_ref,
):
    tiles, edge, _ = values_ref.shape
    gradient = jnp.sum(grads_ref[...], axis=0, keepdims=True)
    step = jnp.sum(inverses_ref[section] * gradient, axis=1, keepdims=True)
    square = (edge, edge)
    on_diagonal = lax.broadcasted_iota(jnp.int32, square, 0) == lax.broadcasted_iota(
        jnp.int32, square, 1
    )
    step = jnp.sum(jnp.where(on_diagonal, step, 0.0), axis=0, keepdims=True)
    old = old_ref[pl.ds(section, 1), :]
    raised = old + step
    size = jnp.maximum(jnp.abs(raised) - l1_penalty, 0.0)
    shrunk = jnp.where(raised < 0.0, -size, size)
    shrunk_ref[...] = shrunk
    change = jnp.broadcast_to(shrunk - old, (chunk, edge)).astype(jnp.bfloat16)
    image_ref[...] = jnp.zeros_like(image_ref)

    def run(part):
        image_ref[pl.ds(part * chunk, chunk), :] = tile_products(
            lambda first: change, lambda first: listed_tiles(section, part, ids_ref, values_ref), chunk
        )

    for_parts(section, ids_ref, run)
    landed = placed_sum(placing_ref[section], image_ref[...])
    weight = state_ref[1]
    residual = state_ref[0] - weight * landed
    if len(moved_ref.shape) == 3:
        moved_ref[0] = residual
        moved_ref[1] = weight
    else:
        moved_ref[...] = residual


def blocks_kernel(sections, targets_smem, beta_ref, *refs):
    blocks_ref = refs[sections]
    blocks_ref[...] = beta_ref[...]
    for section in range(sections):
        blocks_ref[pl.ds(targets_smem[0, section], 1), :] = refs[section][...]


def from_behind(value, axis, steps):
    count = lax.axis_size(axis)
    pairs = [(source, (source + steps) % count) for source in range(count)]
    return lax.ppermute(value, axis, pairs)


def gathered(parts, axis):
    count, edge = parts.shape
    order = list(range(count))
    if count % 2 == 0:
        half = count // 2
        far_apart = [pair // 2 if pair % 2 == 0 else half - 1 - pair // 2 for pair in range(half)]
        order = [2 * chip + 1 for chip in far_apart] + [2 * chip for chip in far_apart]
    received = lax.all_to_all(
        parts.reshape(count, 1, edge), axis, 0, 0, axis_index_groups=[order]
    )
    return received.reshape(count, edge)


def per_device(labels, beta, tile_rows, tile_cols, tile_values, block_order, hess_inv):
    sections = lax.axis_size("feat")
    samp_count = lax.axis_size("samp")
    tiles, edge = tile_values.shape[2], tile_values.shape[4]
    row_blocks = labels.shape[0] // edge
    group_blocks = row_blocks // sections
    blocks = beta.reshape(-1, edge)
    inverses = hess_inv[0]
    values = tile_values[0, 0]
    partial_sum, old_blocks = pl.pallas_call(
        margins_kernel,
        out_shape=(float_of((row_blocks, edge)), float_of((sections, edge))),
        in_specs=[HBM] * 5,
        out_specs=(VMEM, VMEM),
        scratch_shapes=[
            pltpu.VMEM((tiles, edge), jnp.float32),
            pltpu.VMEM(blocks.shape, jnp.float32),
            pltpu.VMEM((1, tiles), jnp.int32),
            pltpu.VMEM(values.shape, jnp.bfloat16),
            pltpu.SMEM((1, tiles), jnp.int32),
            pltpu.SMEM((1, sections), jnp.int32),
            pltpu.SemaphoreType.DMA((4,)),
            pltpu.SemaphoreType.DMA((tiles // chunk,)),
        ],
        compiler_params=pltpu.CompilerParams(vmem_limit_bytes=58 << 20),
    )(tile_cols[0], block_order, tile_rows[0], blocks, values)
    parts = lax.all_to_all(
        partial_sum.reshape(sections, group_blocks, edge),
        "feat",
        0,
        0,
        axis_index_groups=[middle_first(sections)],
    )
    group_shape = (group_blocks, edge)
    total = pltpu.VMEM((chunk, edge), jnp.float32)
    state, grads, ids, picking, placing = call(
        first_kernel,
        (
            float_of((2, *group_shape)),
            float_of((samp_count, edge)),
            jax.ShapeDtypeStruct((sections, tiles), jnp.int32),
            float_of((sections, tiles, group_blocks)),
            float_of((sections, group_blocks, tiles)),
        ),
        [VMEM] * 6,
        [total],
    )(parts, labels.reshape(row_blocks, edge), tile_rows[0], tile_cols[0], block_order, values)
    shrunk_blocks = []
    for section in range(sections):
        final = section + 1 == sections
        moving, shrunk = call(
            functools.partial(update_kernel, section),
            (float_of(group_shape if final else (2, *group_shape)), float_of((1, edge))),
            [VMEM] * 7,
            [pltpu.VMEM((tiles, edge), jnp.float32)],
        )(gathered(grads, "samp"), state, ids, placing, old_blocks, inverses, values)
        shrunk_blocks.append(shrunk)
        state = from_behind(moving, "feat", 1)
        if not final:
            grads = call(
                functools.partial(gradient_kernel, section + 1),
                float_of((samp_count, edge)),
                [VMEM] * 4,
                [total],
            )(state, ids, picking, values)
    blocks = call(
        functools.partial(blocks_kernel, sections),
        float_of(blocks.shape),
        [SMEM] + [VMEM] * (1 + sections),
        [],
    )(block_order, blocks, *shrunk_blocks)
    return (blocks.reshape(-1), state.reshape(-1))


def solution(mesh):
    placed = (
        P("samp"),
        P("feat"),
        P("samp", "feat", None),
        P("samp", "feat", None),
        P("samp", "feat", None, None, None),
        P("feat", None),
        P("feat", None, None, None),
    )
    return jax.shard_map(
        per_device,
        mesh=mesh,
        in_specs=placed,
        out_specs=(P("feat"), P(("samp", "feat"))),
        check_vma=False,
    )
```

```python
import functools

import jax
import jax.numpy as jnp
from jax import lax
from jax.experimental import pallas as pl
from jax.experimental.pallas import tpu as pltpu
from jax.sharding import PartitionSpec as P

exact_prec = lax.Precision.HIGHEST
l1_penalty = 0.25
chunk = 16

VMEM = pl.BlockSpec(memory_space=pltpu.VMEM)
SMEM = pl.BlockSpec(memory_space=pltpu.SMEM)
HBM = pl.BlockSpec(memory_space=pltpu.HBM)


def float_of(shape):
    return jax.ShapeDtypeStruct(shape, jnp.float32)


def call(kernel, out_shape, in_specs, scratch_shapes):
    single = not isinstance(out_shape, tuple)
    return pl.pallas_call(
        kernel,
        out_shape=out_shape,
        in_specs=in_specs,
        out_specs=VMEM if single else tuple(VMEM for _ in out_shape),
        scratch_shapes=scratch_shapes,
        compiler_params=pltpu.CompilerParams(vmem_limit_bytes=24 << 20),
    )


def middle_first(count):
    return sorted(range(count), key=lambda index: (abs(index - count // 2), index))


def tile_products(vectors_of, tiles_of, tiles):
    pieces = []
    for first in range(0, tiles, chunk):
        vectors = vectors_of(first)
        edge = vectors.shape[1]
        products = lax.dot_general(
            vectors,
            tiles_of(first).reshape(chunk * edge, edge),
            (((1,), (1,)), ((), ())),
            preferred_element_type=jnp.float32,
        )
        sub = lax.broadcasted_iota(jnp.int32, (chunk, edge), 0)
        piece = products[:, :edge]
        for inner in range(1, chunk):
            piece = jnp.where(sub == inner, products[:, inner * edge : (inner + 1) * edge], piece)
        pieces.append(piece)
    return jnp.concatenate(pieces, axis=0)


def placed_sum(chosen, rows):
    high = rows.astype(jnp.bfloat16)
    rest = rows - high.astype(jnp.float32)
    middle = rest.astype(jnp.bfloat16)
    low = (rest - middle.astype(jnp.float32)).astype(jnp.bfloat16)
    ones = chosen.astype(jnp.bfloat16)
    return sum(
        jnp.dot(ones, part, preferred_element_type=jnp.float32) for part in (low, middle, high)
    )


def over_lanes(left, right):
    return lax.dot_general(
        left.astype(jnp.bfloat16),
        right.astype(jnp.bfloat16),
        (((1,), (1,)), ((), ())),
        preferred_element_type=jnp.float32,
    )


def listed(row_in_group, taken, group_blocks):
    tiles = taken.shape[1]
    square = (tiles, tiles)
    sub = lax.broadcasted_iota(jnp.int32, square, 0)
    lane = lax.broadcasted_iota(jnp.int32, square, 1)
    taken = jnp.broadcast_to(taken, (8, tiles)).astype(jnp.float32)
    before = over_lanes(taken, (lane < sub).astype(jnp.float32))
    in_slot = (sub == before[0:1].astype(jnp.int32)) & (taken[0:1] > 0.0)
    numbers = lax.broadcasted_iota(jnp.int32, (8, tiles), 1) + 1
    short = group_blocks - row_in_group
    facts = jnp.where(lax.broadcasted_iota(jnp.int32, (8, tiles), 0) == 0, numbers, short)
    found = over_lanes(facts.astype(jnp.float32), in_slot.astype(jnp.float32)).astype(jnp.int32)
    return found[0:1] - 1, group_blocks - found[1:2]


def margins_kernel(
    cols_hbm, targets_hbm, rows_hbm, beta_hbm, values_hbm,
    partial_ref, old_ref, lists_ref,
    picked_ref, beta_ref, rows_ref, cols_ref, values_ref,
    cols_smem, targets_smem, small_sem, tile_sem,
):
    tiles = cols_smem.shape[1]
    sections = targets_smem.shape[1]
    row_blocks = partial_ref.shape[0]
    small = [
        pltpu.make_async_copy(cols_hbm, cols_smem, small_sem.at[0]),
        pltpu.make_async_copy(beta_hbm, beta_ref, small_sem.at[1]),
        pltpu.make_async_copy(targets_hbm, targets_smem, small_sem.at[2]),
        pltpu.make_async_copy(rows_hbm, rows_ref, small_sem.at[3]),
        pltpu.make_async_copy(cols_hbm, cols_ref, small_sem.at[4]),
    ]
    large = [
        pltpu.make_async_copy(
            values_hbm.at[pl.ds(first, chunk)],
            values_ref.at[pl.ds(first, chunk)],
            tile_sem.at[first // chunk],
        )
        for first in range(0, tiles, chunk)
    ]
    for copy in small + large:
        copy.start()
    for copy in small:
        copy.wait()
    for tile in range(tiles):
        picked_ref[pl.ds(tile, 1), :] = beta_ref[pl.ds(cols_smem[0, tile], 1), :]
    for section in range(sections):
        old_ref[pl.ds(section, 1), :] = beta_ref[pl.ds(targets_smem[0, section], 1), :]

    my_index = lax.axis_index("feat")
    group_blocks = row_blocks // sections
    for section in range(sections):
        group = lax.rem(my_index - section + sections, sections)
        row_in_group = rows_ref[...] - group * group_blocks
        taken = (
            (row_in_group >= 0)
            & (row_in_group < group_blocks)
            & (cols_ref[...] == targets_smem[0, section])
        )
        ids, places = listed(row_in_group, taken, group_blocks)
        lists_ref[pl.ds(2 * section, 1), :] = ids
        lists_ref[pl.ds(2 * section + 1, 1), :] = places

    def tiles_of(first):
        large[first // chunk].wait()
        return values_ref[pl.ds(first, chunk)]

    products = tile_products(
        lambda first: picked_ref[pl.ds(first, chunk), :].astype(jnp.bfloat16), tiles_of, tiles
    )
    block_ids = lax.broadcasted_iota(jnp.int32, (row_blocks, tiles), 0)
    placing = (block_ids == rows_ref[...]).astype(jnp.float32)
    partial = placed_sum(placing, products)
    for place, group in enumerate(middle_first(sections)):
        partial_ref[pl.ds(place * group_blocks, group_blocks), :] = partial[
            group * group_blocks : (group + 1) * group_blocks
        ]


def listed_tiles(section, part, lists_ref, values_ref):
    return jnp.concatenate(
        [
            values_ref[jnp.maximum(lists_ref[2 * section, part * chunk + inner], 0)]
            for inner in range(chunk)
        ],
        axis=0,
    )


def for_parts(section, lists_ref, run):
    run(0)
    for part in range(1, lists_ref.shape[1] // chunk):
        pl.when(lists_ref[2 * section, part * chunk] >= 0)(functools.partial(run, part))


def gradient_of_all(residual, chosen, values_ref):
    tiles, edge, _ = values_ref.shape
    picked = lax.dot_general(
        chosen.astype(jnp.bfloat16),
        residual.astype(jnp.bfloat16),
        (((0,), (0,)), ((), ())),
        preferred_element_type=jnp.float32,
    )
    sub = lax.broadcasted_iota(jnp.int32, (chunk, edge), 0)
    spread = []
    for tile in range(tiles):
        first = tile - tile % chunk
        kept = jnp.where(sub == tile - first, picked[first : first + chunk], 0.0)
        spread.append(kept.astype(jnp.bfloat16))
    summed = jnp.dot(
        jnp.concatenate(spread, axis=1),
        values_ref[...].reshape(tiles * edge, edge),
        preferred_element_type=jnp.float32,
    )
    return jnp.sum(summed, axis=0, keepdims=True)


def first_kernel(
    parts_ref, labels_ref, rows_ref, cols_ref, targets_ref, values_ref, state_ref, grad_ref
):
    group_blocks = parts_ref.shape[1]
    first_row = lax.axis_index("feat") * group_blocks
    sub_ids = lax.broadcasted_iota(jnp.int32, (group_blocks, rows_ref.shape[1]), 0)
    same_row = sub_ids + first_row == rows_ref[...]
    chosen = (same_row & (cols_ref[...] == targets_ref[:, 0:1])).astype(jnp.float32)
    margins = parts_ref[0]
    for part in range(1, parts_ref.shape[0]):
        margins = margins + parts_ref[part]
    probability = 1.0 / (1.0 + jnp.exp(-margins))
    labels = labels_ref[pl.ds(pl.multiple_of(first_row, 8), group_blocks), :]
    residual = labels.astype(jnp.float32) - probability
    state_ref[0] = residual
    state_ref[1] = probability * (1.0 - probability)
    grad = gradient_of_all(residual, chosen, values_ref)
    grad_ref[...] = jnp.broadcast_to(grad, grad_ref.shape)


def gradient_kernel(section, state_ref, lists_ref, values_ref, grad_ref, rows_ref, total_ref):
    _, group_blocks, edge = state_ref.shape
    rows_ref[pl.ds(0, group_blocks), :] = state_ref[0]
    rows_ref[pl.ds(group_blocks, 8), :] = jnp.zeros((8, edge), jnp.float32)

    def run(part):
        spread = []
        for inner in range(chunk):
            place = lists_ref[2 * section + 1, part * chunk + inner]
            row = jnp.broadcast_to(rows_ref[pl.ds(place, 1), :], (chunk, edge))
            spread.append(row.astype(jnp.bfloat16))
        total = jnp.dot(
            jnp.concatenate(spread, axis=1),
            listed_tiles(section, part, lists_ref, values_ref),
            preferred_element_type=jnp.float32,
        )
        total_ref[...] = total if part == 0 else total_ref[...] + total

    for_parts(section, lists_ref, run)
    grad_ref[...] = jnp.broadcast_to(total_ref[0:1, :], grad_ref.shape)


def update_kernel(
    section, grads_ref, state_ref, lists_ref, old_ref, inverses_ref, values_ref,
    moved_ref, shrunk_ref, landed_ref,
):
    _, group_blocks, edge = state_ref.shape
    gradient = jnp.sum(grads_ref[...], axis=0, keepdims=True)
    step = jnp.sum(inverses_ref[section] * gradient, axis=1, keepdims=True)
    square = (edge, edge)
    on_diagonal = lax.broadcasted_iota(jnp.int32, square, 0) == lax.broadcasted_iota(
        jnp.int32, square, 1
    )
    step = jnp.sum(jnp.where(on_diagonal, step, 0.0), axis=0, keepdims=True)
    old = old_ref[pl.ds(section, 1), :]
    raised = old + step
    size = jnp.maximum(jnp.abs(raised) - l1_penalty, 0.0)
    shrunk = jnp.where(raised < 0.0, -size, size)
    shrunk_ref[...] = shrunk
    change = jnp.broadcast_to(shrunk - old, (chunk, edge)).astype(jnp.bfloat16)
    landed_ref[...] = jnp.zeros_like(landed_ref)

    def run(part):
        images = lax.dot_general(
            change,
            listed_tiles(section, part, lists_ref, values_ref),
            (((1,), (1,)), ((), ())),
            preferred_element_type=jnp.float32,
        )
        for inner in range(chunk):
            place = lists_ref[2 * section + 1, part * chunk + inner]
            image = images[0:1, inner * edge : (inner + 1) * edge]
            landed_ref[pl.ds(place, 1), :] = landed_ref[pl.ds(place, 1), :] + image

    for_parts(section, lists_ref, run)
    weight = state_ref[1]
    residual = state_ref[0] - weight * landed_ref[pl.ds(0, group_blocks), :]
    if len(moved_ref.shape) == 3:
        moved_ref[0] = residual
        moved_ref[1] = weight
    else:
        moved_ref[...] = residual


def blocks_kernel(sections, targets_smem, beta_ref, *refs):
    blocks_ref = refs[sections]
    blocks_ref[...] = beta_ref[...]
    for section in range(sections):
        blocks_ref[pl.ds(targets_smem[0, section], 1), :] = refs[section][...]


def from_behind(value, axis, steps):
    count = lax.axis_size(axis)
    pairs = [(source, (source + steps) % count) for source in range(count)]
    return lax.ppermute(value, axis, pairs)


def gathered(parts, axis):
    count, edge = parts.shape
    order = list(range(count))
    if count % 2 == 0:
        half = count // 2
        far_apart = [pair // 2 if pair % 2 == 0 else half - 1 - pair // 2 for pair in range(half)]
        order = [2 * chip + 1 for chip in far_apart] + [2 * chip for chip in far_apart]
    received = lax.all_to_all(
        parts.reshape(count, 1, edge), axis, 0, 0, axis_index_groups=[order]
    )
    return received.reshape(count, edge)


def per_device(labels, beta, tile_rows, tile_cols, tile_values, block_order, hess_inv):
    sections = lax.axis_size("feat")
    samp_count = lax.axis_size("samp")
    tiles, edge = tile_values.shape[2], tile_values.shape[4]
    row_blocks = labels.shape[0] // edge
    group_blocks = row_blocks // sections
    blocks = beta.reshape(-1, edge)
    inverses = hess_inv[0]
    values = tile_values[0, 0]
    partial_sum, old_blocks, lists = pl.pallas_call(
        margins_kernel,
        out_shape=(
            float_of((row_blocks, edge)),
            float_of((sections, edge)),
            jax.ShapeDtypeStruct((2 * sections, tiles), jnp.int32),
        ),
        in_specs=[HBM] * 5,
        out_specs=(VMEM, VMEM, VMEM),
        scratch_shapes=[
            pltpu.VMEM((tiles, edge), jnp.float32),
            pltpu.VMEM(blocks.shape, jnp.float32),
            pltpu.VMEM((1, tiles), jnp.int32),
            pltpu.VMEM((1, tiles), jnp.int32),
            pltpu.VMEM(values.shape, jnp.bfloat16),
            pltpu.SMEM((1, tiles), jnp.int32),
            pltpu.SMEM((1, sections), jnp.int32),
            pltpu.SemaphoreType.DMA((5,)),
            pltpu.SemaphoreType.DMA((tiles // chunk,)),
        ],
        compiler_params=pltpu.CompilerParams(vmem_limit_bytes=58 << 20),
    )(tile_cols[0], block_order, tile_rows[0], blocks, values)
    parts = lax.all_to_all(
        partial_sum.reshape(sections, group_blocks, edge),
        "feat",
        0,
        0,
        axis_index_groups=[middle_first(sections)],
    )
    group_shape = (group_blocks, edge)
    state, grads = call(
        first_kernel,
        (float_of((2, *group_shape)), float_of((samp_count, edge))),
        [VMEM] * 6,
        [],
    )(parts, labels.reshape(row_blocks, edge), tile_rows[0], tile_cols[0], block_order, values)
    padded = pltpu.VMEM((group_blocks + 8, edge), jnp.float32)
    shrunk_blocks = []
    for section in range(sections):
        final = section + 1 == sections
        moving, shrunk = call(
            functools.partial(update_kernel, section),
            (float_of(group_shape if final else (2, *group_shape)), float_of((1, edge))),
            [VMEM] * 6,
            [padded],
        )(gathered(grads, "samp"), state, lists, old_blocks, inverses, values)
        shrunk_blocks.append(shrunk)
        state = from_behind(moving, "feat", 1)
        if not final:
            grads = call(
                functools.partial(gradient_kernel, section + 1),
                float_of((samp_count, edge)),
                [VMEM] * 3,
                [padded, pltpu.VMEM((chunk, edge), jnp.float32)],
            )(state, lists, values)
    blocks = call(
        functools.partial(blocks_kernel, sections),
        float_of(blocks.shape),
        [SMEM] + [VMEM] * (1 + sections),
        [],
    )(block_order, blocks, *shrunk_blocks)
    return (blocks.reshape(-1), state.reshape(-1))


def solution(mesh):
    placed = (
        P("samp"),
        P("feat"),
        P("samp", "feat", None),
        P("samp", "feat", None),
        P("samp", "feat", None, None, None),
        P("feat", None),
        P("feat", None, None, None),
    )
    return jax.shard_map(
        per_device,
        mesh=mesh,
        in_specs=placed,
        out_specs=(P("feat"), P(("samp", "feat"))),
        check_vma=False,
    )
```

```python
import functools

import jax
import jax.numpy as jnp
from jax import lax
from jax.experimental import pallas as pl
from jax.experimental.pallas import tpu as pltpu
from jax.sharding import PartitionSpec as P

exact_prec = lax.Precision.HIGHEST
l1_penalty = 0.25
chunk = 16
copied = 4

VMEM = pl.BlockSpec(memory_space=pltpu.VMEM)
SMEM = pl.BlockSpec(memory_space=pltpu.SMEM)
HBM = pl.BlockSpec(memory_space=pltpu.HBM)


def float_of(shape):
    return jax.ShapeDtypeStruct(shape, jnp.float32)


def call(kernel, out_shape, in_specs, scratch_shapes):
    single = not isinstance(out_shape, tuple)
    return pl.pallas_call(
        kernel,
        out_shape=out_shape,
        in_specs=in_specs,
        out_specs=VMEM if single else tuple(VMEM for _ in out_shape),
        scratch_shapes=scratch_shapes,
        compiler_params=pltpu.CompilerParams(vmem_limit_bytes=24 << 20),
    )


def middle_first(count):
    return sorted(range(count), key=lambda index: (abs(index - count // 2), index))


def tile_products(vectors_of, tiles_of, tiles):
    pieces = []
    for first in range(0, tiles, chunk):
        vectors = vectors_of(first)
        edge = vectors.shape[1]
        products = lax.dot_general(
            vectors,
            tiles_of(first).reshape(chunk * edge, edge),
            (((1,), (1,)), ((), ())),
            preferred_element_type=jnp.float32,
        )
        sub = lax.broadcasted_iota(jnp.int32, (chunk, edge), 0)
        piece = products[:, :edge]
        for inner in range(1, chunk):
            piece = jnp.where(sub == inner, products[:, inner * edge : (inner + 1) * edge], piece)
        pieces.append(piece)
    return jnp.concatenate(pieces, axis=0)


def placed_sum(chosen, rows):
    high = rows.astype(jnp.bfloat16)
    rest = rows - high.astype(jnp.float32)
    middle = rest.astype(jnp.bfloat16)
    low = (rest - middle.astype(jnp.float32)).astype(jnp.bfloat16)
    ones = chosen.astype(jnp.bfloat16)
    return sum(
        jnp.dot(ones, part, preferred_element_type=jnp.float32) for part in (low, middle, high)
    )


def over_lanes(left, right):
    return lax.dot_general(
        left.astype(jnp.bfloat16),
        right.astype(jnp.bfloat16),
        (((1,), (1,)), ((), ())),
        preferred_element_type=jnp.float32,
    )


def listed(row_in_group, taken, group_blocks):
    tiles = taken.shape[1]
    square = (tiles, tiles)
    sub = lax.broadcasted_iota(jnp.int32, square, 0)
    lane = lax.broadcasted_iota(jnp.int32, square, 1)
    taken = jnp.broadcast_to(taken, (8, tiles)).astype(jnp.float32)
    before = over_lanes(taken, (lane < sub).astype(jnp.float32))
    in_slot = (sub == before[0:1].astype(jnp.int32)) & (taken[0:1] > 0.0)
    numbers = lax.broadcasted_iota(jnp.int32, (8, tiles), 1) + 1
    short = group_blocks - row_in_group
    facts = jnp.where(lax.broadcasted_iota(jnp.int32, (8, tiles), 0) == 0, numbers, short)
    found = over_lanes(facts.astype(jnp.float32), in_slot.astype(jnp.float32)).astype(jnp.int32)
    return found[0:1] - 1, group_blocks - found[1:2]


def margins_kernel(
    cols_hbm, targets_hbm, rows_hbm, beta_hbm, values_hbm,
    partial_ref, old_ref, lists_ref,
    picked_ref, beta_ref, rows_ref, cols_ref, values_ref,
    cols_smem, targets_smem, small_sem, tile_sem,
):
    tiles = cols_smem.shape[1]
    sections = targets_smem.shape[1]
    row_blocks = partial_ref.shape[0]
    small = [
        pltpu.make_async_copy(cols_hbm, cols_smem, small_sem.at[0]),
        pltpu.make_async_copy(beta_hbm, beta_ref, small_sem.at[1]),
        pltpu.make_async_copy(targets_hbm, targets_smem, small_sem.at[2]),
        pltpu.make_async_copy(rows_hbm, rows_ref, small_sem.at[3]),
        pltpu.make_async_copy(cols_hbm, cols_ref, small_sem.at[4]),
    ]
    large = [
        pltpu.make_async_copy(
            values_hbm.at[pl.ds(first, copied)],
            values_ref.at[pl.ds(first, copied)],
            tile_sem.at[first // copied],
        )
        for first in range(0, tiles, copied)
    ]
    for copy in small + large:
        copy.start()
    for copy in small:
        copy.wait()
    for tile in range(tiles):
        picked_ref[pl.ds(tile, 1), :] = beta_ref[pl.ds(cols_smem[0, tile], 1), :]
    for section in range(sections):
        old_ref[pl.ds(section, 1), :] = beta_ref[pl.ds(targets_smem[0, section], 1), :]

    my_index = lax.axis_index("feat")
    group_blocks = row_blocks // sections
    for section in range(sections):
        group = lax.rem(my_index - section + sections, sections)
        row_in_group = rows_ref[...] - group * group_blocks
        taken = (
            (row_in_group >= 0)
            & (row_in_group < group_blocks)
            & (cols_ref[...] == targets_smem[0, section])
        )
        ids, places = listed(row_in_group, taken, group_blocks)
        lists_ref[pl.ds(2 * section, 1), :] = ids
        lists_ref[pl.ds(2 * section + 1, 1), :] = places

    def tiles_of(first):
        for copy in large[first // copied : (first + chunk) // copied]:
            copy.wait()
        return values_ref[pl.ds(first, chunk)]

    products = tile_products(
        lambda first: picked_ref[pl.ds(first, chunk), :].astype(jnp.bfloat16), tiles_of, tiles
    )
    block_ids = lax.broadcasted_iota(jnp.int32, (row_blocks, tiles), 0)
    placing = (block_ids == rows_ref[...]).astype(jnp.float32)
    partial = placed_sum(placing, products)
    for place, group in enumerate(middle_first(sections)):
        partial_ref[pl.ds(place * group_blocks, group_blocks), :] = partial[
            group * group_blocks : (group + 1) * group_blocks
        ]


def listed_tiles(section, part, lists_ref, values_ref):
    return jnp.concatenate(
        [
            values_ref[jnp.maximum(lists_ref[2 * section, part * chunk + inner], 0)]
            for inner in range(chunk)
        ],
        axis=0,
    )


def for_parts(section, lists_ref, run, part=0):
    run(part)
    if (part + 1) * chunk < lists_ref.shape[1]:
        more = lists_ref[2 * section, (part + 1) * chunk] >= 0
        pl.when(more)(functools.partial(for_parts, section, lists_ref, run, part + 1))


def gradient_of_all(residual, chosen, values_ref):
    tiles, edge, _ = values_ref.shape
    picked = lax.dot_general(
        chosen.astype(jnp.bfloat16),
        residual.astype(jnp.bfloat16),
        (((0,), (0,)), ((), ())),
        preferred_element_type=jnp.float32,
    )
    sub = lax.broadcasted_iota(jnp.int32, (chunk, edge), 0)
    spread = []
    for tile in range(tiles):
        first = tile - tile % chunk
        kept = jnp.where(sub == tile - first, picked[first : first + chunk], 0.0)
        spread.append(kept.astype(jnp.bfloat16))
    summed = jnp.dot(
        jnp.concatenate(spread, axis=1),
        values_ref[...].reshape(tiles * edge, edge),
        preferred_element_type=jnp.float32,
    )
    return jnp.sum(summed, axis=0, keepdims=True)


def first_kernel(
    parts_ref, labels_ref, rows_ref, cols_ref, targets_ref, values_ref, state_ref, grad_ref
):
    group_blocks = parts_ref.shape[1]
    first_row = lax.axis_index("feat") * group_blocks
    sub_ids = lax.broadcasted_iota(jnp.int32, (group_blocks, rows_ref.shape[1]), 0)
    same_row = sub_ids + first_row == rows_ref[...]
    chosen = (same_row & (cols_ref[...] == targets_ref[:, 0:1])).astype(jnp.float32)
    margins = parts_ref[0]
    for part in range(1, parts_ref.shape[0]):
        margins = margins + parts_ref[part]
    probability = 1.0 / (1.0 + jnp.exp(-margins))
    labels = labels_ref[pl.ds(pl.multiple_of(first_row, 8), group_blocks), :]
    residual = labels.astype(jnp.float32) - probability
    state_ref[0] = residual
    state_ref[1] = probability * (1.0 - probability)
    grad = gradient_of_all(residual, chosen, values_ref)
    grad_ref[...] = jnp.broadcast_to(grad, grad_ref.shape)


def gradient_kernel(section, state_ref, lists_ref, values_ref, grad_ref, rows_ref, total_ref):
    _, group_blocks, edge = state_ref.shape
    rows_ref[pl.ds(0, group_blocks), :] = state_ref[0]
    rows_ref[pl.ds(group_blocks, 8), :] = jnp.zeros((8, edge), jnp.float32)

    def run(part):
        spread = []
        for inner in range(chunk):
            place = lists_ref[2 * section + 1, part * chunk + inner]
            row = jnp.broadcast_to(rows_ref[pl.ds(place, 1), :], (chunk, edge))
            spread.append(row.astype(jnp.bfloat16))
        total = jnp.dot(
            jnp.concatenate(spread, axis=1),
            listed_tiles(section, part, lists_ref, values_ref),
            preferred_element_type=jnp.float32,
        )
        total_ref[...] = total if part == 0 else total_ref[...] + total

    for_parts(section, lists_ref, run)
    grad_ref[...] = jnp.broadcast_to(total_ref[0:1, :], grad_ref.shape)


def update_kernel(
    section, grads_ref, state_ref, lists_ref, old_ref, inverses_ref, values_ref,
    moved_ref, shrunk_ref, landed_ref,
):
    _, group_blocks, edge = state_ref.shape
    gradient = jnp.sum(grads_ref[...], axis=0, keepdims=True)
    step = jnp.sum(inverses_ref[section] * gradient, axis=1, keepdims=True)
    square = (edge, edge)
    on_diagonal = lax.broadcasted_iota(jnp.int32, square, 0) == lax.broadcasted_iota(
        jnp.int32, square, 1
    )
    step = jnp.sum(jnp.where(on_diagonal, step, 0.0), axis=0, keepdims=True)
    old = old_ref[pl.ds(section, 1), :]
    raised = old + step
    size = jnp.maximum(jnp.abs(raised) - l1_penalty, 0.0)
    shrunk = jnp.where(raised < 0.0, -size, size)
    shrunk_ref[...] = shrunk
    change = jnp.broadcast_to(shrunk - old, (chunk, edge)).astype(jnp.bfloat16)
    landed_ref[...] = jnp.zeros_like(landed_ref)

    def run(part):
        images = lax.dot_general(
            change,
            listed_tiles(section, part, lists_ref, values_ref),
            (((1,), (1,)), ((), ())),
            preferred_element_type=jnp.float32,
        )
        for inner in range(chunk):
            place = lists_ref[2 * section + 1, part * chunk + inner]
            image = images[0:1, inner * edge : (inner + 1) * edge]
            landed_ref[pl.ds(place, 1), :] = landed_ref[pl.ds(place, 1), :] + image

    for_parts(section, lists_ref, run)
    weight = state_ref[1]
    residual = state_ref[0] - weight * landed_ref[pl.ds(0, group_blocks), :]
    if len(moved_ref.shape) == 3:
        moved_ref[0] = residual
        moved_ref[1] = weight
    else:
        moved_ref[...] = residual


def blocks_kernel(sections, targets_smem, beta_ref, *refs):
    blocks_ref = refs[sections]
    blocks_ref[...] = beta_ref[...]
    for section in range(sections):
        blocks_ref[pl.ds(targets_smem[0, section], 1), :] = refs[section][...]


def from_behind(value, axis, steps):
    count = lax.axis_size(axis)
    pairs = [(source, (source + steps) % count) for source in range(count)]
    return lax.ppermute(value, axis, pairs)


def gathered(parts, axis):
    count, edge = parts.shape
    order = list(range(count))
    if count % 2 == 0:
        half = count // 2
        far_apart = [pair // 2 if pair % 2 == 0 else half - 1 - pair // 2 for pair in range(half)]
        order = [2 * chip + 1 for chip in far_apart] + [2 * chip for chip in far_apart]
    received = lax.all_to_all(
        parts.reshape(count, 1, edge), axis, 0, 0, axis_index_groups=[order]
    )
    return received.reshape(count, edge)


def per_device(labels, beta, tile_rows, tile_cols, tile_values, block_order, hess_inv):
    sections = lax.axis_size("feat")
    samp_count = lax.axis_size("samp")
    tiles, edge = tile_values.shape[2], tile_values.shape[4]
    row_blocks = labels.shape[0] // edge
    group_blocks = row_blocks // sections
    blocks = beta.reshape(-1, edge)
    inverses = hess_inv[0]
    values = tile_values[0, 0]
    partial_sum, old_blocks, lists = pl.pallas_call(
        margins_kernel,
        out_shape=(
            float_of((row_blocks, edge)),
            float_of((sections, edge)),
            jax.ShapeDtypeStruct((2 * sections, tiles), jnp.int32),
        ),
        in_specs=[HBM] * 5,
        out_specs=(VMEM, VMEM, VMEM),
        scratch_shapes=[
            pltpu.VMEM((tiles, edge), jnp.float32),
            pltpu.VMEM(blocks.shape, jnp.float32),
            pltpu.VMEM((1, tiles), jnp.int32),
            pltpu.VMEM((1, tiles), jnp.int32),
            pltpu.VMEM(values.shape, jnp.bfloat16),
            pltpu.SMEM((1, tiles), jnp.int32),
            pltpu.SMEM((1, sections), jnp.int32),
            pltpu.SemaphoreType.DMA((5,)),
            pltpu.SemaphoreType.DMA((tiles // copied,)),
        ],
        compiler_params=pltpu.CompilerParams(vmem_limit_bytes=58 << 20),
    )(tile_cols[0], block_order, tile_rows[0], blocks, values)
    parts = lax.all_to_all(
        partial_sum.reshape(sections, group_blocks, edge),
        "feat",
        0,
        0,
        axis_index_groups=[middle_first(sections)],
    )
    group_shape = (group_blocks, edge)
    state, grads = call(
        first_kernel,
        (float_of((2, *group_shape)), float_of((samp_count, edge))),
        [VMEM] * 6,
        [],
    )(parts, labels.reshape(row_blocks, edge), tile_rows[0], tile_cols[0], block_order, values)
    padded = pltpu.VMEM((group_blocks + 8, edge), jnp.float32)
    shrunk_blocks = []
    for section in range(sections):
        final = section + 1 == sections
        moving, shrunk = call(
            functools.partial(update_kernel, section),
            (float_of(group_shape if final else (2, *group_shape)), float_of((1, edge))),
            [VMEM] * 6,
            [padded],
        )(gathered(grads, "samp"), state, lists, old_blocks, inverses, values)
        shrunk_blocks.append(shrunk)
        state = from_behind(moving, "feat", 1)
        if not final:
            grads = call(
                functools.partial(gradient_kernel, section + 1),
                float_of((samp_count, edge)),
                [VMEM] * 3,
                [padded, pltpu.VMEM((chunk, edge), jnp.float32)],
            )(state, lists, values)
    blocks = call(
        functools.partial(blocks_kernel, sections),
        float_of(blocks.shape),
        [SMEM] + [VMEM] * (1 + sections),
        [],
    )(block_order, blocks, *shrunk_blocks)
    return (blocks.reshape(-1), state.reshape(-1))


def solution(mesh):
    placed = (
        P("samp"),
        P("feat"),
        P("samp", "feat", None),
        P("samp", "feat", None),
        P("samp", "feat", None, None, None),
        P("feat", None),
        P("feat", None, None, None),
    )
    return jax.shard_map(
        per_device,
        mesh=mesh,
        in_specs=placed,
        out_specs=(P("feat"), P(("samp", "feat"))),
        check_vma=False,
    )
```

```python
import functools

import jax
import jax.numpy as jnp
from jax import lax
from jax.experimental import pallas as pl
from jax.experimental.pallas import tpu as pltpu
from jax.sharding import PartitionSpec as P

exact_prec = lax.Precision.HIGHEST
l1_penalty = 0.25
chunk = 16
copied = 16

VMEM = pl.BlockSpec(memory_space=pltpu.VMEM)
SMEM = pl.BlockSpec(memory_space=pltpu.SMEM)
HBM = pl.BlockSpec(memory_space=pltpu.HBM)


def float_of(shape):
    return jax.ShapeDtypeStruct(shape, jnp.float32)


def call(kernel, out_shape, in_specs, scratch_shapes):
    single = not isinstance(out_shape, tuple)
    return pl.pallas_call(
        kernel,
        out_shape=out_shape,
        in_specs=in_specs,
        out_specs=VMEM if single else tuple(VMEM for _ in out_shape),
        scratch_shapes=scratch_shapes,
        compiler_params=pltpu.CompilerParams(vmem_limit_bytes=24 << 20),
    )


def middle_first(count):
    return sorted(range(count), key=lambda index: (abs(index - count // 2), index))


def tile_products(vectors_of, tiles_of, tiles):
    pieces = []
    for first in range(0, tiles, chunk):
        vectors = vectors_of(first)
        edge = vectors.shape[1]
        products = lax.dot_general(
            vectors,
            tiles_of(first).reshape(chunk * edge, edge),
            (((1,), (1,)), ((), ())),
            preferred_element_type=jnp.float32,
        )
        sub = lax.broadcasted_iota(jnp.int32, (chunk, edge), 0)
        piece = products[:, :edge]
        for inner in range(1, chunk):
            piece = jnp.where(sub == inner, products[:, inner * edge : (inner + 1) * edge], piece)
        pieces.append(piece)
    return jnp.concatenate(pieces, axis=0)


def placed_sum(chosen, rows):
    high = rows.astype(jnp.bfloat16)
    rest = rows - high.astype(jnp.float32)
    middle = rest.astype(jnp.bfloat16)
    low = (rest - middle.astype(jnp.float32)).astype(jnp.bfloat16)
    ones = chosen.astype(jnp.bfloat16)
    return sum(
        jnp.dot(ones, part, preferred_element_type=jnp.float32) for part in (low, middle, high)
    )


def over_lanes(left, right):
    return lax.dot_general(
        left.astype(jnp.bfloat16),
        right.astype(jnp.bfloat16),
        (((1,), (1,)), ((), ())),
        preferred_element_type=jnp.float32,
    )


def bits_of(group_blocks):
    return group_blocks.bit_length()


def listed(row_in_group, taken, group_blocks):
    tiles = taken.shape[1]
    square = (tiles, tiles)
    sub = lax.broadcasted_iota(jnp.int32, square, 0)
    lane = lax.broadcasted_iota(jnp.int32, square, 1)
    taken = jnp.broadcast_to(taken, (8, tiles)).astype(jnp.float32)
    before = over_lanes(taken, (lane < sub).astype(jnp.float32))
    in_slot = (sub == before[0:1].astype(jnp.int32)) & (taken[0:1] > 0.0)
    numbers = lax.broadcasted_iota(jnp.int32, (8, tiles), 1)
    short = group_blocks - row_in_group
    facts = jnp.where(lax.broadcasted_iota(jnp.int32, (8, tiles), 0) == 0, numbers, short)
    found = over_lanes(facts.astype(jnp.float32), in_slot.astype(jnp.float32)).astype(jnp.int32)
    return found[0:1] * 2 ** bits_of(group_blocks) + group_blocks - found[1:2]


def margins_kernel(
    cols_hbm, targets_hbm, rows_hbm, beta_hbm, values_hbm,
    partial_ref, old_ref, lists_ref,
    picked_ref, beta_ref, rows_ref, cols_ref, values_ref,
    cols_smem, targets_smem, small_sem, tile_sem,
):
    tiles = cols_smem.shape[1]
    sections = targets_smem.shape[1]
    row_blocks = partial_ref.shape[0]
    small = [
        pltpu.make_async_copy(cols_hbm, cols_smem, small_sem.at[0]),
        pltpu.make_async_copy(beta_hbm, beta_ref, small_sem.at[1]),
        pltpu.make_async_copy(targets_hbm, targets_smem, small_sem.at[2]),
        pltpu.make_async_copy(rows_hbm, rows_ref, small_sem.at[3]),
        pltpu.make_async_copy(cols_hbm, cols_ref, small_sem.at[4]),
    ]
    large = [
        pltpu.make_async_copy(
            values_hbm.at[pl.ds(first, copied)],
            values_ref.at[pl.ds(first, copied)],
            tile_sem.at[first // copied],
        )
        for first in range(0, tiles, copied)
    ]
    for copy in small + large:
        copy.start()
    for copy in small:
        copy.wait()
    for tile in range(tiles):
        picked_ref[pl.ds(tile, 1), :] = beta_ref[pl.ds(cols_smem[0, tile], 1), :]
    for section in range(sections):
        old_ref[pl.ds(section, 1), :] = beta_ref[pl.ds(targets_smem[0, section], 1), :]

    def tiles_of(first):
        for copy in large[first // copied : (first + chunk) // copied]:
            copy.wait()
        return values_ref[pl.ds(first, chunk)]

    products = tile_products(
        lambda first: picked_ref[pl.ds(first, chunk), :].astype(jnp.bfloat16), tiles_of, tiles
    )
    my_index = lax.axis_index("feat")
    group_blocks = row_blocks // sections
    for section in range(sections):
        group = lax.rem(my_index - section + sections, sections)
        row_in_group = rows_ref[...] - group * group_blocks
        taken = (
            (row_in_group >= 0)
            & (row_in_group < group_blocks)
            & (cols_ref[...] == targets_smem[0, section])
        )
        lists_ref[pl.ds(section, 1), :] = listed(row_in_group, taken, group_blocks)

    block_ids = lax.broadcasted_iota(jnp.int32, (row_blocks, tiles), 0)
    placing = (block_ids == rows_ref[...]).astype(jnp.float32)
    partial = placed_sum(placing, products)
    for place, group in enumerate(middle_first(sections)):
        partial_ref[pl.ds(place * group_blocks, group_blocks), :] = partial[
            group * group_blocks : (group + 1) * group_blocks
        ]


def listed_slots(section, part, group_blocks, lists_ref, values_ref):
    bits = bits_of(group_blocks)
    found = [lists_ref[section, part * chunk + inner] for inner in range(chunk)]
    tiles = [values_ref[lax.shift_right_logical(number, bits)] for number in found]
    return jnp.concatenate(tiles, axis=0), [number & (2**bits - 1) for number in found]


def for_parts(section, group_blocks, lists_ref, run, part=0):
    run(part)
    if (part + 1) * chunk < lists_ref.shape[1]:
        more = lists_ref[section, (part + 1) * chunk] != group_blocks
        pl.when(more)(
            functools.partial(for_parts, section, group_blocks, lists_ref, run, part + 1)
        )


def gradient_of_all(residual, chosen, values_ref):
    tiles, edge, _ = values_ref.shape
    picked = lax.dot_general(
        chosen.astype(jnp.bfloat16),
        residual.astype(jnp.bfloat16),
        (((0,), (0,)), ((), ())),
        preferred_element_type=jnp.float32,
    )
    sub = lax.broadcasted_iota(jnp.int32, (chunk, edge), 0)
    spread = []
    for tile in range(tiles):
        first = tile - tile % chunk
        kept = jnp.where(sub == tile - first, picked[first : first + chunk], 0.0)
        spread.append(kept.astype(jnp.bfloat16))
    summed = jnp.dot(
        jnp.concatenate(spread, axis=1),
        values_ref[...].reshape(tiles * edge, edge),
        preferred_element_type=jnp.float32,
    )
    return jnp.sum(summed, axis=0, keepdims=True)


def first_kernel(
    parts_ref, labels_ref, rows_ref, cols_ref, targets_ref, values_ref, state_ref, grad_ref
):
    group_blocks = parts_ref.shape[1]
    first_row = lax.axis_index("feat") * group_blocks
    sub_ids = lax.broadcasted_iota(jnp.int32, (group_blocks, rows_ref.shape[1]), 0)
    same_row = sub_ids + first_row == rows_ref[...]
    chosen = (same_row & (cols_ref[...] == targets_ref[:, 0:1])).astype(jnp.float32)
    margins = parts_ref[0]
    for part in range(1, parts_ref.shape[0]):
        margins = margins + parts_ref[part]
    probability = 1.0 / (1.0 + jnp.exp(-margins))
    labels = labels_ref[pl.ds(pl.multiple_of(first_row, 8), group_blocks), :]
    residual = labels.astype(jnp.float32) - probability
    state_ref[0] = residual
    state_ref[1] = probability * (1.0 - probability)
    grad = gradient_of_all(residual, chosen, values_ref)
    grad_ref[...] = jnp.broadcast_to(grad, grad_ref.shape)


def gradient_kernel(section, state_ref, lists_ref, values_ref, grad_ref, rows_ref, total_ref):
    _, group_blocks, edge = state_ref.shape
    rows_ref[pl.ds(0, group_blocks), :] = state_ref[0]
    rows_ref[pl.ds(group_blocks, 8), :] = jnp.zeros((8, edge), jnp.float32)

    def run(part):
        tiles, places = listed_slots(section, part, group_blocks, lists_ref, values_ref)
        spread = []
        for place in places:
            row = jnp.broadcast_to(rows_ref[pl.ds(place, 1), :], (chunk, edge))
            spread.append(row.astype(jnp.bfloat16))
        total = jnp.dot(
            jnp.concatenate(spread, axis=1), tiles, preferred_element_type=jnp.float32
        )
        total_ref[...] = total if part == 0 else total_ref[...] + total

    for_parts(section, group_blocks, lists_ref, run)
    grad_ref[...] = jnp.broadcast_to(total_ref[0:1, :], grad_ref.shape)


def update_kernel(
    section, grads_ref, state_ref, lists_ref, old_ref, inverses_ref, values_ref,
    moved_ref, shrunk_ref, landed_ref,
):
    _, group_blocks, edge = state_ref.shape
    gradient = jnp.sum(grads_ref[...], axis=0, keepdims=True)
    step = jnp.sum(inverses_ref[section] * gradient, axis=1, keepdims=True)
    square = (edge, edge)
    on_diagonal = lax.broadcasted_iota(jnp.int32, square, 0) == lax.broadcasted_iota(
        jnp.int32, square, 1
    )
    step = jnp.sum(jnp.where(on_diagonal, step, 0.0), axis=0, keepdims=True)
    old = old_ref[pl.ds(section, 1), :]
    raised = old + step
    size = jnp.maximum(jnp.abs(raised) - l1_penalty, 0.0)
    shrunk = jnp.where(raised < 0.0, -size, size)
    shrunk_ref[...] = shrunk
    change = jnp.broadcast_to(shrunk - old, (chunk, edge)).astype(jnp.bfloat16)
    landed_ref[...] = jnp.zeros_like(landed_ref)

    def run(part):
        tiles, places = listed_slots(section, part, group_blocks, lists_ref, values_ref)
        images = lax.dot_general(
            change, tiles, (((1,), (1,)), ((), ())), preferred_element_type=jnp.float32
        )
        for inner, place in enumerate(places):
            image = images[0:1, inner * edge : (inner + 1) * edge]
            landed_ref[pl.ds(place, 1), :] = landed_ref[pl.ds(place, 1), :] + image

    for_parts(section, group_blocks, lists_ref, run)
    weight = state_ref[1]
    residual = state_ref[0] - weight * landed_ref[pl.ds(0, group_blocks), :]
    if len(moved_ref.shape) == 3:
        moved_ref[0] = residual
        moved_ref[1] = weight
    else:
        moved_ref[...] = residual


def blocks_kernel(sections, targets_smem, beta_ref, *refs):
    blocks_ref = refs[sections]
    blocks_ref[...] = beta_ref[...]
    for section in range(sections):
        blocks_ref[pl.ds(targets_smem[0, section], 1), :] = refs[section][...]


def from_behind(value, axis, steps):
    count = lax.axis_size(axis)
    pairs = [(source, (source + steps) % count) for source in range(count)]
    return lax.ppermute(value, axis, pairs)


def gathered(parts, axis):
    count, edge = parts.shape
    order = list(range(count))
    if count % 2 == 0:
        half = count // 2
        far_apart = [pair // 2 if pair % 2 == 0 else half - 1 - pair // 2 for pair in range(half)]
        order = [2 * chip + 1 for chip in far_apart] + [2 * chip for chip in far_apart]
    received = lax.all_to_all(
        parts.reshape(count, 1, edge), axis, 0, 0, axis_index_groups=[order]
    )
    return received.reshape(count, edge)


def per_device(labels, beta, tile_rows, tile_cols, tile_values, block_order, hess_inv):
    sections = lax.axis_size("feat")
    samp_count = lax.axis_size("samp")
    tiles, edge = tile_values.shape[2], tile_values.shape[4]
    row_blocks = labels.shape[0] // edge
    group_blocks = row_blocks // sections
    blocks = beta.reshape(-1, edge)
    inverses = hess_inv[0]
    values = tile_values[0, 0]
    partial_sum, old_blocks, lists = pl.pallas_call(
        margins_kernel,
        out_shape=(
            float_of((row_blocks, edge)),
            float_of((sections, edge)),
            jax.ShapeDtypeStruct((sections, tiles), jnp.int32),
        ),
        in_specs=[HBM] * 5,
        out_specs=(VMEM, VMEM, VMEM),
        scratch_shapes=[
            pltpu.VMEM((tiles, edge), jnp.float32),
            pltpu.VMEM(blocks.shape, jnp.float32),
            pltpu.VMEM((1, tiles), jnp.int32),
            pltpu.VMEM((1, tiles), jnp.int32),
            pltpu.VMEM(values.shape, jnp.bfloat16),
            pltpu.SMEM((1, tiles), jnp.int32),
            pltpu.SMEM((1, sections), jnp.int32),
            pltpu.SemaphoreType.DMA((5,)),
            pltpu.SemaphoreType.DMA((tiles // copied,)),
        ],
        compiler_params=pltpu.CompilerParams(vmem_limit_bytes=58 << 20),
    )(tile_cols[0], block_order, tile_rows[0], blocks, values)
    parts = lax.all_to_all(
        partial_sum.reshape(sections, group_blocks, edge),
        "feat",
        0,
        0,
        axis_index_groups=[middle_first(sections)],
    )
    group_shape = (group_blocks, edge)
    state, grads = call(
        first_kernel,
        (float_of((2, *group_shape)), float_of((samp_count, edge))),
        [VMEM] * 6,
        [],
    )(parts, labels.reshape(row_blocks, edge), tile_rows[0], tile_cols[0], block_order, values)
    padded = pltpu.VMEM((group_blocks + 8, edge), jnp.float32)
    shrunk_blocks = []
    for section in range(sections):
        final = section + 1 == sections
        moving, shrunk = call(
            functools.partial(update_kernel, section),
            (float_of(group_shape if final else (2, *group_shape)), float_of((1, edge))),
            [VMEM] * 6,
            [padded],
        )(gathered(grads, "samp"), state, lists, old_blocks, inverses, values)
        shrunk_blocks.append(shrunk)
        state = from_behind(moving, "feat", 1)
        if not final:
            grads = call(
                functools.partial(gradient_kernel, section + 1),
                float_of((samp_count, edge)),
                [VMEM] * 3,
                [padded, pltpu.VMEM((chunk, edge), jnp.float32)],
            )(state, lists, values)
    blocks = call(
        functools.partial(blocks_kernel, sections),
        float_of(blocks.shape),
        [SMEM] + [VMEM] * (1 + sections),
        [],
    )(block_order, blocks, *shrunk_blocks)
    return (blocks.reshape(-1), state.reshape(-1))


def solution(mesh):
    placed = (
        P("samp"),
        P("feat"),
        P("samp", "feat", None),
        P("samp", "feat", None),
        P("samp", "feat", None, None, None),
        P("feat", None),
        P("feat", None, None, None),
    )
    return jax.shard_map(
        per_device,
        mesh=mesh,
        in_specs=placed,
        out_specs=(P("feat"), P(("samp", "feat"))),
        check_vma=False,
    )
```

```python
import functools

import jax
import jax.numpy as jnp
from jax import lax
from jax.experimental import pallas as pl
from jax.experimental.pallas import tpu as pltpu
from jax.sharding import PartitionSpec as P

exact_prec = lax.Precision.HIGHEST
l1_penalty = 0.25
chunk = 16
copied = 16

VMEM = pl.BlockSpec(memory_space=pltpu.VMEM)
SMEM = pl.BlockSpec(memory_space=pltpu.SMEM)
HBM = pl.BlockSpec(memory_space=pltpu.HBM)


def float_of(shape):
    return jax.ShapeDtypeStruct(shape, jnp.float32)


def call(kernel, out_shape, in_specs, scratch_shapes):
    single = not isinstance(out_shape, tuple)
    return pl.pallas_call(
        kernel,
        out_shape=out_shape,
        in_specs=in_specs,
        out_specs=VMEM if single else tuple(VMEM for _ in out_shape),
        scratch_shapes=scratch_shapes,
        compiler_params=pltpu.CompilerParams(vmem_limit_bytes=24 << 20),
    )


def last_first(count):
    return list(range(count))[::-1]


def tile_products(vectors_of, tiles_of, tiles):
    pieces = []
    for first in range(0, tiles, chunk):
        vectors = vectors_of(first)
        edge = vectors.shape[1]
        products = lax.dot_general(
            vectors,
            tiles_of(first).reshape(chunk * edge, edge),
            (((1,), (1,)), ((), ())),
            preferred_element_type=jnp.float32,
        )
        sub = lax.broadcasted_iota(jnp.int32, (chunk, edge), 0)
        piece = products[:, :edge]
        for inner in range(1, chunk):
            piece = jnp.where(sub == inner, products[:, inner * edge : (inner + 1) * edge], piece)
        pieces.append(piece)
    return jnp.concatenate(pieces, axis=0)


def placed_sum(chosen, rows):
    high = rows.astype(jnp.bfloat16)
    rest = rows - high.astype(jnp.float32)
    middle = rest.astype(jnp.bfloat16)
    low = (rest - middle.astype(jnp.float32)).astype(jnp.bfloat16)
    ones = chosen.astype(jnp.bfloat16)
    return sum(
        jnp.dot(ones, part, preferred_element_type=jnp.float32) for part in (low, middle, high)
    )


def over_lanes(left, right):
    return lax.dot_general(
        left.astype(jnp.bfloat16),
        right.astype(jnp.bfloat16),
        (((1,), (1,)), ((), ())),
        preferred_element_type=jnp.float32,
    )


def bits_of(group_blocks):
    return group_blocks.bit_length()


def listed(row_in_group, taken, group_blocks):
    tiles = taken.shape[1]
    square = (tiles, tiles)
    sub = lax.broadcasted_iota(jnp.int32, square, 0)
    lane = lax.broadcasted_iota(jnp.int32, square, 1)
    taken = jnp.broadcast_to(taken, (8, tiles)).astype(jnp.float32)
    before = over_lanes(taken, (lane < sub).astype(jnp.float32))
    in_slot = (sub == before[0:1].astype(jnp.int32)) & (taken[0:1] > 0.0)
    numbers = lax.broadcasted_iota(jnp.int32, (8, tiles), 1)
    short = group_blocks - row_in_group
    facts = jnp.where(lax.broadcasted_iota(jnp.int32, (8, tiles), 0) == 0, numbers, short)
    found = over_lanes(facts.astype(jnp.float32), in_slot.astype(jnp.float32)).astype(jnp.int32)
    return found[0:1] * 2 ** bits_of(group_blocks) + group_blocks - found[1:2]


def margins_kernel(
    cols_hbm, targets_hbm, rows_hbm, beta_hbm, values_hbm,
    partial_ref, old_ref, lists_ref,
    picked_ref, beta_ref, rows_ref, cols_ref, values_ref,
    cols_smem, targets_smem, small_sem, tile_sem,
):
    tiles = cols_smem.shape[1]
    sections = targets_smem.shape[1]
    row_blocks = partial_ref.shape[0]
    small = [
        pltpu.make_async_copy(cols_hbm, cols_smem, small_sem.at[0]),
        pltpu.make_async_copy(beta_hbm, beta_ref, small_sem.at[1]),
        pltpu.make_async_copy(targets_hbm, targets_smem, small_sem.at[2]),
        pltpu.make_async_copy(rows_hbm, rows_ref, small_sem.at[3]),
        pltpu.make_async_copy(cols_hbm, cols_ref, small_sem.at[4]),
    ]
    large = [
        pltpu.make_async_copy(
            values_hbm.at[pl.ds(first, copied)],
            values_ref.at[pl.ds(first, copied)],
            tile_sem.at[first // copied],
        )
        for first in range(0, tiles, copied)
    ]
    for copy in small + large:
        copy.start()
    for copy in small:
        copy.wait()
    for tile in range(tiles):
        picked_ref[pl.ds(tile, 1), :] = beta_ref[pl.ds(cols_smem[0, tile], 1), :]
    for section in range(sections):
        old_ref[pl.ds(section, 1), :] = beta_ref[pl.ds(targets_smem[0, section], 1), :]

    def tiles_of(first):
        for copy in large[first // copied : (first + chunk) // copied]:
            copy.wait()
        return values_ref[pl.ds(first, chunk)]

    products = tile_products(
        lambda first: picked_ref[pl.ds(first, chunk), :].astype(jnp.bfloat16), tiles_of, tiles
    )
    my_index = lax.axis_index("feat")
    group_blocks = row_blocks // sections
    for section in range(sections):
        group = lax.rem(my_index - section + sections, sections)
        row_in_group = rows_ref[...] - group * group_blocks
        taken = (
            (row_in_group >= 0)
            & (row_in_group < group_blocks)
            & (cols_ref[...] == targets_smem[0, section])
        )
        lists_ref[pl.ds(section, 1), :] = listed(row_in_group, taken, group_blocks)

    block_ids = lax.broadcasted_iota(jnp.int32, (row_blocks, tiles), 0)
    placing = (block_ids == rows_ref[...]).astype(jnp.float32)
    partial = placed_sum(placing, products)
    for place, group in enumerate(last_first(sections)):
        partial_ref[pl.ds(place * group_blocks, group_blocks), :] = partial[
            group * group_blocks : (group + 1) * group_blocks
        ]


def listed_slots(section, part, group_blocks, lists_ref, values_ref):
    bits = bits_of(group_blocks)
    found = [lists_ref[section, part * chunk + inner] for inner in range(chunk)]
    tiles = [values_ref[lax.shift_right_logical(number, bits)] for number in found]
    return jnp.concatenate(tiles, axis=0), [number & (2**bits - 1) for number in found]


def for_parts(section, group_blocks, lists_ref, run, part=0):
    run(part)
    if (part + 1) * chunk < lists_ref.shape[1]:
        more = lists_ref[section, (part + 1) * chunk] != group_blocks
        pl.when(more)(
            functools.partial(for_parts, section, group_blocks, lists_ref, run, part + 1)
        )


def gradient_of_all(residual, chosen, values_ref):
    tiles, edge, _ = values_ref.shape
    picked = lax.dot_general(
        chosen.astype(jnp.bfloat16),
        residual.astype(jnp.bfloat16),
        (((0,), (0,)), ((), ())),
        preferred_element_type=jnp.float32,
    )
    sub = lax.broadcasted_iota(jnp.int32, (chunk, edge), 0)
    spread = []
    for tile in range(tiles):
        first = tile - tile % chunk
        kept = jnp.where(sub == tile - first, picked[first : first + chunk], 0.0)
        spread.append(kept.astype(jnp.bfloat16))
    summed = jnp.dot(
        jnp.concatenate(spread, axis=1),
        values_ref[...].reshape(tiles * edge, edge),
        preferred_element_type=jnp.float32,
    )
    return jnp.sum(summed, axis=0, keepdims=True)


def first_kernel(
    parts_ref, labels_ref, rows_ref, cols_ref, targets_ref, values_ref, state_ref, grad_ref
):
    group_blocks = parts_ref.shape[1]
    first_row = lax.axis_index("feat") * group_blocks
    sub_ids = lax.broadcasted_iota(jnp.int32, (group_blocks, rows_ref.shape[1]), 0)
    same_row = sub_ids + first_row == rows_ref[...]
    chosen = (same_row & (cols_ref[...] == targets_ref[:, 0:1])).astype(jnp.float32)
    margins = parts_ref[0]
    for part in range(1, parts_ref.shape[0]):
        margins = margins + parts_ref[part]
    probability = 1.0 / (1.0 + jnp.exp(-margins))
    labels = labels_ref[pl.ds(pl.multiple_of(first_row, 8), group_blocks), :]
    residual = labels.astype(jnp.float32) - probability
    state_ref[0] = residual
    state_ref[1] = probability * (1.0 - probability)
    grad = gradient_of_all(residual, chosen, values_ref)
    grad_ref[...] = jnp.broadcast_to(grad, grad_ref.shape)


def gradient_kernel(section, state_ref, lists_ref, values_ref, grad_ref, rows_ref, total_ref):
    _, group_blocks, edge = state_ref.shape
    rows_ref[pl.ds(0, group_blocks), :] = state_ref[0]
    rows_ref[pl.ds(group_blocks, 8), :] = jnp.zeros((8, edge), jnp.float32)

    def run(part):
        tiles, places = listed_slots(section, part, group_blocks, lists_ref, values_ref)
        spread = []
        for place in places:
            row = jnp.broadcast_to(rows_ref[pl.ds(place, 1), :], (chunk, edge))
            spread.append(row.astype(jnp.bfloat16))
        total = jnp.dot(
            jnp.concatenate(spread, axis=1), tiles, preferred_element_type=jnp.float32
        )
        total_ref[...] = total if part == 0 else total_ref[...] + total

    for_parts(section, group_blocks, lists_ref, run)
    grad_ref[...] = jnp.broadcast_to(total_ref[0:1, :], grad_ref.shape)


def update_kernel(
    section, grads_ref, state_ref, lists_ref, old_ref, inverses_ref, values_ref,
    moved_ref, shrunk_ref, landed_ref,
):
    _, group_blocks, edge = state_ref.shape
    gradient = jnp.sum(grads_ref[...], axis=0, keepdims=True)
    step = jnp.sum(inverses_ref[section] * gradient, axis=1, keepdims=True)
    square = (edge, edge)
    on_diagonal = lax.broadcasted_iota(jnp.int32, square, 0) == lax.broadcasted_iota(
        jnp.int32, square, 1
    )
    step = jnp.sum(jnp.where(on_diagonal, step, 0.0), axis=0, keepdims=True)
    old = old_ref[pl.ds(section, 1), :]
    raised = old + step
    size = jnp.maximum(jnp.abs(raised) - l1_penalty, 0.0)
    shrunk = jnp.where(raised < 0.0, -size, size)
    shrunk_ref[...] = shrunk
    change = jnp.broadcast_to(shrunk - old, (chunk, edge)).astype(jnp.bfloat16)
    landed_ref[...] = jnp.zeros_like(landed_ref)

    def run(part):
        tiles, places = listed_slots(section, part, group_blocks, lists_ref, values_ref)
        images = lax.dot_general(
            change, tiles, (((1,), (1,)), ((), ())), preferred_element_type=jnp.float32
        )
        for inner, place in enumerate(places):
            image = images[0:1, inner * edge : (inner + 1) * edge]
            landed_ref[pl.ds(place, 1), :] = landed_ref[pl.ds(place, 1), :] + image

    for_parts(section, group_blocks, lists_ref, run)
    weight = state_ref[1]
    residual = state_ref[0] - weight * landed_ref[pl.ds(0, group_blocks), :]
    if len(moved_ref.shape) == 3:
        moved_ref[0] = residual
        moved_ref[1] = weight
    else:
        moved_ref[...] = residual


def blocks_kernel(sections, targets_smem, beta_ref, *refs):
    blocks_ref = refs[sections]
    blocks_ref[...] = beta_ref[...]
    for section in range(sections):
        blocks_ref[pl.ds(targets_smem[0, section], 1), :] = refs[section][...]


def from_behind(value, axis, steps):
    count = lax.axis_size(axis)
    pairs = [(source, (source + steps) % count) for source in range(count)]
    return lax.ppermute(value, axis, pairs)


def gathered(parts, axis):
    count, edge = parts.shape
    order = list(range(count))
    if count % 2 == 0:
        half = count // 2
        far_apart = [half - 1 - pair // 2 if pair % 2 == 0 else pair // 2 for pair in range(half)]
        order = [2 * chip + 1 for chip in far_apart] + [2 * chip for chip in far_apart]
    received = lax.all_to_all(
        parts.reshape(count, 1, edge), axis, 0, 0, axis_index_groups=[order]
    )
    return received.reshape(count, edge)


def per_device(labels, beta, tile_rows, tile_cols, tile_values, block_order, hess_inv):
    sections = lax.axis_size("feat")
    samp_count = lax.axis_size("samp")
    tiles, edge = tile_values.shape[2], tile_values.shape[4]
    row_blocks = labels.shape[0] // edge
    group_blocks = row_blocks // sections
    blocks = beta.reshape(-1, edge)
    inverses = hess_inv[0]
    values = tile_values[0, 0]
    partial_sum, old_blocks, lists = pl.pallas_call(
        margins_kernel,
        out_shape=(
            float_of((row_blocks, edge)),
            float_of((sections, edge)),
            jax.ShapeDtypeStruct((sections, tiles), jnp.int32),
        ),
        in_specs=[HBM] * 5,
        out_specs=(VMEM, VMEM, VMEM),
        scratch_shapes=[
            pltpu.VMEM((tiles, edge), jnp.float32),
            pltpu.VMEM(blocks.shape, jnp.float32),
            pltpu.VMEM((1, tiles), jnp.int32),
            pltpu.VMEM((1, tiles), jnp.int32),
            pltpu.VMEM(values.shape, jnp.bfloat16),
            pltpu.SMEM((1, tiles), jnp.int32),
            pltpu.SMEM((1, sections), jnp.int32),
            pltpu.SemaphoreType.DMA((5,)),
            pltpu.SemaphoreType.DMA((tiles // copied,)),
        ],
        compiler_params=pltpu.CompilerParams(vmem_limit_bytes=58 << 20),
    )(tile_cols[0], block_order, tile_rows[0], blocks, values)
    parts = lax.all_to_all(
        partial_sum.reshape(sections, group_blocks, edge),
        "feat",
        0,
        0,
        axis_index_groups=[last_first(sections)],
    )
    group_shape = (group_blocks, edge)
    state, grads = call(
        first_kernel,
        (float_of((2, *group_shape)), float_of((samp_count, edge))),
        [VMEM] * 6,
        [],
    )(parts, labels.reshape(row_blocks, edge), tile_rows[0], tile_cols[0], block_order, values)
    padded = pltpu.VMEM((group_blocks + 8, edge), jnp.float32)
    shrunk_blocks = []
    for section in range(sections):
        final = section + 1 == sections
        moving, shrunk = call(
            functools.partial(update_kernel, section),
            (float_of(group_shape if final else (2, *group_shape)), float_of((1, edge))),
            [VMEM] * 6,
            [padded],
        )(gathered(grads, "samp"), state, lists, old_blocks, inverses, values)
        shrunk_blocks.append(shrunk)
        state = from_behind(moving, "feat", 1)
        if not final:
            grads = call(
                functools.partial(gradient_kernel, section + 1),
                float_of((samp_count, edge)),
                [VMEM] * 3,
                [padded, pltpu.VMEM((chunk, edge), jnp.float32)],
            )(state, lists, values)
    blocks = call(
        functools.partial(blocks_kernel, sections),
        float_of(blocks.shape),
        [SMEM] + [VMEM] * (1 + sections),
        [],
    )(block_order, blocks, *shrunk_blocks)
    return (blocks.reshape(-1), state.reshape(-1))


def solution(mesh):
    placed = (
        P("samp"),
        P("feat"),
        P("samp", "feat", None),
        P("samp", "feat", None),
        P("samp", "feat", None, None, None),
        P("feat", None),
        P("feat", None, None, None),
    )
    return jax.shard_map(
        per_device,
        mesh=mesh,
        in_specs=placed,
        out_specs=(P("feat"), P(("samp", "feat"))),
        check_vma=False,
    )
```

```python
import functools

import jax
import jax.numpy as jnp
from jax import lax
from jax.experimental import pallas as pl
from jax.experimental.pallas import tpu as pltpu
from jax.sharding import PartitionSpec as P

exact_prec = lax.Precision.HIGHEST
l1_penalty = 0.25
chunk = 16
copied = 32

VMEM = pl.BlockSpec(memory_space=pltpu.VMEM)
SMEM = pl.BlockSpec(memory_space=pltpu.SMEM)
HBM = pl.BlockSpec(memory_space=pltpu.HBM)


def float_of(shape):
    return jax.ShapeDtypeStruct(shape, jnp.float32)


def call(kernel, out_shape, in_specs, scratch_shapes):
    single = not isinstance(out_shape, tuple)
    return pl.pallas_call(
        kernel,
        out_shape=out_shape,
        in_specs=in_specs,
        out_specs=VMEM if single else tuple(VMEM for _ in out_shape),
        scratch_shapes=scratch_shapes,
        compiler_params=pltpu.CompilerParams(vmem_limit_bytes=24 << 20),
    )


def middle_first(count):
    return sorted(range(count), key=lambda index: (abs(index - count // 2), index))


def tile_products(vectors_of, tiles_of, tiles):
    pieces = []
    for first in range(0, tiles, chunk):
        vectors = vectors_of(first)
        edge = vectors.shape[1]
        products = lax.dot_general(
            vectors,
            tiles_of(first).reshape(chunk * edge, edge),
            (((1,), (1,)), ((), ())),
            preferred_element_type=jnp.float32,
        )
        sub = lax.broadcasted_iota(jnp.int32, (chunk, edge), 0)
        piece = products[:, :edge]
        for inner in range(1, chunk):
            piece = jnp.where(sub == inner, products[:, inner * edge : (inner + 1) * edge], piece)
        pieces.append(piece)
    return jnp.concatenate(pieces, axis=0)


def placed_sum(chosen, rows):
    high = rows.astype(jnp.bfloat16)
    rest = rows - high.astype(jnp.float32)
    middle = rest.astype(jnp.bfloat16)
    low = (rest - middle.astype(jnp.float32)).astype(jnp.bfloat16)
    ones = chosen.astype(jnp.bfloat16)
    return sum(
        jnp.dot(ones, part, preferred_element_type=jnp.float32) for part in (low, middle, high)
    )


def over_lanes(left, right):
    return lax.dot_general(
        left.astype(jnp.bfloat16),
        right.astype(jnp.bfloat16),
        (((1,), (1,)), ((), ())),
        preferred_element_type=jnp.float32,
    )


def bits_of(group_blocks):
    return group_blocks.bit_length()


def listed(row_in_group, taken, group_blocks):
    tiles = taken.shape[1]
    square = (tiles, tiles)
    sub = lax.broadcasted_iota(jnp.int32, square, 0)
    lane = lax.broadcasted_iota(jnp.int32, square, 1)
    taken = jnp.broadcast_to(taken, (8, tiles)).astype(jnp.float32)
    before = over_lanes(taken, (lane < sub).astype(jnp.float32))
    in_slot = (sub == before[0:1].astype(jnp.int32)) & (taken[0:1] > 0.0)
    numbers = lax.broadcasted_iota(jnp.int32, (8, tiles), 1)
    short = group_blocks - row_in_group
    facts = jnp.where(lax.broadcasted_iota(jnp.int32, (8, tiles), 0) == 0, numbers, short)
    found = over_lanes(facts.astype(jnp.float32), in_slot.astype(jnp.float32)).astype(jnp.int32)
    return found[0:1] * 2 ** bits_of(group_blocks) + group_blocks - found[1:2]


def margins_kernel(
    cols_hbm, targets_hbm, rows_hbm, beta_hbm, values_hbm,
    partial_ref, old_ref, lists_ref,
    picked_ref, beta_ref, rows_ref, cols_ref, values_ref,
    cols_smem, targets_smem, small_sem, tile_sem,
):
    tiles = cols_smem.shape[1]
    sections = targets_smem.shape[1]
    row_blocks = partial_ref.shape[0]
    small = [
        pltpu.make_async_copy(cols_hbm, cols_smem, small_sem.at[0]),
        pltpu.make_async_copy(beta_hbm, beta_ref, small_sem.at[1]),
        pltpu.make_async_copy(targets_hbm, targets_smem, small_sem.at[2]),
        pltpu.make_async_copy(rows_hbm, rows_ref, small_sem.at[3]),
        pltpu.make_async_copy(cols_hbm, cols_ref, small_sem.at[4]),
    ]
    large = [
        pltpu.make_async_copy(
            values_hbm.at[pl.ds(first, copied)],
            values_ref.at[pl.ds(first, copied)],
            tile_sem.at[first // copied],
        )
        for first in range(0, tiles, copied)
    ]
    for copy in small + large:
        copy.start()
    for copy in small:
        copy.wait()
    for tile in range(tiles):
        picked_ref[pl.ds(tile, 1), :] = beta_ref[pl.ds(cols_smem[0, tile], 1), :]
    for section in range(sections):
        old_ref[pl.ds(section, 1), :] = beta_ref[pl.ds(targets_smem[0, section], 1), :]

    def tiles_of(first):
        if first % copied == 0:
            large[first // copied].wait()
        return values_ref[pl.ds(first, chunk)]

    products = tile_products(
        lambda first: picked_ref[pl.ds(first, chunk), :].astype(jnp.bfloat16), tiles_of, tiles
    )
    my_index = lax.axis_index("feat")
    group_blocks = row_blocks // sections
    for section in range(sections):
        group = lax.rem(my_index - section + sections, sections)
        row_in_group = rows_ref[...] - group * group_blocks
        taken = (
            (row_in_group >= 0)
            & (row_in_group < group_blocks)
            & (cols_ref[...] == targets_smem[0, section])
        )
        lists_ref[pl.ds(section, 1), :] = listed(row_in_group, taken, group_blocks)

    block_ids = lax.broadcasted_iota(jnp.int32, (row_blocks, tiles), 0)
    placing = (block_ids == rows_ref[...]).astype(jnp.float32)
    partial = placed_sum(placing, products)
    for place, group in enumerate(middle_first(sections)):
        partial_ref[pl.ds(place * group_blocks, group_blocks), :] = partial[
            group * group_blocks : (group + 1) * group_blocks
        ]


def listed_slots(section, part, group_blocks, lists_ref, values_ref):
    bits = bits_of(group_blocks)
    found = [lists_ref[section, part * chunk + inner] for inner in range(chunk)]
    tiles = [values_ref[lax.shift_right_logical(number, bits)] for number in found]
    return jnp.concatenate(tiles, axis=0), [number & (2**bits - 1) for number in found]


def for_parts(section, group_blocks, lists_ref, run, part=0):
    run(part)
    if (part + 1) * chunk < lists_ref.shape[1]:
        more = lists_ref[section, (part + 1) * chunk] != group_blocks
        pl.when(more)(
            functools.partial(for_parts, section, group_blocks, lists_ref, run, part + 1)
        )


def gradient_of_all(residual, chosen, values_ref):
    tiles, edge, _ = values_ref.shape
    picked = lax.dot_general(
        chosen.astype(jnp.bfloat16),
        residual.astype(jnp.bfloat16),
        (((0,), (0,)), ((), ())),
        preferred_element_type=jnp.float32,
    )
    sub = lax.broadcasted_iota(jnp.int32, (chunk, edge), 0)
    spread = []
    for tile in range(tiles):
        first = tile - tile % chunk
        kept = jnp.where(sub == tile - first, picked[first : first + chunk], 0.0)
        spread.append(kept.astype(jnp.bfloat16))
    summed = jnp.dot(
        jnp.concatenate(spread, axis=1),
        values_ref[...].reshape(tiles * edge, edge),
        preferred_element_type=jnp.float32,
    )
    return jnp.sum(summed, axis=0, keepdims=True)


def first_kernel(
    parts_ref, labels_ref, rows_ref, cols_ref, targets_ref, values_ref, state_ref, grad_ref
):
    group_blocks = parts_ref.shape[1]
    first_row = lax.axis_index("feat") * group_blocks
    sub_ids = lax.broadcasted_iota(jnp.int32, (group_blocks, rows_ref.shape[1]), 0)
    same_row = sub_ids + first_row == rows_ref[...]
    chosen = (same_row & (cols_ref[...] == targets_ref[:, 0:1])).astype(jnp.float32)
    margins = parts_ref[0]
    for part in range(1, parts_ref.shape[0]):
        margins = margins + parts_ref[part]
    probability = 1.0 / (1.0 + jnp.exp(-margins))
    labels = labels_ref[pl.ds(pl.multiple_of(first_row, 8), group_blocks), :]
    residual = labels.astype(jnp.float32) - probability
    state_ref[0] = residual
    state_ref[1] = probability * (1.0 - probability)
    grad = gradient_of_all(residual, chosen, values_ref)
    grad_ref[...] = jnp.broadcast_to(grad, grad_ref.shape)


def gradient_kernel(section, state_ref, lists_ref, values_ref, grad_ref, rows_ref, total_ref):
    _, group_blocks, edge = state_ref.shape
    rows_ref[pl.ds(0, group_blocks), :] = state_ref[0]
    rows_ref[pl.ds(group_blocks, 8), :] = jnp.zeros((8, edge), jnp.float32)

    def run(part):
        tiles, places = listed_slots(section, part, group_blocks, lists_ref, values_ref)
        spread = []
        for place in places:
            row = jnp.broadcast_to(rows_ref[pl.ds(place, 1), :], (chunk, edge))
            spread.append(row.astype(jnp.bfloat16))
        total = jnp.dot(
            jnp.concatenate(spread, axis=1), tiles, preferred_element_type=jnp.float32
        )
        total_ref[...] = total if part == 0 else total_ref[...] + total

    for_parts(section, group_blocks, lists_ref, run)
    grad_ref[...] = jnp.broadcast_to(total_ref[0:1, :], grad_ref.shape)


def update_kernel(
    section, grads_ref, state_ref, lists_ref, old_ref, inverses_ref, values_ref,
    moved_ref, shrunk_ref, landed_ref,
):
    _, group_blocks, edge = state_ref.shape
    gradient = jnp.sum(grads_ref[...], axis=0, keepdims=True)
    step = jnp.sum(inverses_ref[section] * gradient, axis=1, keepdims=True)
    square = (edge, edge)
    on_diagonal = lax.broadcasted_iota(jnp.int32, square, 0) == lax.broadcasted_iota(
        jnp.int32, square, 1
    )
    step = jnp.sum(jnp.where(on_diagonal, step, 0.0), axis=0, keepdims=True)
    old = old_ref[pl.ds(section, 1), :]
    raised = old + step
    size = jnp.maximum(jnp.abs(raised) - l1_penalty, 0.0)
    shrunk = jnp.where(raised < 0.0, -size, size)
    shrunk_ref[...] = shrunk
    change = jnp.broadcast_to(shrunk - old, (chunk, edge)).astype(jnp.bfloat16)
    landed_ref[...] = jnp.zeros_like(landed_ref)

    def run(part):
        tiles, places = listed_slots(section, part, group_blocks, lists_ref, values_ref)
        images = lax.dot_general(
            change, tiles, (((1,), (1,)), ((), ())), preferred_element_type=jnp.float32
        )
        for inner, place in enumerate(places):
            image = images[0:1, inner * edge : (inner + 1) * edge]
            landed_ref[pl.ds(place, 1), :] = landed_ref[pl.ds(place, 1), :] + image

    for_parts(section, group_blocks, lists_ref, run)
    weight = state_ref[1]
    residual = state_ref[0] - weight * landed_ref[pl.ds(0, group_blocks), :]
    if len(moved_ref.shape) == 3:
        moved_ref[0] = residual
        moved_ref[1] = weight
    else:
        moved_ref[...] = residual


def blocks_kernel(sections, targets_smem, beta_ref, *refs):
    blocks_ref = refs[sections]
    blocks_ref[...] = beta_ref[...]
    for section in range(sections):
        blocks_ref[pl.ds(targets_smem[0, section], 1), :] = refs[section][...]


def from_behind(value, axis, steps):
    count = lax.axis_size(axis)
    pairs = [(source, (source + steps) % count) for source in range(count)]
    return lax.ppermute(value, axis, pairs)


def gathered(parts, axis):
    count, edge = parts.shape
    order = list(range(count))
    if count % 2 == 0:
        half = count // 2
        far_apart = [half - 1 - pair // 2 if pair % 2 == 0 else pair // 2 for pair in range(half)]
        order = [2 * chip + 1 for chip in far_apart] + [2 * chip for chip in far_apart]
    received = lax.all_to_all(
        parts.reshape(count, 1, edge), axis, 0, 0, axis_index_groups=[order]
    )
    return received.reshape(count, edge)


def per_device(labels, beta, tile_rows, tile_cols, tile_values, block_order, hess_inv):
    sections = lax.axis_size("feat")
    samp_count = lax.axis_size("samp")
    tiles, edge = tile_values.shape[2], tile_values.shape[4]
    row_blocks = labels.shape[0] // edge
    group_blocks = row_blocks // sections
    blocks = beta.reshape(-1, edge)
    inverses = hess_inv[0]
    values = tile_values[0, 0]
    partial_sum, old_blocks, lists = pl.pallas_call(
        margins_kernel,
        out_shape=(
            float_of((row_blocks, edge)),
            float_of((sections, edge)),
            jax.ShapeDtypeStruct((sections, tiles), jnp.int32),
        ),
        in_specs=[HBM] * 5,
        out_specs=(VMEM, VMEM, VMEM),
        scratch_shapes=[
            pltpu.VMEM((tiles, edge), jnp.float32),
            pltpu.VMEM(blocks.shape, jnp.float32),
            pltpu.VMEM((1, tiles), jnp.int32),
            pltpu.VMEM((1, tiles), jnp.int32),
            pltpu.VMEM(values.shape, jnp.bfloat16),
            pltpu.SMEM((1, tiles), jnp.int32),
            pltpu.SMEM((1, sections), jnp.int32),
            pltpu.SemaphoreType.DMA((5,)),
            pltpu.SemaphoreType.DMA((tiles // copied,)),
        ],
        compiler_params=pltpu.CompilerParams(vmem_limit_bytes=58 << 20),
    )(tile_cols[0], block_order, tile_rows[0], blocks, values)
    parts = lax.all_to_all(
        partial_sum.reshape(sections, group_blocks, edge),
        "feat",
        0,
        0,
        axis_index_groups=[middle_first(sections)],
    )
    group_shape = (group_blocks, edge)
    state, grads = call(
        first_kernel,
        (float_of((2, *group_shape)), float_of((samp_count, edge))),
        [VMEM] * 6,
        [],
    )(parts, labels.reshape(row_blocks, edge), tile_rows[0], tile_cols[0], block_order, values)
    padded = pltpu.VMEM((group_blocks + 8, edge), jnp.float32)
    shrunk_blocks = []
    for section in range(sections):
        final = section + 1 == sections
        moving, shrunk = call(
            functools.partial(update_kernel, section),
            (float_of(group_shape if final else (2, *group_shape)), float_of((1, edge))),
            [VMEM] * 6,
            [padded],
        )(gathered(grads, "samp"), state, lists, old_blocks, inverses, values)
        shrunk_blocks.append(shrunk)
        state = from_behind(moving, "feat", 1)
        if not final:
            grads = call(
                functools.partial(gradient_kernel, section + 1),
                float_of((samp_count, edge)),
                [VMEM] * 3,
                [padded, pltpu.VMEM((chunk, edge), jnp.float32)],
            )(state, lists, values)
    blocks = call(
        functools.partial(blocks_kernel, sections),
        float_of(blocks.shape),
        [SMEM] + [VMEM] * (1 + sections),
        [],
    )(block_order, blocks, *shrunk_blocks)
    return (blocks.reshape(-1), state.reshape(-1))


def solution(mesh):
    placed = (
        P("samp"),
        P("feat"),
        P("samp", "feat", None),
        P("samp", "feat", None),
        P("samp", "feat", None, None, None),
        P("feat", None),
        P("feat", None, None, None),
    )
    return jax.shard_map(
        per_device,
        mesh=mesh,
        in_specs=placed,
        out_specs=(P("feat"), P(("samp", "feat"))),
        check_vma=False,
    )
```

```python
import functools

import jax
import jax.numpy as jnp
from jax import lax
from jax.experimental import pallas as pl
from jax.experimental.pallas import tpu as pltpu
from jax.sharding import PartitionSpec as P

exact_prec = lax.Precision.HIGHEST
l1_penalty = 0.25
chunk = 16
copied = 32

VMEM = pl.BlockSpec(memory_space=pltpu.VMEM)
SMEM = pl.BlockSpec(memory_space=pltpu.SMEM)
HBM = pl.BlockSpec(memory_space=pltpu.HBM)


def float_of(shape):
    return jax.ShapeDtypeStruct(shape, jnp.float32)


def call(kernel, out_shape, in_specs, scratch_shapes):
    single = not isinstance(out_shape, tuple)
    return pl.pallas_call(
        kernel,
        out_shape=out_shape,
        in_specs=in_specs,
        out_specs=VMEM if single else tuple(VMEM for _ in out_shape),
        scratch_shapes=scratch_shapes,
        compiler_params=pltpu.CompilerParams(vmem_limit_bytes=24 << 20),
    )


def middle_first(count):
    return sorted(range(count), key=lambda index: (abs(index - count // 2), index))


def tile_products(vectors_of, tiles_of, tiles):
    pieces = []
    for first in range(0, tiles, chunk):
        vectors = vectors_of(first)
        edge = vectors.shape[1]
        products = lax.dot_general(
            vectors,
            tiles_of(first).reshape(chunk * edge, edge),
            (((1,), (1,)), ((), ())),
            preferred_element_type=jnp.float32,
        )
        sub = lax.broadcasted_iota(jnp.int32, (chunk, edge), 0)
        piece = products[:, :edge]
        for inner in range(1, chunk):
            piece = jnp.where(sub == inner, products[:, inner * edge : (inner + 1) * edge], piece)
        pieces.append(piece)
    return jnp.concatenate(pieces, axis=0)


def placed_sum(chosen, rows):
    high = rows.astype(jnp.bfloat16)
    rest = rows - high.astype(jnp.float32)
    middle = rest.astype(jnp.bfloat16)
    low = (rest - middle.astype(jnp.float32)).astype(jnp.bfloat16)
    ones = chosen.astype(jnp.bfloat16)
    return sum(
        jnp.dot(ones, part, preferred_element_type=jnp.float32) for part in (low, middle, high)
    )


def over_lanes(left, right):
    return lax.dot_general(
        left.astype(jnp.bfloat16),
        right.astype(jnp.bfloat16),
        (((1,), (1,)), ((), ())),
        preferred_element_type=jnp.float32,
    )


def bits_of(group_blocks):
    return group_blocks.bit_length()


def listed(row_in_group, taken, group_blocks):
    tiles = taken.shape[1]
    square = (tiles, tiles)
    sub = lax.broadcasted_iota(jnp.int32, square, 0)
    lane = lax.broadcasted_iota(jnp.int32, square, 1)
    taken = jnp.broadcast_to(taken, (8, tiles)).astype(jnp.float32)
    before = over_lanes(taken, (lane < sub).astype(jnp.float32))
    in_slot = (sub == before[0:1].astype(jnp.int32)) & (taken[0:1] > 0.0)
    numbers = lax.broadcasted_iota(jnp.int32, (8, tiles), 1)
    short = group_blocks - row_in_group
    facts = jnp.where(lax.broadcasted_iota(jnp.int32, (8, tiles), 0) == 0, numbers, short)
    found = over_lanes(facts.astype(jnp.float32), in_slot.astype(jnp.float32)).astype(jnp.int32)
    return found[0:1] * 2 ** bits_of(group_blocks) + group_blocks - found[1:2]


def margins_kernel(
    cols_hbm, targets_hbm, rows_hbm, beta_hbm, values_hbm,
    partial_ref, old_ref, lists_ref,
    picked_ref, beta_ref, rows_ref, cols_ref, values_ref,
    cols_smem, targets_smem, small_sem, tile_sem,
):
    tiles = cols_smem.shape[1]
    sections = targets_smem.shape[1]
    row_blocks = partial_ref.shape[0]
    small = [
        pltpu.make_async_copy(cols_hbm, cols_smem, small_sem.at[0]),
        pltpu.make_async_copy(beta_hbm, beta_ref, small_sem.at[1]),
        pltpu.make_async_copy(targets_hbm, targets_smem, small_sem.at[2]),
        pltpu.make_async_copy(rows_hbm, rows_ref, small_sem.at[3]),
        pltpu.make_async_copy(cols_hbm, cols_ref, small_sem.at[4]),
    ]
    large = [
        pltpu.make_async_copy(
            values_hbm.at[pl.ds(first, copied)],
            values_ref.at[pl.ds(first, copied)],
            tile_sem.at[first // copied],
        )
        for first in range(0, tiles, copied)
    ]
    for copy in small + large:
        copy.start()
    for copy in small:
        copy.wait()
    for tile in range(tiles):
        picked_ref[pl.ds(tile, 1), :] = beta_ref[pl.ds(cols_smem[0, tile], 1), :]
    for section in range(sections):
        old_ref[pl.ds(section, 1), :] = beta_ref[pl.ds(targets_smem[0, section], 1), :]

    def tiles_of(first):
        if first % copied == 0:
            large[first // copied].wait()
        return values_ref[pl.ds(first, chunk)]

    products = tile_products(
        lambda first: picked_ref[pl.ds(first, chunk), :].astype(jnp.bfloat16), tiles_of, tiles
    )
    my_index = lax.axis_index("feat")
    group_blocks = row_blocks // sections
    for section in range(sections):
        group = lax.rem(my_index - section + sections, sections)
        row_in_group = rows_ref[...] - group * group_blocks
        taken = (
            (row_in_group >= 0)
            & (row_in_group < group_blocks)
            & (cols_ref[...] == targets_smem[0, section])
        )
        lists_ref[pl.ds(section, 1), :] = listed(row_in_group, taken, group_blocks)

    block_ids = lax.broadcasted_iota(jnp.int32, (row_blocks, tiles), 0)
    placing = (block_ids == rows_ref[...]).astype(jnp.float32)
    partial = placed_sum(placing, products)
    for place, group in enumerate(middle_first(sections)):
        partial_ref[pl.ds(place * group_blocks, group_blocks), :] = partial[
            group * group_blocks : (group + 1) * group_blocks
        ]


def listed_slots(section, part, group_blocks, lists_ref, values_ref):
    bits = bits_of(group_blocks)
    found = [lists_ref[section, part * chunk + inner] for inner in range(chunk)]
    tiles = [values_ref[lax.shift_right_logical(number, bits)] for number in found]
    return jnp.concatenate(tiles, axis=0), [number & (2**bits - 1) for number in found]


def for_parts(section, group_blocks, lists_ref, run, part=0):
    run(part)
    if (part + 1) * chunk < lists_ref.shape[1]:
        more = lists_ref[section, (part + 1) * chunk] != group_blocks
        pl.when(more)(
            functools.partial(for_parts, section, group_blocks, lists_ref, run, part + 1)
        )


def gradient_of_all(residual, chosen, values_ref):
    tiles, edge, _ = values_ref.shape
    picked = lax.dot_general(
        chosen.astype(jnp.bfloat16),
        residual.astype(jnp.bfloat16),
        (((0,), (0,)), ((), ())),
        preferred_element_type=jnp.float32,
    )
    sub = lax.broadcasted_iota(jnp.int32, (chunk, edge), 0)
    spread = []
    for tile in range(tiles):
        first = tile - tile % chunk
        kept = jnp.where(sub == tile - first, picked[first : first + chunk], 0.0)
        spread.append(kept.astype(jnp.bfloat16))
    summed = jnp.dot(
        jnp.concatenate(spread, axis=1),
        values_ref[...].reshape(tiles * edge, edge),
        preferred_element_type=jnp.float32,
    )
    return jnp.sum(summed, axis=0, keepdims=True)


def first_kernel(
    parts_ref, labels_ref, rows_ref, cols_ref, targets_ref, values_ref,
    residual_ref, weight_ref, grad_ref,
):
    group_blocks = parts_ref.shape[1]
    first_row = lax.axis_index("feat") * group_blocks
    sub_ids = lax.broadcasted_iota(jnp.int32, (group_blocks, rows_ref.shape[1]), 0)
    same_row = sub_ids + first_row == rows_ref[...]
    chosen = (same_row & (cols_ref[...] == targets_ref[:, 0:1])).astype(jnp.float32)
    margins = parts_ref[0]
    for part in range(1, parts_ref.shape[0]):
        margins = margins + parts_ref[part]
    probability = 1.0 / (1.0 + jnp.exp(-margins))
    labels = labels_ref[pl.ds(pl.multiple_of(first_row, 8), group_blocks), :]
    residual = labels.astype(jnp.float32) - probability
    residual_ref[...] = residual
    weight_ref[...] = probability * (1.0 - probability)
    grad = gradient_of_all(residual, chosen, values_ref)
    grad_ref[...] = jnp.broadcast_to(grad, grad_ref.shape)


def gradient_kernel(
    section, residual_ref, lists_ref, values_ref, grad_ref, rows_ref, total_ref
):
    group_blocks, edge = residual_ref.shape
    rows_ref[pl.ds(0, group_blocks), :] = residual_ref[...]
    rows_ref[pl.ds(group_blocks, 8), :] = jnp.zeros((8, edge), jnp.float32)

    def run(part):
        tiles, places = listed_slots(section, part, group_blocks, lists_ref, values_ref)
        spread = []
        for place in places:
            row = jnp.broadcast_to(rows_ref[pl.ds(place, 1), :], (chunk, edge))
            spread.append(row.astype(jnp.bfloat16))
        total = jnp.dot(
            jnp.concatenate(spread, axis=1), tiles, preferred_element_type=jnp.float32
        )
        total_ref[...] = total if part == 0 else total_ref[...] + total

    for_parts(section, group_blocks, lists_ref, run)
    grad_ref[...] = jnp.broadcast_to(total_ref[0:1, :], grad_ref.shape)


def joined_kernel(grads_ref, weight_ref, joined_ref):
    joined_ref[...] = grads_ref[...]


def update_kernel(
    section, grads_ref, residual_ref, weight_ref, lists_ref, old_ref, inverses_ref, values_ref,
    moved_ref, shrunk_ref, landed_ref,
):
    group_blocks, edge = residual_ref.shape
    gradient = jnp.sum(grads_ref[...], axis=0, keepdims=True)
    step = jnp.sum(inverses_ref[section] * gradient, axis=1, keepdims=True)
    square = (edge, edge)
    on_diagonal = lax.broadcasted_iota(jnp.int32, square, 0) == lax.broadcasted_iota(
        jnp.int32, square, 1
    )
    step = jnp.sum(jnp.where(on_diagonal, step, 0.0), axis=0, keepdims=True)
    old = old_ref[pl.ds(section, 1), :]
    raised = old + step
    size = jnp.maximum(jnp.abs(raised) - l1_penalty, 0.0)
    shrunk = jnp.where(raised < 0.0, -size, size)
    shrunk_ref[...] = shrunk
    change = jnp.broadcast_to(shrunk - old, (chunk, edge)).astype(jnp.bfloat16)
    landed_ref[...] = jnp.zeros_like(landed_ref)

    def run(part):
        tiles, places = listed_slots(section, part, group_blocks, lists_ref, values_ref)
        images = lax.dot_general(
            change, tiles, (((1,), (1,)), ((), ())), preferred_element_type=jnp.float32
        )
        for inner, place in enumerate(places):
            image = images[0:1, inner * edge : (inner + 1) * edge]
            landed_ref[pl.ds(place, 1), :] = landed_ref[pl.ds(place, 1), :] + image

    for_parts(section, group_blocks, lists_ref, run)
    landed = landed_ref[pl.ds(0, group_blocks), :]
    moved_ref[...] = residual_ref[...] - weight_ref[...] * landed


def blocks_kernel(sections, targets_smem, beta_ref, *refs):
    blocks_ref = refs[sections]
    blocks_ref[...] = beta_ref[...]
    for section in range(sections):
        blocks_ref[pl.ds(targets_smem[0, section], 1), :] = refs[section][...]


def from_behind(value, axis, steps):
    count = lax.axis_size(axis)
    pairs = [(source, (source + steps) % count) for source in range(count)]
    return lax.ppermute(value, axis, pairs)


def gathered(parts, axis):
    count, edge = parts.shape
    order = list(range(count))
    if count % 2 == 0:
        half = count // 2
        far_apart = [half - 1 - pair // 2 if pair % 2 == 0 else pair // 2 for pair in range(half)]
        order = [2 * chip + 1 for chip in far_apart] + [2 * chip for chip in far_apart]
    received = lax.all_to_all(
        parts.reshape(count, 1, edge), axis, 0, 0, axis_index_groups=[order]
    )
    return received.reshape(count, edge)


def per_device(labels, beta, tile_rows, tile_cols, tile_values, block_order, hess_inv):
    sections = lax.axis_size("feat")
    samp_count = lax.axis_size("samp")
    tiles, edge = tile_values.shape[2], tile_values.shape[4]
    row_blocks = labels.shape[0] // edge
    group_blocks = row_blocks // sections
    blocks = beta.reshape(-1, edge)
    inverses = hess_inv[0]
    values = tile_values[0, 0]
    partial_sum, old_blocks, lists = pl.pallas_call(
        margins_kernel,
        out_shape=(
            float_of((row_blocks, edge)),
            float_of((sections, edge)),
            jax.ShapeDtypeStruct((sections, tiles), jnp.int32),
        ),
        in_specs=[HBM] * 5,
        out_specs=(VMEM, VMEM, VMEM),
        scratch_shapes=[
            pltpu.VMEM((tiles, edge), jnp.float32),
            pltpu.VMEM(blocks.shape, jnp.float32),
            pltpu.VMEM((1, tiles), jnp.int32),
            pltpu.VMEM((1, tiles), jnp.int32),
            pltpu.VMEM(values.shape, jnp.bfloat16),
            pltpu.SMEM((1, tiles), jnp.int32),
            pltpu.SMEM((1, sections), jnp.int32),
            pltpu.SemaphoreType.DMA((5,)),
            pltpu.SemaphoreType.DMA((tiles // copied,)),
        ],
        compiler_params=pltpu.CompilerParams(vmem_limit_bytes=58 << 20),
    )(tile_cols[0], block_order, tile_rows[0], blocks, values)
    parts = lax.all_to_all(
        partial_sum.reshape(sections, group_blocks, edge),
        "feat",
        0,
        0,
        axis_index_groups=[middle_first(sections)],
    )
    group_shape = (group_blocks, edge)
    residual, weight, grads = call(
        first_kernel,
        (float_of(group_shape), float_of(group_shape), float_of((samp_count, edge))),
        [VMEM] * 6,
        [],
    )(parts, labels.reshape(row_blocks, edge), tile_rows[0], tile_cols[0], block_order, values)
    padded = pltpu.VMEM((group_blocks + 8, edge), jnp.float32)
    shrunk_blocks = []
    for section in range(sections):
        final = section + 1 == sections
        sums = gathered(grads, "samp")
        moving, shrunk = call(
            functools.partial(update_kernel, section),
            (float_of(group_shape), float_of((1, edge))),
            [VMEM] * 7,
            [padded],
        )(sums, residual, weight, lists, old_blocks, inverses, values)
        shrunk_blocks.append(shrunk)
        residual = from_behind(moving, "feat", 1)
        if not final:
            weight = from_behind(weight, "feat", 1)
            grads = call(
                functools.partial(gradient_kernel, section + 1),
                float_of((samp_count, edge)),
                [VMEM] * 3,
                [padded, pltpu.VMEM((chunk, edge), jnp.float32)],
            )(residual, lists, values)
            grads = call(joined_kernel, float_of((samp_count, edge)), [VMEM] * 2, [])(
                grads, weight
            )
    blocks = call(
        functools.partial(blocks_kernel, sections),
        float_of(blocks.shape),
        [SMEM] + [VMEM] * (1 + sections),
        [],
    )(block_order, blocks, *shrunk_blocks)
    return (blocks.reshape(-1), residual.reshape(-1))


def solution(mesh):
    placed = (
        P("samp"),
        P("feat"),
        P("samp", "feat", None),
        P("samp", "feat", None),
        P("samp", "feat", None, None, None),
        P("feat", None),
        P("feat", None, None, None),
    )
    return jax.shard_map(
        per_device,
        mesh=mesh,
        in_specs=placed,
        out_specs=(P("feat"), P(("samp", "feat"))),
        check_vma=False,
    )
```

```python
import functools

import jax
import jax.numpy as jnp
from jax import lax
from jax.experimental import pallas as pl
from jax.experimental.pallas import tpu as pltpu
from jax.sharding import PartitionSpec as P

exact_prec = lax.Precision.HIGHEST
l1_penalty = 0.25
chunk = 16
copied = 32

VMEM = pl.BlockSpec(memory_space=pltpu.VMEM)
SMEM = pl.BlockSpec(memory_space=pltpu.SMEM)
HBM = pl.BlockSpec(memory_space=pltpu.HBM)


def float_of(shape):
    return jax.ShapeDtypeStruct(shape, jnp.float32)


def call(kernel, out_shape, in_specs, scratch_shapes):
    single = not isinstance(out_shape, tuple)
    return pl.pallas_call(
        kernel,
        out_shape=out_shape,
        in_specs=in_specs,
        out_specs=VMEM if single else tuple(VMEM for _ in out_shape),
        scratch_shapes=scratch_shapes,
        compiler_params=pltpu.CompilerParams(vmem_limit_bytes=24 << 20),
    )


def middle_first(count):
    return sorted(range(count), key=lambda index: (abs(index - count // 2), index))


def tile_products(vectors_of, tiles_of, tiles):
    pieces = []
    for first in range(0, tiles, chunk):
        vectors = vectors_of(first)
        edge = vectors.shape[1]
        products = lax.dot_general(
            vectors,
            tiles_of(first).reshape(chunk * edge, edge),
            (((1,), (1,)), ((), ())),
            preferred_element_type=jnp.float32,
        )
        sub = lax.broadcasted_iota(jnp.int32, (chunk, edge), 0)
        piece = products[:, :edge]
        for inner in range(1, chunk):
            piece = jnp.where(sub == inner, products[:, inner * edge : (inner + 1) * edge], piece)
        pieces.append(piece)
    return jnp.concatenate(pieces, axis=0)


def placed_sum(chosen, rows):
    high = rows.astype(jnp.bfloat16)
    rest = rows - high.astype(jnp.float32)
    middle = rest.astype(jnp.bfloat16)
    low = (rest - middle.astype(jnp.float32)).astype(jnp.bfloat16)
    ones = chosen.astype(jnp.bfloat16)
    return sum(
        jnp.dot(ones, part, preferred_element_type=jnp.float32) for part in (low, middle, high)
    )


def over_lanes(left, right):
    return lax.dot_general(
        left.astype(jnp.bfloat16),
        right.astype(jnp.bfloat16),
        (((1,), (1,)), ((), ())),
        preferred_element_type=jnp.float32,
    )


def bits_of(group_blocks):
    return group_blocks.bit_length()


def listed(row_in_group, taken, group_blocks):
    tiles = taken.shape[1]
    square = (tiles, tiles)
    sub = lax.broadcasted_iota(jnp.int32, square, 0)
    lane = lax.broadcasted_iota(jnp.int32, square, 1)
    taken = jnp.broadcast_to(taken, (8, tiles)).astype(jnp.float32)
    before = over_lanes(taken, (lane < sub).astype(jnp.float32))
    in_slot = (sub == before[0:1].astype(jnp.int32)) & (taken[0:1] > 0.0)
    numbers = lax.broadcasted_iota(jnp.int32, (8, tiles), 1)
    short = group_blocks - row_in_group
    facts = jnp.where(lax.broadcasted_iota(jnp.int32, (8, tiles), 0) == 0, numbers, short)
    found = over_lanes(facts.astype(jnp.float32), in_slot.astype(jnp.float32)).astype(jnp.int32)
    return found[0:1] * 2 ** bits_of(group_blocks) + group_blocks - found[1:2]


def margins_kernel(
    cols_hbm, targets_hbm, rows_hbm, beta_hbm, values_hbm,
    partial_ref, old_ref, lists_ref,
    picked_ref, beta_ref, rows_ref, cols_ref, values_ref,
    cols_smem, targets_smem, small_sem, tile_sem,
):
    tiles = cols_smem.shape[1]
    sections = targets_smem.shape[1]
    row_blocks = partial_ref.shape[0]
    small = [
        pltpu.make_async_copy(cols_hbm, cols_smem, small_sem.at[0]),
        pltpu.make_async_copy(beta_hbm, beta_ref, small_sem.at[1]),
        pltpu.make_async_copy(targets_hbm, targets_smem, small_sem.at[2]),
        pltpu.make_async_copy(rows_hbm, rows_ref, small_sem.at[3]),
        pltpu.make_async_copy(cols_hbm, cols_ref, small_sem.at[4]),
    ]
    large = [
        pltpu.make_async_copy(
            values_hbm.at[pl.ds(first, copied)],
            values_ref.at[pl.ds(first, copied)],
            tile_sem.at[first // copied],
        )
        for first in range(0, tiles, copied)
    ]
    for copy in small + large:
        copy.start()
    for copy in small:
        copy.wait()
    for tile in range(tiles):
        picked_ref[pl.ds(tile, 1), :] = beta_ref[pl.ds(cols_smem[0, tile], 1), :]
    for section in range(sections):
        old_ref[pl.ds(section, 1), :] = beta_ref[pl.ds(targets_smem[0, section], 1), :]

    def tiles_of(first):
        if first % copied == 0:
            large[first // copied].wait()
        return values_ref[pl.ds(first, chunk)]

    products = tile_products(
        lambda first: picked_ref[pl.ds(first, chunk), :].astype(jnp.bfloat16), tiles_of, tiles
    )
    my_index = lax.axis_index("feat")
    group_blocks = row_blocks // sections
    for section in range(sections):
        group = lax.rem(my_index - section + sections, sections)
        row_in_group = rows_ref[...] - group * group_blocks
        taken = (
            (row_in_group >= 0)
            & (row_in_group < group_blocks)
            & (cols_ref[...] == targets_smem[0, section])
        )
        lists_ref[pl.ds(section, 1), :] = listed(row_in_group, taken, group_blocks)

    block_ids = lax.broadcasted_iota(jnp.int32, (row_blocks, tiles), 0)
    placing = (block_ids == rows_ref[...]).astype(jnp.float32)
    partial = placed_sum(placing, products)
    for place, group in enumerate(middle_first(sections)):
        partial_ref[pl.ds(place * group_blocks, group_blocks), :] = partial[
            group * group_blocks : (group + 1) * group_blocks
        ]


def listed_slots(section, part, group_blocks, lists_ref, values_ref):
    bits = bits_of(group_blocks)
    found = [lists_ref[section, part * chunk + inner] for inner in range(chunk)]
    tiles = [values_ref[lax.shift_right_logical(number, bits)] for number in found]
    return jnp.concatenate(tiles, axis=0), [number & (2**bits - 1) for number in found]


def for_parts(section, group_blocks, lists_ref, run, part=0):
    run(part)
    if (part + 1) * chunk < lists_ref.shape[1]:
        more = lists_ref[section, (part + 1) * chunk] != group_blocks
        pl.when(more)(
            functools.partial(for_parts, section, group_blocks, lists_ref, run, part + 1)
        )


def gradient_of_all(residual, chosen, values_ref):
    tiles, edge, _ = values_ref.shape
    picked = lax.dot_general(
        chosen.astype(jnp.bfloat16),
        residual.astype(jnp.bfloat16),
        (((0,), (0,)), ((), ())),
        preferred_element_type=jnp.float32,
    )
    sub = lax.broadcasted_iota(jnp.int32, (chunk, edge), 0)
    spread = []
    for tile in range(tiles):
        first = tile - tile % chunk
        kept = jnp.where(sub == tile - first, picked[first : first + chunk], 0.0)
        spread.append(kept.astype(jnp.bfloat16))
    summed = jnp.dot(
        jnp.concatenate(spread, axis=1),
        values_ref[...].reshape(tiles * edge, edge),
        preferred_element_type=jnp.float32,
    )
    return jnp.sum(summed, axis=0, keepdims=True)


def first_kernel(
    parts_ref, labels_ref, rows_ref, cols_ref, targets_ref, values_ref,
    residual_ref, weight_ref, grad_ref,
):
    group_blocks = parts_ref.shape[1]
    first_row = lax.axis_index("feat") * group_blocks
    sub_ids = lax.broadcasted_iota(jnp.int32, (group_blocks, rows_ref.shape[1]), 0)
    same_row = sub_ids + first_row == rows_ref[...]
    chosen = (same_row & (cols_ref[...] == targets_ref[:, 0:1])).astype(jnp.float32)
    margins = parts_ref[0]
    for part in range(1, parts_ref.shape[0]):
        margins = margins + parts_ref[part]
    probability = 1.0 / (1.0 + jnp.exp(-margins))
    labels = labels_ref[pl.ds(pl.multiple_of(first_row, 8), group_blocks), :]
    residual = labels.astype(jnp.float32) - probability
    residual_ref[...] = residual
    weight_ref[...] = probability * (1.0 - probability)
    grad = gradient_of_all(residual, chosen, values_ref)
    grad_ref[...] = jnp.broadcast_to(grad, grad_ref.shape)


def gradient_kernel(
    section, residual_ref, lists_ref, values_ref, grad_ref, rows_ref, total_ref
):
    group_blocks, edge = residual_ref.shape
    rows_ref[pl.ds(0, group_blocks), :] = residual_ref[...]
    rows_ref[pl.ds(group_blocks, 8), :] = jnp.zeros((8, edge), jnp.float32)

    def run(part):
        tiles, places = listed_slots(section, part, group_blocks, lists_ref, values_ref)
        spread = []
        for place in places:
            row = jnp.broadcast_to(rows_ref[pl.ds(place, 1), :], (chunk, edge))
            spread.append(row.astype(jnp.bfloat16))
        total = jnp.dot(
            jnp.concatenate(spread, axis=1), tiles, preferred_element_type=jnp.float32
        )
        total_ref[...] = total if part == 0 else total_ref[...] + total

    for_parts(section, group_blocks, lists_ref, run)
    grad_ref[...] = jnp.broadcast_to(total_ref[0:1, :], grad_ref.shape)


def parted_kernel(
    section, state_ref, lists_ref, values_ref,
    residual_ref, weight_ref, grad_ref, rows_ref, total_ref,
):
    residual_ref[...] = state_ref[0]
    weight_ref[...] = state_ref[1]
    gradient_kernel(
        section, state_ref.at[0], lists_ref, values_ref, grad_ref, rows_ref, total_ref
    )


def joined_kernel(grads_ref, weight_ref, joined_ref):
    joined_ref[...] = grads_ref[...]


def update_kernel(
    section, grads_ref, residual_ref, weight_ref, lists_ref, old_ref, inverses_ref, values_ref,
    moved_ref, shrunk_ref, landed_ref,
):
    group_blocks, edge = residual_ref.shape
    gradient = jnp.sum(grads_ref[...], axis=0, keepdims=True)
    step = jnp.sum(inverses_ref[section] * gradient, axis=1, keepdims=True)
    square = (edge, edge)
    on_diagonal = lax.broadcasted_iota(jnp.int32, square, 0) == lax.broadcasted_iota(
        jnp.int32, square, 1
    )
    step = jnp.sum(jnp.where(on_diagonal, step, 0.0), axis=0, keepdims=True)
    old = old_ref[pl.ds(section, 1), :]
    raised = old + step
    size = jnp.maximum(jnp.abs(raised) - l1_penalty, 0.0)
    shrunk = jnp.where(raised < 0.0, -size, size)
    shrunk_ref[...] = shrunk
    change = jnp.broadcast_to(shrunk - old, (chunk, edge)).astype(jnp.bfloat16)
    landed_ref[...] = jnp.zeros_like(landed_ref)

    def run(part):
        tiles, places = listed_slots(section, part, group_blocks, lists_ref, values_ref)
        images = lax.dot_general(
            change, tiles, (((1,), (1,)), ((), ())), preferred_element_type=jnp.float32
        )
        for inner, place in enumerate(places):
            image = images[0:1, inner * edge : (inner + 1) * edge]
            landed_ref[pl.ds(place, 1), :] = landed_ref[pl.ds(place, 1), :] + image

    for_parts(section, group_blocks, lists_ref, run)
    landed = landed_ref[pl.ds(0, group_blocks), :]
    residual = residual_ref[...] - weight_ref[...] * landed
    if len(moved_ref.shape) == 3:
        moved_ref[0] = residual
        moved_ref[1] = weight_ref[...]
    else:
        moved_ref[...] = residual


def blocks_kernel(sections, targets_smem, beta_ref, *refs):
    blocks_ref = refs[sections]
    blocks_ref[...] = beta_ref[...]
    for section in range(sections):
        blocks_ref[pl.ds(targets_smem[0, section], 1), :] = refs[section][...]


def from_behind(value, axis, steps):
    count = lax.axis_size(axis)
    pairs = [(source, (source + steps) % count) for source in range(count)]
    return lax.ppermute(value, axis, pairs)


def gathered(parts, axis):
    count, edge = parts.shape
    order = list(range(count))
    if count % 2 == 0:
        half = count // 2
        far_apart = [half - 1 - pair // 2 if pair % 2 == 0 else pair // 2 for pair in range(half)]
        order = [2 * chip + 1 for chip in far_apart] + [2 * chip for chip in far_apart]
    received = lax.all_to_all(
        parts.reshape(count, 1, edge), axis, 0, 0, axis_index_groups=[order]
    )
    return received.reshape(count, edge)


def per_device(labels, beta, tile_rows, tile_cols, tile_values, block_order, hess_inv):
    sections = lax.axis_size("feat")
    samp_count = lax.axis_size("samp")
    tiles, edge = tile_values.shape[2], tile_values.shape[4]
    row_blocks = labels.shape[0] // edge
    group_blocks = row_blocks // sections
    blocks = beta.reshape(-1, edge)
    inverses = hess_inv[0]
    values = tile_values[0, 0]
    partial_sum, old_blocks, lists = pl.pallas_call(
        margins_kernel,
        out_shape=(
            float_of((row_blocks, edge)),
            float_of((sections, edge)),
            jax.ShapeDtypeStruct((sections, tiles), jnp.int32),
        ),
        in_specs=[HBM] * 5,
        out_specs=(VMEM, VMEM, VMEM),
        scratch_shapes=[
            pltpu.VMEM((tiles, edge), jnp.float32),
            pltpu.VMEM(blocks.shape, jnp.float32),
            pltpu.VMEM((1, tiles), jnp.int32),
            pltpu.VMEM((1, tiles), jnp.int32),
            pltpu.VMEM(values.shape, jnp.bfloat16),
            pltpu.SMEM((1, tiles), jnp.int32),
            pltpu.SMEM((1, sections), jnp.int32),
            pltpu.SemaphoreType.DMA((5,)),
            pltpu.SemaphoreType.DMA((tiles // copied,)),
        ],
        compiler_params=pltpu.CompilerParams(vmem_limit_bytes=58 << 20),
    )(tile_cols[0], block_order, tile_rows[0], blocks, values)
    parts = lax.all_to_all(
        partial_sum.reshape(sections, group_blocks, edge),
        "feat",
        0,
        0,
        axis_index_groups=[middle_first(sections)],
    )
    group_shape = (group_blocks, edge)
    residual, weight, grads = call(
        first_kernel,
        (float_of(group_shape), float_of(group_shape), float_of((samp_count, edge))),
        [VMEM] * 6,
        [],
    )(parts, labels.reshape(row_blocks, edge), tile_rows[0], tile_cols[0], block_order, values)
    padded = pltpu.VMEM((group_blocks + 8, edge), jnp.float32)
    shrunk_blocks = []
    for section in range(sections):
        final = section + 1 == sections
        sums = gathered(grads, "samp")
        together = section == 0 and not final
        moving, shrunk = call(
            functools.partial(update_kernel, section),
            (float_of((2, *group_shape) if together else group_shape), float_of((1, edge))),
            [VMEM] * 7,
            [padded],
        )(sums, residual, weight, lists, old_blocks, inverses, values)
        shrunk_blocks.append(shrunk)
        residual = from_behind(moving, "feat", 1)
        scratch = [padded, pltpu.VMEM((chunk, edge), jnp.float32)]
        if together:
            residual, weight, grads = call(
                functools.partial(parted_kernel, section + 1),
                (float_of(group_shape), float_of(group_shape), float_of((samp_count, edge))),
                [VMEM] * 3,
                scratch,
            )(residual, lists, values)
        elif not final:
            weight = from_behind(weight, "feat", 1)
            grads = call(
                functools.partial(gradient_kernel, section + 1),
                float_of((samp_count, edge)),
                [VMEM] * 3,
                scratch,
            )(residual, lists, values)
            grads = call(joined_kernel, float_of((samp_count, edge)), [VMEM] * 2, [])(
                grads, weight
            )
    blocks = call(
        functools.partial(blocks_kernel, sections),
        float_of(blocks.shape),
        [SMEM] + [VMEM] * (1 + sections),
        [],
    )(block_order, blocks, *shrunk_blocks)
    return (blocks.reshape(-1), residual.reshape(-1))


def solution(mesh):
    placed = (
        P("samp"),
        P("feat"),
        P("samp", "feat", None),
        P("samp", "feat", None),
        P("samp", "feat", None, None, None),
        P("feat", None),
        P("feat", None, None, None),
    )
    return jax.shard_map(
        per_device,
        mesh=mesh,
        in_specs=placed,
        out_specs=(P("feat"), P(("samp", "feat"))),
        check_vma=False,
    )
```
